32 devices in a mesh: seq: 8 (over z, x), tp: 4 (over y, core).
Axes of the slice: x: 2, y: 2, z: 4, core: 2. Of those that a mesh axis runs over, the one named last changes fastest.
Arguments:
- inputs: bfloat16 [2048, 768], P('seq'), may hold values from -6 to 6
- value_weight: bfloat16 [768, 768], P(None, 'tp'), may hold values from -0.21875 to 0.21875
- value_bias: float32 [768], P('tp'), may hold values from -3 to 3
- out_weight: bfloat16 [768, 768], P('tp'), may hold values from -0.21875 to 0.21875
- out_bias: float32 [768], replicated, may hold values from -3 to 3
- first_gain: float32 [768], replicated, may hold values from 0.5 to 1.5
- first_shift: float32 [768], replicated, may hold values from -3 to 3
- up_weight: bfloat16 [768, 3072], P(None, 'tp'), may hold values from -0.21875 to 0.21875
- up_bias: float32 [3072], P('tp'), may hold values from -3 to 3
- down_weight: bfloat16 [3072, 768], P('tp'), may hold values from -0.109375 to 0.109375
- down_bias: float32 [768], replicated, may hold values from -3 to 3
- second_gain: float32 [768], replicated, may hold values from 0.5 to 1.5
- second_shift: float32 [768], replicated, may hold values from -3 to 3
- conv_weight: float32 [12, 65], P('tp'), may hold values from -0.75 to 0.75
- query_codes: int32 [2048, 12, 32], P('seq', 'tp'), may hold values from 0 to 255
- key_codes: int32 [2048, 12, 32], P('seq', 'tp'), may hold values from 0 to 255
- masked: int32 [2048], P('seq'), may hold values from 0 to 1, as said below
- out_grad: float32 [2048, 768], P('seq'), may hold values from -6 to 6
Outputs:
- output: bfloat16 [2048, 768], P('seq')
- input_grad: float32 [2048, 768], P('seq')
- grad_value_weight: float32 [768, 768], P(None, 'tp')
- grad_value_bias: float32 [768], P('tp')
- grad_out_weight: float32 [768, 768], P('tp')
- grad_out_bias: float32 [768], replicated
- grad_first_gain: float32 [768], replicated
- grad_first_shift: float32 [768], replicated
- grad_up_weight: float32 [768, 3072], P(None, 'tp')
- grad_up_bias: float32 [3072], P('tp')
- grad_down_weight: float32 [3072, 768], P('tp')
- grad_down_bias: float32 [768], replicated
- grad_second_gain: float32 [768], replicated
- grad_second_shift: float32 [768], replicated
- grad_conv_weight: float32 [12, 65], P('tp')
The draws below stay inside these ranges and needn't reach their ends.
Inputs may be any that keep to these rules, and one draw needn't show every extreme that they name: `masked`: the rows of one device (256 tokens) hold between max(12, 1) and 64 ones; the rows of some device hold exactly 64.
All inputs are finite; a program needn't handle non-finite values.
Results may differ from the reference program's by a relative error of at most 0.017.
Values may be sent and summed in bfloat16 or wider, within the bound.
No kernel may reach another device: no remote copies, remote signals or barrier semaphores. Data moves between devices by JAX's collectives and lax.ppermute only.
A program may use at most 64 MiB of HBM per device.

```python
import jax
import jax.numpy as jnp
from jax import lax

D = 768
HEADS = 12
HEAD_DIM = 64
FF = 3072
HASHES = 32
BUCKETS = 256
HALF = 32
TOK_DEV = 256
NSEQ = 1
LEN = 2048
TOKENS = 2048
WIN = 65


def draw_masked(key, part):
    block_count = TOKENS // TOK_DEV
    block_keys = jax.random.split(jax.random.fold_in(key, 11), block_count)
    most_rows = TOK_DEV // 4
    fewest = max(TOK_DEV // 20, 1)
    counts = jax.random.randint(jax.random.fold_in(key, 12), (block_count,), fewest, most_rows + 1)
    busiest = jax.random.randint(jax.random.fold_in(key, 13), (), 0, block_count)
    counts = jnp.where(jnp.arange(block_count) == busiest, most_rows, counts)
    ranked = jax.vmap(lambda subkey: jax.random.permutation(subkey, TOK_DEV))(block_keys)
    return (ranked < counts[:, None]).astype(jnp.int32).reshape(TOKENS)


def with_ends(array, key, least, top_value):
    longest = array.shape.index(max(array.shape))
    spots = []
    for shift in (0, 1):
        where = [jax.random.randint(jax.random.fold_in(key, axis), (), 0, length) for axis, length in enumerate(array.shape)]
        where[longest] = (where[longest] + shift) % array.shape[longest]
        spots.append(tuple(where))
    return array.at[spots[0]].set(least).at[spots[1]].set(top_value)


def steps_of(own_key, dims, cuts, low, largest):
    def one(position, blocks):
        heights = jax.random.uniform(jax.random.fold_in(jax.random.fold_in(own_key, 6), position), (blocks,), jnp.float32, low / len(cuts), largest / len(cuts))
        return jnp.repeat(jnp.exp(heights), dims[position] // blocks).reshape((-1,) + (1,) * (len(dims) - position - 1))

    gain = one(*cuts[0])
    for cut in cuts[1:]:
        gain = gain * one(*cut)
    return gain


def centred(own_key, shape, scale, bound, pieces=(), held_as=jnp.bfloat16):
    array = scale * jax.random.normal(own_key, shape, jnp.float32)
    if pieces:
        array = array * steps_of(own_key, shape, pieces, -0.22, 0.18)
    return jnp.clip(array, -bound, bound).astype(held_as)


def setup_inputs(seed: int = 0) -> dict:
    keys = jax.random.split(jax.random.key(seed), 19)
    inputs = centred(keys[0], (TOKENS, D), 1.0, 6.0, ((0, 8),))
    value_weight = centred(keys[1], (D, D), D ** -0.5, 0.21875, ((1, 4),))
    value_bias = centred(keys[2], (D,), 0.5, 3.0, ((0, 4),), jnp.float32)
    out_weight = centred(keys[3], (D, D), D ** -0.5, 0.21875, ((0, 4),))
    out_bias = centred(keys[4], (D,), 0.5, 3.0, (), jnp.float32)
    first_gain = jnp.clip(1.0 + 0.1 * jax.random.normal(keys[5], (D,), jnp.float32), 0.5, 1.5)
    first_shift = centred(keys[6], (D,), 0.5, 3.0, (), jnp.float32)
    up_weight = centred(keys[7], (D, FF), D ** -0.5, 0.21875, ((1, 4),))
    up_bias = centred(keys[8], (FF,), 0.5, 3.0, ((0, 4),), jnp.float32)
    down_weight = centred(keys[9], (FF, D), FF ** -0.5, 0.109375, ((0, 4),))
    down_bias = centred(keys[10], (D,), 0.5, 3.0, (), jnp.float32)
    second_gain = jnp.clip(1.0 + 0.1 * jax.random.normal(keys[11], (D,), jnp.float32), 0.5, 1.5)
    second_shift = centred(keys[12], (D,), 0.5, 3.0, (), jnp.float32)
    conv_weight = centred(keys[13], (HEADS, WIN), WIN ** -0.5, 0.75, ((0, 4),), jnp.float32)
    query_codes = with_ends(jax.random.randint(keys[14], (TOKENS, HEADS, HASHES), 0, BUCKETS), jax.random.fold_in(keys[14], 1), 0, BUCKETS - 1).astype(jnp.int32)
    key_codes = with_ends(jax.random.randint(keys[15], (TOKENS, HEADS, HASHES), 0, BUCKETS), jax.random.fold_in(keys[15], 1), 0, BUCKETS - 1).astype(jnp.int32)
    masked = draw_masked(jax.random.fold_in(keys[18], 71), 0)
    out_grad = centred(keys[17], (TOKENS, D), 1.0, 6.0, ((0, 8),), jnp.float32)
    return {"inputs": inputs, "value_weight": value_weight, "value_bias": value_bias, "out_weight": out_weight, "out_bias": out_bias, "first_gain": first_gain, "first_shift": first_shift, "up_weight": up_weight, "up_bias": up_bias, "down_weight": down_weight, "down_bias": down_bias, "second_gain": second_gain, "second_shift": second_shift, "conv_weight": conv_weight, "query_codes": query_codes, "key_codes": key_codes, "masked": masked, "out_grad": out_grad}


@jax.custom_vjp
def low(v):
    return lax.optimization_barrier(v.astype(jnp.bfloat16)).astype(jnp.float32)

@jax.custom_vjp
def low_back(v):
    return v

def low_keep(v):
    return (low(v), None)

def low_pass(kept, grad):
    return (grad,)

def back_keep(v):
    return (v, None)

def back_low(kept, grad):
    return (low(grad),)
low.defvjp(low_keep, low_pass)
low_back.defvjp(back_keep, back_low)

def exact_dot(left_side, right_side):
    return jnp.dot(left_side, right_side, precision=lax.Precision.HIGHEST, preferred_element_type=jnp.float32)

def norm_rows(features, norm_gain, norm_shift):
    centre = features - lax.optimization_barrier(jnp.mean(features, -1, keepdims=True))
    spread = lax.optimization_barrier(jnp.mean(centre * centre, -1, keepdims=True))
    return centre * lax.rsqrt(spread + 1e-05) * norm_gain + norm_shift

def attend(value_sum, conv_term):
    scaled = value_sum * lax.rsqrt(lax.optimization_barrier(jnp.mean(value_sum * value_sum, -1, keepdims=True)) + 1e-05)
    return scaled + conv_term

def bucket_read(operands):
    row_block, key_block, query_block = operands
    hash_slots = jnp.broadcast_to(jnp.arange(HASHES, dtype=jnp.int32)[None, :], key_block.shape)
    spread_rows = jnp.broadcast_to(row_block[:, None, :], key_block.shape + (row_block.shape[-1],))
    bucket_table = jnp.zeros((HASHES, BUCKETS, row_block.shape[-1]), row_block.dtype)
    bucket_table = bucket_table.at[hash_slots, key_block].add(spread_rows)
    bucket_table = low(low_back(bucket_table))
    picked = bucket_table[hash_slots, query_block]
    return low_back(lax.optimization_barrier(jnp.sum(picked, 1)))

def by_head(array_in):
    return array_in.reshape(NSEQ, LEN, HEADS, -1).transpose(0, 2, 1, 3).reshape(NSEQ * HEADS, LEN, -1)

def sequence_conv(value_rows, conv_weight):
    kernel = jnp.repeat(conv_weight.T, HEAD_DIM, axis=1)[:, None, :]
    return lax.conv_general_dilated(value_rows, kernel, (1,), ((HALF, HALF),), dimension_numbers=('NWC', 'WIO', 'NWC'), feature_group_count=value_rows.shape[-1], precision=lax.Precision.HIGHEST)

def forward(weights_in, query_codes, key_codes):
    inputs, value_weight, value_bias, out_weight, out_bias, first_gain, first_shift, up_weight, up_bias, down_weight, down_bias, second_gain, second_shift, conv_weight = weights_in
    value_part = low_back(exact_dot(inputs, value_weight) + value_bias).reshape(TOKENS, HEADS, HEAD_DIM)
    value_low = low(value_part)
    bucket_reads = lax.map(jax.checkpoint(bucket_read), (by_head(value_low), by_head(key_codes), by_head(query_codes)))
    bucket_reads = bucket_reads.reshape(NSEQ, HEADS, LEN, HEAD_DIM).transpose(0, 2, 1, 3).reshape(TOKENS, HEADS, HEAD_DIM) / HASHES
    conv_term = sequence_conv(value_low.reshape(NSEQ, LEN, D), conv_weight).reshape(TOKENS, HEADS, HEAD_DIM)
    context = low(low_back(attend(bucket_reads, conv_term).reshape(TOKENS, D)))
    hidden = inputs + low_back(exact_dot(context, out_weight)) + out_bias
    first = norm_rows(hidden, first_gain, first_shift)
    pre_act = low_back(exact_dot(low(first), up_weight) + up_bias)
    activated = low(jax.nn.gelu(pre_act, approximate=False))
    second = first + low_back(exact_dot(activated, down_weight)) + down_bias
    return norm_rows(second, second_gain, second_shift)

def reference(inputs, value_weight, value_bias, out_weight, out_bias, first_gain, first_shift, up_weight, up_bias, down_weight, down_bias, second_gain, second_shift, conv_weight, query_codes, key_codes, masked, out_grad):
    weights_in = tuple((array_in.astype(jnp.float32) for array_in in (inputs, value_weight, value_bias, out_weight, out_bias, first_gain, first_shift, up_weight, up_bias, down_weight, down_bias, second_gain, second_shift, conv_weight)))
    output, pullback = jax.vjp(lambda params: forward(params, query_codes, key_codes), weights_in)
    gradients = pullback(out_grad * masked.astype(jnp.float32)[:, None])[0]
    return (output.astype(jnp.bfloat16), gradients[0], gradients[1], gradients[2], gradients[3], gradients[4], gradients[5], gradients[6], gradients[7], gradients[8], gradients[9], gradients[10], gradients[11], gradients[12], gradients[13])
```

```python
from functools import partial

import jax
import jax.numpy as jnp
import numpy as np
from jax import lax
from jax.experimental import pallas as pl
from jax.experimental.pallas import tpu as pltpu
from jax.sharding import PartitionSpec as P

F32, BF16, I32 = jnp.float32, jnp.bfloat16, jnp.int32
MIB = 1 << 20


def dot(a, b, dims):
    return lax.dot_general(a, b, (dims, ((), ())), preferred_element_type=F32)


def nn(a, b):
    return dot(a, b, ((1,), (0,)))


def nt(a, b):
    return dot(a, b, ((1,), (1,)))


def tn(a, b):
    return dot(a, b, ((0,), (0,)))


def split2(x):
    high = x.astype(BF16)
    return high, (x - high.astype(F32)).astype(BF16)


def split3(x):
    high = x.astype(BF16)
    rest = x - high.astype(F32)
    middle = rest.astype(BF16)
    return high, middle, (rest - middle.astype(F32)).astype(BF16)


def iota(shape, dim):
    return lax.broadcasted_iota(I32, shape, dim)


def one_zero(condition):
    return jnp.where(condition, 1.0, 0.0).astype(BF16)


def call(body, outs, args, name, scratch=(), smem=0, vmem=40, flops=0, moved=0):
    specs = [pl.BlockSpec(memory_space=pltpu.SMEM)] * smem
    specs += [pl.BlockSpec(memory_space=pltpu.VMEM)] * (len(args) - smem)
    shapes = [outs] if isinstance(outs, tuple) else outs
    shapes = [jax.ShapeDtypeStruct(shape, dtype) for shape, dtype in shapes]
    return pl.pallas_call(
        body,
        out_shape=shapes,
        in_specs=specs,
        out_specs=[pl.BlockSpec(memory_space=pltpu.VMEM)] * len(shapes),
        scratch_shapes=list(scratch),
        compiler_params=pltpu.CompilerParams(vmem_limit_bytes=vmem * MIB),
        cost_estimate=pl.CostEstimate(flops=flops, bytes_accessed=moved, transcendentals=0),
        name=name,
    )(*args)


def norm_stats(rows):
    centre = rows - jnp.mean(rows, -1, keepdims=True)
    spread = jnp.mean(centre * centre, -1, keepdims=True)
    q = lax.rsqrt(spread + 1e-05)
    return centre * q, q


def cdf_of(u):
    return 0.5 * (1.0 + lax.erf(u * 0.7071067811865476))


def gelu_grad(u):
    return cdf_of(u) + u * jnp.exp(-0.5 * u * u) * 0.3989422804014327


def plane_weights(heads, hashes):
    lanes = 128
    rows = heads * hashes
    wide = np.zeros((8 * lanes, 2 * lanes), np.float32)
    tall = np.zeros((64, 8 * rows), np.float32)
    for b in range(8):
        for h in range(heads):
            for m in range(hashes):
                half, power = divmod(m, 16)
                wide[b * lanes + h * hashes + m, half * lanes + h * 8 + b] = 2.0**power
                tall[half * 32 + h * 8 + b, b * rows + h * hashes + m] = 2.0**power
    return jnp.asarray(wide, BF16), jnp.asarray(tall, BF16)


def query_words(codes, wide):
    whole = codes.astype(F32).astype(I32)
    bits = jnp.concatenate(
        [((whole >> b) & 1).astype(F32).astype(BF16) for b in range(8)], axis=1
    )
    both = nn(bits, wide)
    return both[:, :128].astype(I32) | (both[:, 128:].astype(I32) << 16)


def key_words(codes, tall):
    whole = codes.astype(F32).astype(I32)
    bits = jnp.concatenate(
        [((whole >> b) & 1).astype(F32).astype(BF16) for b in range(8)], axis=0
    )
    both = nn(tall, bits)
    return both[:32].astype(I32) | (both[32:].astype(I32) << 16)


def matches(query_block, key_block, head):
    apart = None
    for b in range(8):
        word = head * 8 + b
        unlike = query_block[:, word : word + 1] ^ key_block[word : word + 1, :]
        apart = unlike if apart is None else apart | unlike
    return (32 - lax.population_count(apart)).astype(F32).astype(BF16)


def per_device(
    inputs,
    value_weight,
    value_bias,
    out_weight,
    out_bias,
    first_gain,
    first_shift,
    up_weight,
    up_bias,
    down_weight,
    down_bias,
    second_gain,
    second_shift,
    conv_weight,
    query_codes,
    key_codes,
    masked,
    out_grad,
):
    n = lax.axis_size("seq")
    tp = lax.axis_size("tp")
    tokens, width = inputs.shape
    heads, hashes = query_codes.shape[1], query_codes.shape[2]
    taps = conv_weight.shape[1]
    half = (taps - 1) // 2
    local = value_weight.shape[1]
    dim = local // heads
    hidden_units = up_weight.shape[1]
    chosen = tokens // 4
    rest = tokens - chosen
    piece = rest // tp
    codes_rows = heads * hashes
    window = tokens + 128
    total = n * chosen
    seq_id, tp_id = lax.axis_index("seq"), lax.axis_index("tp")
    ids = jnp.stack([seq_id, tp_id]).astype(I32)
    wide, tall = plane_weights(heads, hashes)

    def swap(array, k):
        return lax.ppermute(array, "tp", [(i, i ^ k) for i in range(tp)])

    def others(array):
        return [swap(array, k) for k in range(1, tp)]

    def exchange(array):
        return lax.all_to_all(array, "seq", 0, 0)

    def row(vector):
        return vector.reshape(1, -1)

    query_t = jnp.transpose(query_codes, (1, 2, 0)).reshape(codes_rows, tokens)
    key_t = jnp.transpose(key_codes, (1, 2, 0)).reshape(codes_rows, tokens)
    value_t = value_weight.T

    def order_body(masked_ref, query_ref, chosen_ref, rest_ref, order_ref):
        flags = jnp.broadcast_to(masked_ref[...].astype(F32), (8, tokens))
        upto = one_zero(iota((tokens, tokens), 0) <= iota((tokens, tokens), 1))
        count = nn(flags.astype(BF16), upto)
        spot = iota((8, tokens), 1).astype(F32)
        target = jnp.where(flags > 0, count - 1.0, count[:, tokens - 1 :] + spot - count)
        order = one_zero(iota((tokens, tokens), 0) == target[:1].astype(I32))
        order_ref[...] = order
        where = jnp.where(
            iota((128 - codes_rows, tokens), 0) == 0, iota((128 - codes_rows, tokens), 1), 0
        )
        table = jnp.concatenate([query_ref[...], where], axis=0).astype(F32).astype(BF16)
        sorted_codes = nt(order, table).astype(BF16)
        for i in range(n):
            chosen_ref[i] = sorted_codes[:chosen]
        rest_ref[...] = sorted_codes[chosen:]

    chosen_codes, rest_codes, order = call(
        order_body,
        [((n, chosen, 128), BF16), ((rest, 128), BF16), ((tokens, tokens), BF16)],
        (row(masked), query_t),
        "order",
    )
    all_codes = exchange(chosen_codes)

    def value_body(inputs_ref, weight_ref, bias_ref, key_ref, value_ref, send_ref):
        values = (nt(inputs_ref[...], weight_ref[...]) + bias_ref[...]).astype(BF16)
        value_ref[...] = values
        same = one_zero(iota((local, local), 0) == iota((local, local), 1))
        send_ref[:codes_rows] = key_ref[...].astype(F32).astype(BF16)
        send_ref[codes_rows:] = nt(same, values).astype(BF16)

    values, value_send = call(
        value_body,
        [((tokens, local), BF16), ((codes_rows + local, tokens), BF16)],
        (inputs, value_t, row(value_bias), key_t),
        "values",
    )
    all_keys = lax.all_gather(value_send, "seq", axis=0)
    out_all = lax.all_gather(out_weight, "tp", axis=0)
    value_all = lax.all_gather(value_t, "tp", axis=0)

    def sort_body(order_ref, inputs_ref, grad_ref, masked_ref, sorted_ref, cot_ref):
        sorted_ref[...] = nn(order_ref[...], inputs_ref[...]).astype(BF16)
        pick = order_ref[:chosen]
        flags = jnp.broadcast_to(masked_ref[...].astype(F32), (8, tokens)).astype(BF16)
        valid = nt(pick, flags)[:, :1]
        parts = split3(grad_ref[...])
        cot_ref[...] = (nn(pick, parts[0]) + nn(pick, parts[1]) + nn(pick, parts[2])) * valid

    sorted_inputs, cot = call(
        sort_body,
        [((tokens, width), BF16), ((chosen, width), F32)],
        (order, inputs, out_grad, row(masked)),
        "sort",
    )

    def taps_body(order_ref, conv_ref, ahead_ref, back_ref, pad_ref):
        pad_ref[...] = jnp.zeros_like(pad_ref)
        pad_ref[:heads, :taps] = conv_ref[...]
        turn = one_zero(iota((128, 128), 0) + iota((128, 128), 1) == taps - 1)
        padded = pad_ref[:, :128]
        parts = split3(padded)
        turned = nn(parts[0], turn) + nn(parts[1], turn) + nn(parts[2], turn)
        blank = jnp.zeros((8, window - 128), F32)
        ahead = jnp.concatenate([padded, blank], axis=1)
        back = jnp.concatenate([turned, blank], axis=1)
        for h in range(heads):
            for source, ref in ((ahead, ahead_ref), (back, back_ref)):
                spread = jnp.broadcast_to(source[h : h + 1], (tokens, window))
                band = pltpu.roll(spread, 0, 1, stride=1, stride_axis=0)
                high, low = split2(band)
                if ref is ahead_ref:
                    high = nn(order_ref[...], high).astype(BF16)
                    low = nn(order_ref[...], low).astype(BF16)
                ref[h, :, :window] = high
                ref[h, :, window:] = low

    bands, back_bands = call(
        taps_body,
        [((heads, tokens, 2 * window), BF16)] * 2,
        (order, conv_weight),
        "taps",
        scratch=[pltpu.VMEM((8, 128), F32)],
    )

    def count_body(ids_ref, codes_ref, send_ref, value_ref, wide_ref, tall_ref, count_ref, out_ref):
        me = ids_ref[0]
        keys = key_words(send_ref[:codes_rows], tall_ref[...])
        queries = query_words(codes_ref[...].reshape(total, 128), wide_ref[...])
        for h in range(heads):
            turned = send_ref[codes_rows + h * dim : codes_rows + (h + 1) * dim]
            for r in range(0, total, tokens):
                for c in range(0, tokens, 128):
                    count_ref[h, r : r + tokens, c : c + 128] = matches(
                        queries[r : r + tokens], keys[:, c : c + 128], h
                    )
            read = nt(count_ref[h], turned).astype(BF16)
            for i in range(n):
                out_ref[i, :chosen, h * dim : (h + 1) * dim] = read[i * chosen : (i + 1) * chosen]
        for i in range(n):
            last, head_rows = value_ref[tokens - half :], value_ref[:half]
            rows = jnp.where(i == me + 1, last.astype(F32), head_rows.astype(F32))
            out_ref[i, chosen:] = rows.astype(BF16)

    counts, reads = call(
        count_body,
        [((heads, total, tokens), BF16), ((n, chosen + half, local), BF16)],
        (ids, all_codes, value_send, values, wide, tall),
        "count",
        smem=1,
    )
    reads = exchange(reads)

    def unit_rows(value_sum):
        return lax.rsqrt(jnp.mean(value_sum * value_sum, -1, keepdims=True) + 1e-05)

    def context_body(ids_ref, reads_ref, value_ref, band_ref, context_ref, sum_ref, near_ref):
        me = ids_ref[0]
        total_read = reads_ref[0, :chosen].astype(F32)
        for i in range(1, n):
            total_read += reads_ref[i, :chosen].astype(F32)
        total_read = total_read * (1.0 / hashes)
        sum_ref[...] = total_read
        before = reads_ref[jnp.maximum(me - 1, 0), chosen:].astype(F32)
        after = reads_ref[jnp.minimum(me + 1, n - 1), chosen:].astype(F32)
        near_ref[:half] = jnp.where(me > 0, before, 0.0).astype(BF16)
        near_ref[half : half + tokens] = value_ref[...]
        near_ref[half + tokens : 2 * half + tokens] = jnp.where(me < n - 1, after, 0.0).astype(BF16)
        near_ref[2 * half + tokens :] = jnp.zeros((window - tokens - 2 * half, local), BF16)
        near = near_ref[...]
        twice = jnp.concatenate([near, near], axis=0)
        for h in range(heads):
            cols = slice(h * dim, (h + 1) * dim)
            mine = total_read[:, cols]
            conv = nn(band_ref[h, :chosen], twice[:, cols])
            context_ref[:, cols] = (mine * unit_rows(mine) + conv).astype(BF16)

    context, value_sum, near = call(
        context_body,
        [((chosen, local), BF16), ((chosen, local), F32), ((window, local), BF16)],
        (ids, reads, values, bands),
        "context",
        smem=1,
    )
    contexts = [context] + others(context)

    def joined(ids_ref, context_refs, out_ref):
        mine = ids_ref[1]
        terms = [nn(ref[...], out_ref[mine ^ k]) for k, ref in enumerate(context_refs)]
        return paired(terms)

    def paired(terms):
        while len(terms) > 1:
            terms = [terms[i] + terms[i + 1] for i in range(0, len(terms), 2)]
        return terms[0]

    def feed(low, up_ref, up_bias_ref, down_ref):
        pre = nn(low, up_ref[...]) + up_bias_ref[...]
        act = (pre * cdf_of(pre)).astype(BF16)
        return pre, nn(act, down_ref[...]).astype(BF16)

    def first_body(ids_ref, *refs):
        context_refs, refs = refs[:tp], refs[tp:]
        (out_ref, inputs_ref, bias_ref, gain_ref, shift_ref, up_ref, up_bias_ref, down_ref, sum_ref,
         hidden_ref, first_ref, pre_ref, part_ref, keep_ref) = refs
        hidden = inputs_ref[:chosen].astype(F32) + joined(ids_ref, context_refs, out_ref) + bias_ref[...]
        hidden_ref[...] = hidden
        unit, _ = norm_stats(hidden)
        first = unit * gain_ref[...] + shift_ref[...]
        first_ref[...] = first
        low = first.astype(BF16)
        pre, part = feed(low, up_ref, up_bias_ref, down_ref)
        pre_ref[...] = pre
        part_ref[...] = part
        keep_ref[:, :width] = low
        keep_ref[:, width : width + local] = context_refs[0][...]
        keep_ref[:, width + local :] = sum_ref[...].astype(BF16)

    hidden, first, pre_act, part, keep = call(
        first_body,
        [((chosen, width), F32), ((chosen, width), F32), ((chosen, hidden_units), F32),
         ((chosen, width), BF16), ((chosen, width + 2 * local), BF16)],
        (ids, *contexts, out_all, sorted_inputs, row(out_bias), row(first_gain), row(first_shift),
         up_weight, row(up_bias), down_weight, value_sum),
        "first",
        smem=1,
    )
    parts = [part] + others(part)
    keeps = lax.all_gather(keep, "seq", axis=0)

    def slope_body(pre_ref, slope_ref):
        slope_ref[...] = gelu_grad(pre_ref[...])

    (slope,) = call(slope_body, ((chosen, hidden_units), F32), (pre_act,), "slope")

    def back_norm(grad, unit, q, gain):
        scaled = grad * gain
        return q * (
            scaled
            - jnp.mean(scaled, -1, keepdims=True)
            - unit * jnp.mean(scaled * unit, -1, keepdims=True)
        )

    def put_sums(ref, sums):
        for i, vector in enumerate(sums):
            ref[i : i + 1] = vector

    def column_sum(array):
        return jnp.sum(array, 0, keepdims=True)

    def second_body(*refs):
        part_refs, refs = refs[:tp], refs[tp:]
        (first_ref, bias_ref, gain_ref, shift_ref, cot_ref, slope_ref, down_ref, up_ref,
         output_ref, grad_ref, back_ref, sums_ref, send_ref) = refs
        second = first_ref[...] + paired([r[...].astype(F32) for r in part_refs]) + bias_ref[...]
        unit, q = norm_stats(second)
        output_ref[...] = (unit * gain_ref[...] + shift_ref[...]).astype(BF16)
        grad = back_norm(cot_ref[...], unit, q, gain_ref[...])
        grad_ref[...] = grad
        low = grad.astype(BF16)
        grad_pre = (nt(low, down_ref[...]) * slope_ref[...]).astype(BF16)
        back_ref[...] = nt(grad_pre, up_ref[...]).astype(BF16)
        put_sums(sums_ref, [column_sum(cot_ref[...] * unit), column_sum(cot_ref[...]), column_sum(grad)])
        send_ref[:, :width] = low
        send_ref[:, width:] = jnp.zeros((chosen, send_ref.shape[1] - width), BF16)

    out_chosen, grad_second, back, sums, down_send = call(
        second_body,
        [((chosen, width), BF16), ((chosen, width), F32), ((chosen, width), BF16), ((8, width), F32),
         ((chosen, width + 256), BF16)],
        (*parts, first, row(down_bias), row(second_gain), row(second_shift), cot, slope, down_weight,
         up_weight),
        "second",
    )
    backs = [back] + others(back)
    down_all = lax.all_gather(down_send, "seq", axis=0)
    part_width = width // 2

    def hidden_body(ids_ref, *refs):
        back_refs, refs = refs[:tp], refs[tp:]
        grad_ref, hidden_ref, gain_ref, sums_ref, out_ref, send_ref, attn_ref, sum_ref = refs
        side = ids_ref[1] % 2
        grad = grad_ref[...] + paired([r[...].astype(F32) for r in back_refs])
        unit, q = norm_stats(hidden_ref[...])
        grad_hidden = back_norm(grad, unit, q, gain_ref[...])
        out_ref[...] = grad_hidden
        attn_ref[...] = grad_hidden.astype(BF16)
        sum_ref[...] = jnp.zeros_like(sum_ref)
        sum_ref[:3] = sums_ref[:3]
        put_sums(sum_ref.at[3:6], [column_sum(grad * unit), column_sum(grad), column_sum(grad_hidden)])
        lanes = pl.ds(pl.multiple_of(side * part_width, part_width), part_width)
        mine, mine_sums = attn_ref[:, lanes], sum_ref[:, lanes].astype(BF16)
        for i in range(n):
            send_ref[i, :chosen] = mine
            send_ref[i, chosen:] = mine_sums

    grad_hidden, attn_send = call(
        hidden_body,
        [((chosen, width), F32), ((n, chosen + 16, part_width), BF16)],
        (ids, *backs, grad_second, hidden, row(first_gain), sums),
        "hidden",
        smem=1,
        scratch=[pltpu.VMEM((chosen, width), BF16), pltpu.VMEM((16, width), F32)],
    )
    attn_mine = exchange(attn_send)
    attn_other = swap(attn_mine, 1)

    def values_body(ids_ref, mine_ref, other_ref, out_ref, keep_ref, count_ref, band_ref, codes_ref,
                    grad_ref, dense_ref, attn_ref, sums_ref, y_ref, read_ref):
        me, side = ids_ref[0], ids_ref[1] % 2
        own = pl.ds(pl.multiple_of(side * part_width, part_width), part_width)
        far = pl.ds(pl.multiple_of((1 - side) * part_width, part_width), part_width)
        for ref, lanes in ((mine_ref, own), (other_ref, far)):
            for i in range(n):
                attn_ref[i * chosen : (i + 1) * chosen, lanes] = ref[i, :chosen]
            sum_all = ref[0, chosen:].astype(F32)
            for i in range(1, n):
                sum_all += ref[i, chosen:].astype(F32)
            sums_ref[:, lanes] = sum_all
        y = nt(attn_ref[...], out_ref[...]).astype(BF16)
        y_ref[...] = y
        for h in range(heads):
            cols = slice(h * dim, (h + 1) * dim)
            read = keep_ref[:, :, width + local + h * dim : width + local + (h + 1) * dim]
            read = read.reshape(total, dim).astype(F32)
            grad = y[:, cols].astype(F32)
            r = unit_rows(read)
            back = r * (grad - read * (r * r) * jnp.mean(grad * read, -1, keepdims=True))
            read_ref[:, cols] = (back * (1.0 / hashes)).astype(BF16)
        dense = jnp.zeros((window, local), F32)
        for step in (-1, 0, 1):
            source = jnp.clip(me + step, 0, n - 1)
            inside = jnp.logical_and(me + step >= 0, me + step < n)
            there = y_ref[pl.ds(pl.multiple_of(source * chosen, chosen), chosen)]
            spots = codes_ref[source][:, codes_rows : codes_rows + 1].astype(F32).astype(I32)
            spots = jnp.where(inside, spots + step * tokens + half, -1)
            place = one_zero(spots == iota((chosen, window), 1))
            dense += tn(place, there)
        dense_low = dense.astype(BF16)
        dense_ref[...] = dense_low
        twice = jnp.concatenate([dense_low, dense_low], axis=0)
        for h in range(heads):
            cols = slice(h * dim, (h + 1) * dim)
            grad = tn(count_ref[h], read_ref[:, cols]) + nn(band_ref[h], twice[:, cols])
            grad_ref[:, cols] = grad.astype(BF16)

    grad_values, dense, attn_all, vectors = call(
        values_body,
        [((tokens, local), BF16), ((window, local), BF16), ((total, width), BF16), ((16, width), F32)],
        (ids, attn_mine, attn_other, out_weight, keeps, counts, back_bands, all_codes),
        "values_back",
        smem=1,
        scratch=[pltpu.VMEM((total, local), BF16), pltpu.VMEM((total, local), BF16)],
    )
    grads = [grad_values] + others(grad_values)

    share = local // n
    extra = 8

    def value_grad_body(inputs_ref, grad_ref, dense_ref, near_ref, send_ref, row_ref):
        grad = grad_ref[...]
        weight = tn(grad, inputs_ref[...]).astype(BF16)
        row_ref[...] = jnp.zeros_like(row_ref)
        row_ref[:1, :local] = column_sum(grad.astype(F32))
        turn = one_zero(iota((tokens, tokens), 0) + iota((tokens, tokens), 1) == tokens - 1)
        turned = nn(turn, dense_ref[half : half + tokens]).astype(BF16)
        for h in range(heads):
            cols = slice(h * dim, (h + 1) * dim)
            both = nt(turned[:, cols], near_ref[:, cols])
            aligned = pltpu.roll(both, window - tokens + 1, 1, stride=1, stride_axis=0)
            row_ref[1 + h : 2 + h, :128] = column_sum(aligned)[:, :128]
        for i in range(n):
            send_ref[i, :share] = weight[i * share : (i + 1) * share]
            send_ref[i, share:] = row_ref[...].astype(BF16)

    (value_part,) = call(
        value_grad_body,
        ((n, share + extra, width), BF16),
        (inputs, grad_values, dense, near),
        "value_grad",
        scratch=[pltpu.VMEM((extra, width), F32)],
    )
    value_part = exchange(value_part)

    def value_sum_body(part_ref, send_ref, row_ref):
        whole = part_ref[0].astype(F32)
        for i in range(1, n):
            whole += part_ref[i].astype(F32)
        for i in range(n):
            send_ref[i] = whole[:share].astype(BF16)
        row_ref[...] = whole[share:]

    value_send_back, value_rows = call(
        value_sum_body,
        [((n, share, width), BF16), ((extra, width), F32)],
        (value_part,),
        "value_sums",
    )
    value_grad = exchange(value_send_back).reshape(local, width).astype(F32).T

    def input_body(ids_ref, *refs):
        grad_refs, refs = refs[:tp], refs[tp:]
        weight_ref, order_ref, hidden_ref, out_ref = refs
        mine = ids_ref[1]
        pick = order_ref[:chosen]
        parts = split3(hidden_ref[...])
        placed = tn(pick, parts[0]) + tn(pick, parts[1]) + tn(pick, parts[2])
        terms = [nn(ref[...], weight_ref[mine ^ k]) for k, ref in enumerate(grad_refs)]
        out_ref[...] = placed + paired(terms)

    (input_grad,) = call(
        input_body,
        ((tokens, width), F32),
        (ids, *grads, value_all, order, grad_hidden),
        "input_grad",
        smem=1,
    )

    step_rows = chosen

    def weights_body(keep_ref, down_ref, up_w_ref, up_bias_ref, down_w_ref,
                     up_ref, up_sum_ref, grad_ref, act_ref, pre_ref):
        up_sum_ref[...] = jnp.zeros_like(up_sum_ref)

        @pl.loop(0, n)
        def _(i):
            rows = pl.ds(pl.multiple_of(i * step_rows, step_rows), step_rows)
            pre = nn(keep_ref[i, :, :width], up_w_ref[...]) + up_bias_ref[...]
            cdf = cdf_of(pre)
            act_ref[rows] = (pre * cdf).astype(BF16)
            slope = cdf + pre * jnp.exp(-0.5 * pre * pre) * 0.3989422804014327
            grad_pre = (nt(down_ref[i, :, :width], down_w_ref[...]) * slope).astype(BF16)
            pre_ref[rows] = grad_pre
            up_sum_ref[:1] += column_sum(grad_pre.astype(F32))

        first_low = keep_ref[:, :, :width].reshape(total, width)
        up_ref[...] = tn(first_low, pre_ref[...])
        grad_ref[...] = tn(act_ref[...], down_ref[:, :, :width].reshape(total, width))

    grad_up, up_sum, grad_down = call(
        weights_body,
        [((width, hidden_units), F32), ((8, hidden_units), F32), ((hidden_units, width), F32)],
        (keeps, down_all, up_weight, row(up_bias), down_weight),
        "weights",
        scratch=[pltpu.VMEM((total, hidden_units), BF16), pltpu.VMEM((total, hidden_units), BF16)],
    )

    def out_grad_body(keep_ref, attn_ref, out_ref):
        context_all = keep_ref[:, :, width : width + local].reshape(total, local)
        out_ref[...] = tn(context_all, attn_ref[...])

    (grad_out,) = call(out_grad_body, ((local, width), F32), (keeps, attn_all), "out_grad")

    def rest_body(codes_ref, keys_ref, wide_ref, tall_ref, band_ref, near_ref, context_ref,
                  count_ref, sum_ref):
        queries = query_words(codes_ref[...], wide_ref[...])
        sum_ref[...] = jnp.zeros_like(sum_ref)

        @pl.loop(0, n)
        def _(i):
            block = keys_ref[i]
            keys = key_words(block[:codes_rows], tall_ref[...])
            for h in range(heads):
                for c in range(0, tokens, 128):
                    count_ref[:, c : c + 128] = matches(queries, keys[:, c : c + 128], h)
                turned = block[codes_rows + h * dim : codes_rows + (h + 1) * dim]
                sum_ref[:, h * dim : (h + 1) * dim] += nt(count_ref[...], turned)

        near = near_ref[...]
        twice = jnp.concatenate([near, near], axis=0)
        for h in range(heads):
            cols = slice(h * dim, (h + 1) * dim)
            mine = sum_ref[:, cols] * (1.0 / hashes)
            conv = nn(band_ref[h, chosen:], twice[:, cols])
            context_ref[:, cols] = (mine * unit_rows(mine) + conv).astype(BF16)

    (rest_context,) = call(
        rest_body,
        ((rest, local), BF16),
        (rest_codes, all_keys, wide, tall, bands, near),
        "rest_context",
        scratch=[pltpu.VMEM((rest, tokens), BF16), pltpu.VMEM((rest, local), F32)],
    )
    rest_contexts = [rest_context] + others(rest_context)

    def rest_first_body(ids_ref, *refs):
        context_refs, refs = refs[:tp], refs[tp:]
        (out_ref, inputs_ref, bias_ref, gain_ref, shift_ref, up_ref, up_bias_ref, down_ref), refs = (
            refs[:8], refs[8:])
        send_refs, (first_ref, all_ref, part_ref) = refs[:tp], refs[tp:]
        mine = ids_ref[1]
        hidden = inputs_ref[chosen:].astype(F32) + joined(ids_ref, context_refs, out_ref) + bias_ref[...]
        unit, _ = norm_stats(hidden)
        first = unit * gain_ref[...] + shift_ref[...]
        all_ref[...] = first
        part_ref[...] = feed(first.astype(BF16), up_ref, up_bias_ref, down_ref)[1]
        for k in range(tp):
            rows = pl.ds(pl.multiple_of((mine ^ k) * piece, piece), piece)
            send_refs[k][...] = part_ref[rows]
        first_ref[...] = all_ref[pl.ds(pl.multiple_of(mine * piece, piece), piece)]

    *rest_parts, rest_first = call(
        rest_first_body,
        [((piece, width), BF16)] * tp + [((piece, width), F32)],
        (ids, *rest_contexts, out_all, sorted_inputs, row(out_bias), row(first_gain), row(first_shift),
         up_weight, row(up_bias), down_weight),
        "rest_first",
        smem=1,
        scratch=[pltpu.VMEM((rest, width), F32), pltpu.VMEM((rest, width), BF16)],
    )
    rest_parts = [rest_parts[0]] + [swap(rest_parts[k], k) for k in range(1, tp)]

    def rest_second_body(*refs):
        part_refs, (first_ref, bias_ref, gain_ref, shift_ref, out_ref) = refs[:tp], refs[tp:]
        second = first_ref[...] + paired([r[...].astype(F32) for r in part_refs]) + bias_ref[...]
        unit, _ = norm_stats(second)
        out_ref[...] = (unit * gain_ref[...] + shift_ref[...]).astype(BF16)

    (rest_out,) = call(
        rest_second_body,
        ((piece, width), BF16),
        (*rest_parts, rest_first, row(down_bias), row(second_gain), row(second_shift)),
        "rest_second",
    )
    rest_outs = [rest_out] + others(rest_out)

    def output_body(ids_ref, *refs):
        out_refs, (chosen_ref, order_ref, out_ref, sorted_ref) = refs[:tp], refs[tp:]
        mine = ids_ref[1]
        sorted_ref[:chosen] = chosen_ref[...]
        for k in range(tp):
            rows = pl.ds(pl.multiple_of(chosen + (mine ^ k) * piece, 16), piece)
            sorted_ref[rows] = out_refs[k][...]
        out_ref[...] = tn(order_ref[...], sorted_ref[...]).astype(BF16)

    (output,) = call(
        output_body,
        ((tokens, width), BF16),
        (ids, *rest_outs, out_chosen, order),
        "output",
        smem=1,
        scratch=[pltpu.VMEM((tokens, width), BF16)],
    )
    return (
        output,
        input_grad,
        value_grad,
        value_rows[0, :local],
        grad_out,
        vectors[5],
        vectors[3],
        vectors[4],
        grad_up,
        up_sum[0],
        grad_down,
        vectors[2],
        vectors[0],
        vectors[1],
        value_rows[1 : 1 + heads, :taps],
    )


def solution(mesh):
    return jax.shard_map(
        per_device,
        mesh=mesh,
        in_specs=(
            P("seq", None),
            P(None, "tp"),
            P("tp"),
            P("tp", None),
            P(),
            P(),
            P(),
            P(None, "tp"),
            P("tp"),
            P("tp", None),
            P(),
            P(),
            P(),
            P("tp", None),
            P("seq", "tp", None),
            P("seq", "tp", None),
            P("seq"),
            P("seq", None),
        ),
        out_specs=(
            P("seq", None),
            P("seq", None),
            P(None, "tp"),
            P("tp"),
            P("tp", None),
            P(),
            P(),
            P(),
            P(None, "tp"),
            P("tp"),
            P("tp", None),
            P(),
            P(),
            P(),
            P("tp", None),
        ),
        check_vma=False,
    )
```

```python
from functools import partial

import jax
import jax.numpy as jnp
import numpy as np
from jax import lax
from jax.experimental import pallas as pl
from jax.experimental.pallas import tpu as pltpu
from jax.sharding import PartitionSpec as P

F32, BF16, I32 = jnp.float32, jnp.bfloat16, jnp.int32
MIB = 1 << 20
VMEM_MIB = 20


def dot(a, b, dims):
    return lax.dot_general(a, b, (dims, ((), ())), preferred_element_type=F32)


def nn(a, b):
    return dot(a, b, ((1,), (0,)))


def nt(a, b):
    return dot(a, b, ((1,), (1,)))


def tn(a, b):
    return dot(a, b, ((0,), (0,)))


def split2(x):
    high = x.astype(BF16)
    return high, (x - high.astype(F32)).astype(BF16)


def split3(x):
    high = x.astype(BF16)
    rest = x - high.astype(F32)
    middle = rest.astype(BF16)
    return high, middle, (rest - middle.astype(F32)).astype(BF16)


def iota(shape, dim):
    return lax.broadcasted_iota(I32, shape, dim)


def one_zero(condition):
    return jnp.where(condition, 1.0, 0.0).astype(BF16)


def call(body, outs, args, name, scratch=(), smem=0, far=(), far_out=(), late=(), early=(),
         after=(), us=1.0):
    shapes = [outs] if isinstance(outs, tuple) else outs
    count = len(args)
    arrays = [*args, *(jax.ShapeDtypeStruct(shape, dtype) for shape, dtype in shapes)]
    moved = [*far, *(count + i for i in far_out)]
    spaces = [
        pltpu.SMEM if i < smem else pltpu.HBM if i in moved else pltpu.VMEM for i in range(len(arrays))
    ]
    inner = [pltpu.VMEM(arrays[i].shape, arrays[i].dtype) for i in moved]
    extra = len(after)

    held = sum(
        int(np.prod(ref.shape)) * jnp.dtype(ref.dtype).itemsize for ref in (*inner, *scratch)
    )
    limit = max(VMEM_MIB * MIB, held + 12 * MIB)

    def kernel(*refs):
        refs = list(refs[:count] + refs[count + extra :])
        given, here, rest = refs[: len(arrays)], refs[len(arrays) :][: len(inner)], refs[len(arrays) + len(inner) :]
        copies = []
        for slot, i in enumerate(moved):
            pair = (refs[i], here[slot]) if i < count else (here[slot], refs[i])
            copies.append(pltpu.make_async_copy(*pair, rest[-1].at[slot]))
            given[i] = here[slot]
        for copy in copies[: len(far)]:
            copy.start()
        for i, copy in zip(far, copies):
            if i not in late:
                copy.wait()

        def ready():
            for i, copy in zip(far, copies):
                if i in late:
                    copy.wait()

        sends = dict(zip(far_out, copies[len(far) :]))

        def finish(i):
            sends[i].start()

        options = {"ready": ready} if late else {}
        if early:
            options["finish"] = finish
        body(*given, *(rest[:-1] if moved else rest), **options)
        for i in sends:
            if i not in early:
                finish(i)
        for copy in sends.values():
            copy.wait()

    placed = [
        a if i < smem else pltpu.with_memory_space_constraint(a, spaces[i]) for i, a in enumerate(args)
    ]
    return pl.pallas_call(
        kernel,
        out_shape=[spaces[i](arrays[i].shape, arrays[i].dtype) for i in range(count, len(arrays))],
        in_specs=[pl.BlockSpec(memory_space=space) for space in spaces[:count]]
        + [pl.BlockSpec(memory_space=space) for _, space in after],
        out_specs=[pl.BlockSpec(memory_space=space) for space in spaces[count:]],
        scratch_shapes=[*inner, *scratch, *([pltpu.SemaphoreType.DMA((len(inner),))] if moved else [])],
        compiler_params=pltpu.CompilerParams(vmem_limit_bytes=limit),
        cost_estimate=pl.CostEstimate(
            flops=int(us * 1.1e9), bytes_accessed=0, transcendentals=0
        ),
        name=name,
    )(*placed, *(pltpu.with_memory_space_constraint(*pair) for pair in after))


def line(ref):
    return ref[...].reshape(1, ref.shape[0])


def norm_stats(rows):
    centre = rows - jnp.mean(rows, -1, keepdims=True)
    spread = jnp.mean(centre * centre, -1, keepdims=True)
    q = lax.rsqrt(spread + 1e-05)
    return centre * q, q


def cdf_of(u):
    return 0.5 * (1.0 + lax.erf(u * 0.7071067811865476))


def gelu_grad(u):
    return cdf_of(u) + u * jnp.exp(-0.5 * u * u) * 0.3989422804014327


def plane_weights(heads, hashes):
    lanes = 128
    rows = heads * hashes
    wide = np.zeros((8 * lanes, 2 * lanes), np.float32)
    tall = np.zeros((64, 8 * rows), np.float32)
    for b in range(8):
        for h in range(heads):
            for m in range(hashes):
                half, power = divmod(m, 16)
                wide[b * lanes + h * hashes + m, half * lanes + h * 8 + b] = 2.0**power
                tall[half * 32 + h * 8 + b, b * rows + h * hashes + m] = 2.0**power
    return jnp.asarray(wide, BF16), jnp.asarray(tall, BF16)


def query_words(codes, wide):
    whole = codes.astype(F32).astype(I32)
    bits = jnp.concatenate(
        [((whole >> b) & 1).astype(F32).astype(BF16) for b in range(8)], axis=1
    )
    both = nn(bits, wide)
    return both[:, :128].astype(I32) | (both[:, 128:].astype(I32) << 16)


def key_words(codes, tall):
    whole = codes.astype(F32).astype(I32)
    bits = jnp.concatenate(
        [((whole >> b) & 1).astype(F32).astype(BF16) for b in range(8)], axis=0
    )
    both = nn(tall, bits)
    return both[:32].astype(I32) | (both[32:].astype(I32) << 16)


def matches(query_block, key_block, head):
    apart = None
    for b in range(8):
        word = head * 8 + b
        unlike = query_block[:, word : word + 1] ^ key_block[word : word + 1, :]
        apart = unlike if apart is None else apart | unlike
    return (32 - lax.population_count(apart)).astype(F32).astype(BF16)


def per_device(
    inputs,
    value_weight,
    value_bias,
    out_weight,
    out_bias,
    first_gain,
    first_shift,
    up_weight,
    up_bias,
    down_weight,
    down_bias,
    second_gain,
    second_shift,
    conv_weight,
    query_codes,
    key_codes,
    masked,
    out_grad,
):
    n = lax.axis_size("seq")
    tp = lax.axis_size("tp")
    tokens, width = inputs.shape
    heads, hashes = query_codes.shape[1], query_codes.shape[2]
    taps = conv_weight.shape[1]
    half = (taps - 1) // 2
    local = value_weight.shape[1]
    dim = local // heads
    units = up_weight.shape[1]
    chosen = tokens // 4
    rest = tokens - chosen
    piece = rest // tp
    part_rows = chosen // tp
    part_width = width // 2
    codes_rows = heads * hashes
    window = tokens + 128
    total = n * chosen
    ids = jnp.stack([lax.axis_index("seq"), lax.axis_index("tp")]).astype(I32)
    wide, tall = plane_weights(heads, hashes)

    previous = []

    def run(*args, also=(), **options):
        results = call(*args, after=(*previous, *also), **options)
        previous[:] = [(results[0], pltpu.HBM if 0 in options.get("far_out", ()) else pltpu.VMEM)]
        return results

    def swap(array, k):
        return lax.ppermute(array, "tp", [(i, i ^ k) for i in range(tp)])

    def others(array):
        return [swap(array, k) for k in range(1, tp)]

    def exchange(array):
        return lax.all_to_all(array, "seq", 0, 0)

    query_t = jnp.transpose(query_codes, (1, 2, 0)).reshape(codes_rows, tokens)
    key_t = jnp.transpose(key_codes, (1, 2, 0)).reshape(codes_rows, tokens)
    value_t = value_weight.T
    out_all = [out_weight] + others(out_weight)
    value_all = [value_t] + others(value_t)

    def order_body(masked_ref, query_ref, chosen_ref, rest_ref, order_ref):
        flags = jnp.broadcast_to(line(masked_ref).astype(F32), (8, tokens))
        upto = one_zero(iota((tokens, tokens), 0) <= iota((tokens, tokens), 1))
        count = nn(flags.astype(BF16), upto)
        spot = iota((8, tokens), 1).astype(F32)
        target = jnp.where(flags > 0, count - 1.0, count[:, tokens - 1 :] + spot - count)
        order = one_zero(iota((tokens, tokens), 0) == target[:1].astype(I32))
        order_ref[...] = order
        where = jnp.where(
            iota((128 - codes_rows, tokens), 0) == 0, iota((128 - codes_rows, tokens), 1), 0
        )
        table = jnp.concatenate([query_ref[...], where], axis=0).astype(F32).astype(BF16)
        sorted_codes = nt(order, table).astype(BF16)
        for i in range(n):
            chosen_ref[i] = sorted_codes[:chosen]
        rest_ref[...] = sorted_codes[chosen:]

    chosen_codes, rest_codes, order = run(
        order_body,
        [((n, chosen, 128), BF16), ((rest, 128), BF16), ((tokens, tokens), BF16)],
        (masked, query_t),
        "order",
        far=(0, 1),
        far_out=(1, 2),
        us=2,
    )
    all_codes = exchange(chosen_codes)

    def prepare_body(inputs_ref, weight_ref, bias_ref, key_ref, order_ref, grad_ref, masked_ref, conv_ref,
                     value_ref, send_ref, top_ref, low_ref, cot_ref, band_ref, low_band_ref, back_ref,
                     pad_ref):
        values = (nt(inputs_ref[...], weight_ref[...]) + line(bias_ref)).astype(BF16)
        value_ref[...] = values
        same = one_zero(iota((local, local), 0) == iota((local, local), 1))
        send_ref[:codes_rows] = key_ref[...].astype(F32).astype(BF16)
        send_ref[codes_rows:] = nt(same, values).astype(BF16)
        order = order_ref[...]
        moved = nn(order, inputs_ref[...]).astype(BF16)
        top_ref[...] = moved[:chosen]
        low_ref[...] = moved[chosen:]
        pick = order_ref[:chosen]
        flags = jnp.broadcast_to(line(masked_ref).astype(F32), (8, tokens)).astype(BF16)
        valid = nt(pick, flags)[:, :1]
        parts = split3(grad_ref[...])
        cot_ref[...] = (nn(pick, parts[0]) + nn(pick, parts[1]) + nn(pick, parts[2])) * valid
        pad_ref[...] = jnp.zeros_like(pad_ref)
        pad_ref[:heads, :taps] = conv_ref[...]
        turn = one_zero(iota((128, 128), 0) + iota((128, 128), 1) == taps - 1)
        padded = pad_ref[...]
        parts = split3(padded)
        turned = nn(parts[0], turn) + nn(parts[1], turn) + nn(parts[2], turn)
        blank = jnp.zeros((8, window - 128), F32)
        for h in range(heads):
            for ahead, source in ((True, padded), (False, turned)):
                long = jnp.concatenate([source, blank], axis=1)
                spread = jnp.broadcast_to(long[h : h + 1], (tokens, window))
                band = pltpu.roll(spread, 0, 1, stride=1, stride_axis=0)
                for at, level in zip((0, window), split2(band)):
                    if ahead:
                        moved = nn(order, level).astype(BF16)
                        band_ref[h, :, at : at + window] = moved[:chosen]
                        low_band_ref[h, :, at : at + window] = moved[chosen:]
                    else:
                        back_ref[h, :, at : at + window] = level

    values, value_send, top_inputs, low_inputs, cot, bands, low_bands, back_bands = run(
        prepare_body,
        [((tokens, local), BF16), ((codes_rows + local, tokens), BF16), ((chosen, width), BF16),
         ((rest, width), BF16), ((chosen, width), F32), ((heads, chosen, 2 * window), BF16),
         ((heads, rest, 2 * window), BF16), ((heads, tokens, 2 * window), BF16)],
        (inputs, value_t, value_bias, key_t, order, out_grad, masked, conv_weight),
        "prepare",
        far=tuple(range(8)),
        far_out=(0, 2, 3, 4, 5, 6, 7),
        scratch=[pltpu.VMEM((8, 128), F32)],
        us=4,
    )
    all_keys = lax.all_gather(value_send, "seq", axis=0)

    def count_body(ids_ref, codes_ref, send_ref, value_ref, wide_ref, tall_ref, count_ref, out_ref, finish):
        me = ids_ref[0]
        keys = key_words(send_ref[:codes_rows], tall_ref[...])
        queries = query_words(codes_ref[...].reshape(total, 128), wide_ref[...])
        for h in range(heads):
            for r in range(0, total, tokens):
                for c in range(0, tokens, 128):
                    count_ref[h, r : r + tokens, c : c + 128] = matches(
                        queries[r : r + tokens], keys[:, c : c + 128], h
                    )
        finish(0)
        for h in range(heads):
            turned = send_ref[codes_rows + h * dim : codes_rows + (h + 1) * dim]
            read = nt(count_ref[h], turned).astype(BF16)
            for i in range(n):
                out_ref[i, :chosen, h * dim : (h + 1) * dim] = read[i * chosen : (i + 1) * chosen]
        for i in range(n):
            last, head_rows = value_ref[tokens - half :], value_ref[:half]
            rows = jnp.where(i == me + 1, last.astype(F32), head_rows.astype(F32))
            out_ref[i, chosen:] = rows.astype(BF16)

    counts, reads = run(
        count_body,
        [((heads, total, tokens), BF16), ((n, chosen + half, local), BF16)],
        (ids, all_codes, value_send, values, wide, tall),
        "count",
        far=(3, 4, 5),
        far_out=(0,),
        early=(0,),
        smem=1,
        us=5,
    )
    reads = exchange(reads)

    def unit_rows(value_sum):
        return lax.rsqrt(jnp.mean(value_sum * value_sum, -1, keepdims=True) + 1e-05)

    def context_body(ids_ref, reads_ref, value_ref, band_ref, context_ref, sum_ref, near_ref):
        me = ids_ref[0]
        total_read = reads_ref[0, :chosen].astype(F32)
        for i in range(1, n):
            total_read += reads_ref[i, :chosen].astype(F32)
        total_read = total_read * (1.0 / hashes)
        sum_ref[...] = total_read
        before = reads_ref[jnp.maximum(me - 1, 0), chosen:].astype(F32)
        after = reads_ref[jnp.minimum(me + 1, n - 1), chosen:].astype(F32)
        near_ref[:half] = jnp.where(me > 0, before, 0.0).astype(BF16)
        near_ref[half : half + tokens] = value_ref[...]
        near_ref[half + tokens : 2 * half + tokens] = jnp.where(me < n - 1, after, 0.0).astype(BF16)
        near_ref[2 * half + tokens :] = jnp.zeros((window - tokens - 2 * half, local), BF16)
        near = near_ref[...]
        twice = jnp.concatenate([near, near], axis=0)
        for h in range(heads):
            cols = slice(h * dim, (h + 1) * dim)
            mine = total_read[:, cols]
            conv = nn(band_ref[h], twice[:, cols])
            context_ref[:, cols] = (mine * unit_rows(mine) + conv).astype(BF16)

    context, value_sum, near = run(
        context_body,
        [((chosen, local), BF16), ((chosen, local), F32), ((window, local), BF16)],
        (ids, reads, values, bands),
        "context",
        far=(2, 3),
        far_out=(2,),
        smem=1,
        us=2,
    )
    contexts = [context] + others(context)

    def paired(terms):
        while len(terms) > 1:
            terms = [terms[i] + terms[i + 1] for i in range(0, len(terms), 2)]
        return terms[0]

    def joined(context_refs, out_refs):
        return paired([nn(a[...], b[...]) for a, b in zip(context_refs, out_refs)])

    def feed(low, up_ref, up_bias_ref, down_ref):
        pre = nn(low, up_ref[...]) + line(up_bias_ref)
        act = (pre * cdf_of(pre)).astype(BF16)
        return pre, nn(act, down_ref[...]).astype(BF16)

    def first_body(*refs, ready, finish):
        context_refs, out_refs, refs = refs[:tp], refs[tp : 2 * tp], refs[2 * tp :]
        (inputs_ref, bias_ref, gain_ref, shift_ref, up_ref, up_bias_ref, down_ref,
         part_ref, hidden_ref, first_ref, pre_ref) = refs
        hidden = joined(context_refs, out_refs)
        ready()
        hidden = inputs_ref[...].astype(F32) + hidden + line(bias_ref)
        hidden_ref[...] = hidden
        finish(1)
        unit, _ = norm_stats(hidden)
        first = unit * line(gain_ref) + line(shift_ref)
        first_ref[...] = first
        finish(2)
        pre, part = feed(first.astype(BF16), up_ref, up_bias_ref, down_ref)
        pre_ref[...] = pre
        part_ref[...] = part

    part, hidden, first, pre_act = run(
        first_body,
        [((chosen, width), BF16), ((chosen, width), F32), ((chosen, width), F32), ((chosen, units), F32)],
        (*contexts, *out_all, top_inputs, out_bias, first_gain, first_shift, up_weight, up_bias, down_weight),
        "first",
        far=tuple(range(tp, 2 * tp + 4)) + (2 * tp + 5,),
        far_out=(1, 2, 3),
        early=(1, 2),
        late=tuple(range(2 * tp, 2 * tp + 4)) + (2 * tp + 5,),
        us=3,
    )
    parts = [part] + others(part)

    def slope_body(pre_ref, slope_ref):
        slope_ref[...] = gelu_grad(pre_ref[...])

    (slope,) = run(slope_body, ((chosen, units), F32), (pre_act,), "slope", far=(0,), us=1.5)

    def back_norm(grad, unit, q, gain):
        scaled = grad * gain
        return q * (
            scaled
            - jnp.mean(scaled, -1, keepdims=True)
            - unit * jnp.mean(scaled * unit, -1, keepdims=True)
        )

    def put_sums(ref, sums):
        for i, vector in enumerate(sums):
            ref[i : i + 1] = vector

    def column_sum(array):
        return jnp.sum(array, 0, keepdims=True)

    def second_body(*refs, ready, finish):
        part_refs, refs = refs[:tp], refs[tp:]
        (first_ref, bias_ref, gain_ref, shift_ref, cot_ref, slope_ref, down_ref, up_ref,
         context_ref, output_ref, grad_ref, back_ref, sums_ref, keep_ref) = refs
        second = paired([r[...].astype(F32) for r in part_refs])
        ready()
        second = first_ref[...] + second + line(bias_ref)
        unit, q = norm_stats(second)
        output_ref[...] = (unit * line(gain_ref) + line(shift_ref)).astype(BF16)
        finish(0)
        grad = back_norm(cot_ref[...], unit, q, line(gain_ref))
        grad_ref[...] = grad
        low = grad.astype(BF16)
        grad_pre = (nt(low, down_ref[...]) * slope_ref[...]).astype(BF16)
        back_ref[...] = nt(grad_pre, up_ref[...]).astype(BF16)
        put_sums(sums_ref, [column_sum(cot_ref[...] * unit), column_sum(cot_ref[...]), column_sum(grad)])
        keep_ref[:, :width] = first_ref[...].astype(BF16)
        keep_ref[:, width : 2 * width] = low
        keep_ref[:, 2 * width :] = context_ref[...]

    out_chosen, grad_second, back, sums, keep = run(
        second_body,
        [((chosen, width), BF16), ((chosen, width), F32), ((chosen, width), BF16), ((8, width), F32),
         ((chosen, 2 * width + local), BF16)],
        (*parts, first, down_bias, second_gain, second_shift, cot, slope, down_weight, up_weight, context),
        "second",
        far=tuple(range(tp, tp + 5)),
        late=tuple(range(tp, tp + 5)),
        far_out=(0, 4),
        early=(0,),
        us=3,
    )
    backs = [back] + others(back)
    keeps = lax.all_gather(keep, "seq", axis=0)

    def hidden_body(ids_ref, *refs, ready):
        back_refs, refs = refs[:tp], refs[tp:]
        grad_ref, hidden_ref, gain_ref, sums_ref, read_ref, out_ref, send_ref, attn_ref, sum_ref = refs
        side = ids_ref[1] % 2
        grad = grad_ref[...] + paired([r[...].astype(F32) for r in back_refs])
        ready()
        unit, q = norm_stats(hidden_ref[...])
        grad_hidden = back_norm(grad, unit, q, line(gain_ref))
        out_ref[...] = grad_hidden
        attn_ref[...] = grad_hidden.astype(BF16)
        sum_ref[...] = jnp.zeros_like(sum_ref)
        sum_ref[:3] = sums_ref[:3]
        put_sums(sum_ref.at[3:6], [column_sum(grad * unit), column_sum(grad), column_sum(grad_hidden)])
        lanes = pl.ds(pl.multiple_of(side * part_width, part_width), part_width)
        mine, mine_sums = attn_ref[:, lanes], sum_ref[:, lanes].astype(BF16)
        read = read_ref[...].astype(BF16)
        for i in range(n):
            send_ref[i, :chosen] = mine
            send_ref[i, chosen : chosen + 16] = mine_sums
            send_ref[i, chosen + 16 :, :local] = read[: chosen // 2]
            send_ref[i, chosen + 16 :, local:] = read[chosen // 2 :]

    grad_hidden, attn_send = run(
        hidden_body,
        [((chosen, width), F32), ((n, chosen + 16 + chosen // 2, part_width), BF16)],
        (ids, *backs, grad_second, hidden, first_gain, sums, value_sum),
        "hidden",
        also=((all_keys, pltpu.HBM),),
        far=(tp + 2, tp + 3),
        late=(tp + 2, tp + 3),
        far_out=(0,),
        smem=1,
        scratch=[pltpu.VMEM((chosen, width), BF16), pltpu.VMEM((16, width), F32)],
        us=2,
    )
    attn_mine = exchange(attn_send)

    def rest_body(codes_ref, keys_ref, wide_ref, tall_ref, band_ref, near_ref, context_ref,
                  key_ref, turned_ref, word_ref, count_ref, ready):
        queries = query_words(codes_ref[...], wide_ref[...])
        ready()
        for i in range(n):
            key_ref[:, i * tokens : (i + 1) * tokens] = keys_ref[i, :codes_rows]
            turned_ref[:, i * tokens : (i + 1) * tokens] = keys_ref[i, codes_rows:]
        word_ref[...] = key_words(key_ref[...], tall_ref[...])
        near = near_ref[...]
        twice = jnp.concatenate([near, near], axis=0)
        for h in range(heads):
            @pl.loop(0, n * tokens // 256)
            def _(i):
                for c in range(2):
                    lanes = pl.ds(pl.multiple_of(i * 256 + c * 128, 128), 128)
                    count_ref[:, lanes] = matches(queries, word_ref[:, lanes], h)

            cols = slice(h * dim, (h + 1) * dim)
            mine = nt(count_ref[...], turned_ref[cols]) * (1.0 / hashes)
            conv = nn(band_ref[h], twice[:, cols])
            context_ref[:, cols] = (mine * unit_rows(mine) + conv).astype(BF16)

    (rest_context,) = run(
        rest_body,
        ((rest, local), BF16),
        (rest_codes, all_keys, wide, tall, low_bands, near),
        "rest_context",
        far=(0, 1, 2, 3, 4, 5),
        late=(1, 4, 5),
        scratch=[pltpu.VMEM((codes_rows, n * tokens), BF16), pltpu.VMEM((local, n * tokens), BF16),
                 pltpu.VMEM((32, n * tokens), I32), pltpu.VMEM((rest, n * tokens), BF16)],
        us=12,
    )
    rest_contexts = [rest_context] + others(rest_context)

    def values_body(ids_ref, mine_ref, other_ref, out_ref, count_ref, band_ref, codes_ref,
                    grad_ref, dense_ref, attn_ref, *refs, ready):
        vector_refs, (y_ref, read_ref, reads_ref, sums_ref) = refs[:6], refs[6:]
        me, side = ids_ref[0], ids_ref[1] % 2
        own = pl.ds(pl.multiple_of(side * part_width, part_width), part_width)
        far = pl.ds(pl.multiple_of((1 - side) * part_width, part_width), part_width)
        for ref, lanes in ((mine_ref, own), (other_ref, far)):
            for i in range(n):
                attn_ref[i * chosen : (i + 1) * chosen, lanes] = ref[i, :chosen]
            sum_all = ref[0, chosen : chosen + 16].astype(F32)
            for i in range(1, n):
                sum_all += ref[i, chosen : chosen + 16].astype(F32)
            sums_ref[:, lanes] = sum_all
        for i, ref in enumerate(vector_refs):
            ref[...] = sums_ref[i : i + 1].reshape(width)
        for i in range(n):
            for at in range(2):
                reads_ref[i * chosen + at * (chosen // 2) : i * chosen + (at + 1) * (chosen // 2)] = mine_ref[
                    i, chosen + 16 :, at * local : (at + 1) * local
                ]
        y = nt(attn_ref[...], out_ref[...]).astype(BF16)
        y_ref[...] = y
        ready()
        for h in range(heads):
            cols = slice(h * dim, (h + 1) * dim)
            read = reads_ref[:, cols].astype(F32)
            grad = y[:, cols].astype(F32)
            r = unit_rows(read)
            back = r * (grad - read * (r * r) * jnp.mean(grad * read, -1, keepdims=True))
            read_ref[:, cols] = (back * (1.0 / hashes)).astype(BF16)
        dense = jnp.zeros((window, local), F32)
        for step in (-1, 0, 1):
            source = jnp.clip(me + step, 0, n - 1)
            inside = jnp.logical_and(me + step >= 0, me + step < n)
            there = y_ref[pl.ds(pl.multiple_of(source * chosen, chosen), chosen)]
            spots = codes_ref[source][:, codes_rows : codes_rows + 1].astype(F32).astype(I32)
            spots = jnp.where(inside, spots + step * tokens + half, -1)
            place = one_zero(spots == iota((chosen, window), 1))
            dense += tn(place, there)
        dense_low = dense.astype(BF16)
        dense_ref[...] = dense_low
        twice = jnp.concatenate([dense_low, dense_low], axis=0)
        for h in range(heads):
            cols = slice(h * dim, (h + 1) * dim)
            grad = tn(count_ref[h], read_ref[:, cols]) + nn(band_ref[h], twice[:, cols])
            grad_ref[:, cols] = grad.astype(BF16)

    attn_other = swap(lax.optimization_barrier((attn_mine, rest_context))[0], 1)
    grad_values, dense, attn_all, *vectors = run(
        values_body,
        [((tokens, local), BF16), ((window, local), BF16), ((total, width), BF16)] + [((width,), F32)] * 6,
        (ids, attn_mine, attn_other, out_weight, counts, back_bands, all_codes),
        "values_back",
        far=(3, 4, 5, 6),
        late=(4, 5, 6),
        far_out=(2, 3, 4, 5, 6, 7, 8),
        smem=1,
        scratch=[pltpu.VMEM((total, local), BF16)] * 3 + [
                 pltpu.VMEM((16, width), F32)],
        us=6,
    )
    grads = [grad_values] + others(grad_values)

    share = local // n
    extra = 8

    def value_grad_body(inputs_ref, grad_ref, dense_ref, near_ref, send_ref, row_ref):
        grad = grad_ref[...]
        weight = tn(grad, inputs_ref[...]).astype(BF16)
        row_ref[...] = jnp.zeros_like(row_ref)
        row_ref[:1, :local] = column_sum(grad.astype(F32))
        turn = one_zero(iota((tokens, tokens), 0) + iota((tokens, tokens), 1) == tokens - 1)
        turned = nn(turn, dense_ref[half : half + tokens]).astype(BF16)
        for h in range(heads):
            cols = slice(h * dim, (h + 1) * dim)
            both = nt(turned[:, cols], near_ref[:, cols])
            aligned = pltpu.roll(both, window - tokens + 1, 1, stride=1, stride_axis=0)
            row_ref[1 + h : 2 + h, :128] = column_sum(aligned)[:, :128]
        for i in range(n):
            send_ref[i, :share] = weight[i * share : (i + 1) * share]
            send_ref[i, share:] = row_ref[...].astype(BF16)

    (value_part,) = run(
        value_grad_body,
        ((n, share + extra, width), BF16),
        (inputs, grad_values, dense, near),
        "value_grad",
        far=(0, 3),
        scratch=[pltpu.VMEM((extra, width), F32)],
        us=2.5,
    )
    value_part = exchange(value_part)

    def rest_first_body(*refs, ready):
        context_refs, out_refs, refs = refs[:tp], refs[tp : 2 * tp], refs[2 * tp :]
        (inputs_ref, bias_ref, gain_ref, shift_ref, up_ref, up_bias_ref, down_ref, part_ref, first_ref) = refs
        hidden = joined(context_refs, out_refs)
        ready()
        hidden = inputs_ref[...].astype(F32) + hidden + line(bias_ref)
        unit, _ = norm_stats(hidden)
        first = unit * line(gain_ref) + line(shift_ref)
        first_ref[...] = first
        part_ref[...] = feed(first.astype(BF16), up_ref, up_bias_ref, down_ref)[1]

    rest_part, rest_first = run(
        rest_first_body,
        [((rest, width), BF16), ((rest, width), F32)],
        (*rest_contexts, *out_all, low_inputs, out_bias, first_gain, first_shift, up_weight, up_bias,
         down_weight),
        "rest_first",
        far=tuple(range(tp, 2 * tp + 4)) + (2 * tp + 5,),
        late=tuple(range(2 * tp, 2 * tp + 4)) + (2 * tp + 5,),
        far_out=(1,),
        us=4,
    )
    rest_parts = [rest_part] + others(rest_part)

    def input_body(*refs):
        grad_refs, weight_refs, (order_ref, hidden_ref, out_ref) = (
            refs[:tp], refs[tp : 2 * tp], refs[2 * tp :])
        pick = order_ref[:chosen]
        parts = split3(hidden_ref[...])
        placed = tn(pick, parts[0]) + tn(pick, parts[1]) + tn(pick, parts[2])
        out_ref[...] = placed + joined(grad_refs, weight_refs)

    (input_grad,) = run(
        input_body,
        ((tokens, width), F32),
        (*grads, *value_all, order, grad_hidden),
        "input_grad",
        far=tuple(range(tp, 2 * tp + 2)),
        far_out=(0,),
        us=4,
    )

    def value_sum_body(part_ref, send_ref, bias_ref, taps_ref):
        whole = part_ref[0].astype(F32)
        for i in range(1, n):
            whole += part_ref[i].astype(F32)
        for i in range(n):
            send_ref[i] = whole[:share].astype(BF16)
        bias_ref[...] = whole[share : share + 1, :local].reshape(local)
        taps_ref[...] = whole[share + 1 : share + 1 + heads, :taps]

    value_send_back, grad_value_bias, grad_taps = run(
        value_sum_body,
        [((n, share, width), BF16), ((local,), F32), ((heads, taps), F32)],
        (value_part,),
        "value_sums",
        far_out=(1, 2),
        us=1.5,
    )
    value_grad = exchange(value_send_back).reshape(local, width).astype(F32).T

    def output_body(*refs):
        part_refs, refs = refs[:tp], refs[tp:]
        first_ref, bias_ref, gain_ref, shift_ref, chosen_ref, order_ref, out_ref, sorted_ref = refs
        second = first_ref[...] + paired([r[...].astype(F32) for r in part_refs]) + line(bias_ref)
        unit, _ = norm_stats(second)
        sorted_ref[:chosen] = chosen_ref[...]
        sorted_ref[chosen:] = (unit * line(gain_ref) + line(shift_ref)).astype(BF16)
        out_ref[...] = tn(order_ref[...], sorted_ref[...]).astype(BF16)

    (output,) = run(
        output_body,
        ((tokens, width), BF16),
        (*rest_parts, rest_first, down_bias, second_gain, second_shift, out_chosen, order),
        "output",
        far=tuple(range(tp, tp + 6)),
        far_out=(0,),
        scratch=[pltpu.VMEM((tokens, width), BF16)],
        us=3,
    )

    def weights_body(keep_ref, attn_ref, up_w_ref, up_bias_ref, down_w_ref,
                     up_ref, up_sum_ref, grad_ref, out_ref, act_ref, pre_ref, finish):
        up_sum = jnp.zeros((1, units), F32)
        for i in range(n):
            rows = slice(i * chosen, (i + 1) * chosen)
            pre = nn(keep_ref[i, :, :width], up_w_ref[...]) + line(up_bias_ref)
            cdf = cdf_of(pre)
            act_ref[rows] = (pre * cdf).astype(BF16)
            slope = cdf + pre * jnp.exp(-0.5 * pre * pre) * 0.3989422804014327
            grad_pre = (nt(keep_ref[i, :, width : 2 * width], down_w_ref[...]) * slope).astype(BF16)
            pre_ref[rows] = grad_pre
            up_sum += column_sum(grad_pre.astype(F32))
        up_sum_ref[...] = up_sum.reshape(units)
        up_ref[...] = tn(keep_ref[:, :, :width].reshape(total, width), pre_ref[...])
        finish(0)
        grad_ref[...] = tn(act_ref[...], keep_ref[:, :, width : 2 * width].reshape(total, width))
        finish(2)
        out_ref[...] = tn(keep_ref[:, :, 2 * width :].reshape(total, local), attn_ref[...])

    grad_up, up_sum, grad_down, grad_out = run(
        weights_body,
        [((width, units), F32), ((units,), F32), ((units, width), F32), ((local, width), F32)],
        (keeps, attn_all, up_weight, up_bias, down_weight),
        "weights",
        far=(0, 1, 3),
        far_out=(0, 1, 2, 3),
        early=(0, 2),
        scratch=[pltpu.VMEM((total, units), BF16)] * 2,
        us=9,
    )

    return (
        output,
        input_grad,
        value_grad,
        grad_value_bias,
        grad_out,
        vectors[5],
        vectors[3],
        vectors[4],
        grad_up,
        up_sum,
        grad_down,
        vectors[2],
        vectors[0],
        vectors[1],
        grad_taps,
    )


def solution(mesh):
    return jax.shard_map(
        per_device,
        mesh=mesh,
        in_specs=(
            P("seq", None),
            P(None, "tp"),
            P("tp"),
            P("tp", None),
            P(),
            P(),
            P(),
            P(None, "tp"),
            P("tp"),
            P("tp", None),
            P(),
            P(),
            P(),
            P("tp", None),
            P("seq", "tp", None),
            P("seq", "tp", None),
            P("seq"),
            P("seq", None),
        ),
        out_specs=(
            P("seq", None),
            P("seq", None),
            P(None, "tp"),
            P("tp"),
            P("tp", None),
            P(),
            P(),
            P(),
            P(None, "tp"),
            P("tp"),
            P("tp", None),
            P(),
            P(),
            P(),
            P("tp", None),
        ),
        check_vma=False,
    )
```

```python
from functools import partial

import jax
import jax.numpy as jnp
import numpy as np
from jax import lax
from jax.experimental import pallas as pl
from jax.experimental.pallas import tpu as pltpu
from jax.sharding import PartitionSpec as P

F32, BF16, I32 = jnp.float32, jnp.bfloat16, jnp.int32
MIB = 1 << 20
VMEM_MIB = 20


def dot(a, b, dims):
    return lax.dot_general(a, b, (dims, ((), ())), preferred_element_type=F32)


def nn(a, b):
    return dot(a, b, ((1,), (0,)))


def nt(a, b):
    return dot(a, b, ((1,), (1,)))


def tn(a, b):
    return dot(a, b, ((0,), (0,)))


def split2(x):
    high = x.astype(BF16)
    return high, (x - high.astype(F32)).astype(BF16)


def split3(x):
    high = x.astype(BF16)
    rest = x - high.astype(F32)
    middle = rest.astype(BF16)
    return high, middle, (rest - middle.astype(F32)).astype(BF16)


def iota(shape, dim):
    return lax.broadcasted_iota(I32, shape, dim)


def one_zero(condition):
    return jnp.where(condition, 1.0, 0.0).astype(BF16)


def call(body, outs, args, name, scratch=(), smem=0, far=(), far_out=(), late=(), early=(),
         after=(), us=1.0):
    shapes = [outs] if isinstance(outs, tuple) else outs
    count = len(args)
    arrays = [*args, *(jax.ShapeDtypeStruct(shape, dtype) for shape, dtype in shapes)]
    moved = [*far, *(count + i for i in far_out)]
    spaces = [
        pltpu.SMEM if i < smem else pltpu.HBM if i in moved else pltpu.VMEM for i in range(len(arrays))
    ]
    inner = [pltpu.VMEM(arrays[i].shape, arrays[i].dtype) for i in moved]
    extra = len(after)

    held = sum(
        int(np.prod(ref.shape)) * jnp.dtype(ref.dtype).itemsize for ref in (*inner, *scratch)
    )
    limit = max(VMEM_MIB * MIB, held + 12 * MIB)

    def kernel(*refs):
        refs = list(refs[:count] + refs[count + extra :])
        given, here, rest = refs[: len(arrays)], refs[len(arrays) :][: len(inner)], refs[len(arrays) + len(inner) :]
        copies = []
        for slot, i in enumerate(moved):
            pair = (refs[i], here[slot]) if i < count else (here[slot], refs[i])
            copies.append(pltpu.make_async_copy(*pair, rest[-1].at[slot]))
            given[i] = here[slot]
        for copy in copies[: len(far)]:
            copy.start()
        for i, copy in zip(far, copies):
            if i not in late:
                copy.wait()

        def ready():
            for i, copy in zip(far, copies):
                if i in late:
                    copy.wait()

        sends = dict(zip(far_out, copies[len(far) :]))

        def finish(i):
            sends[i].start()

        options = {"ready": ready} if late else {}
        if early:
            options["finish"] = finish
        body(*given, *(rest[:-1] if moved else rest), **options)
        for i in sends:
            if i not in early:
                finish(i)
        for copy in sends.values():
            copy.wait()

    placed = [
        a if i < smem else pltpu.with_memory_space_constraint(a, spaces[i]) for i, a in enumerate(args)
    ]
    return pl.pallas_call(
        kernel,
        out_shape=[spaces[i](arrays[i].shape, arrays[i].dtype) for i in range(count, len(arrays))],
        in_specs=[pl.BlockSpec(memory_space=space) for space in spaces[:count]]
        + [pl.BlockSpec(memory_space=space) for _, space in after],
        out_specs=[pl.BlockSpec(memory_space=space) for space in spaces[count:]],
        scratch_shapes=[*inner, *scratch, *([pltpu.SemaphoreType.DMA((len(inner),))] if moved else [])],
        compiler_params=pltpu.CompilerParams(vmem_limit_bytes=limit),
        cost_estimate=pl.CostEstimate(
            flops=int(us * 1.1e9), bytes_accessed=0, transcendentals=0
        ),
        name=name,
    )(*placed, *(pltpu.with_memory_space_constraint(*pair) for pair in after))


def line(ref):
    return ref[...].reshape(1, ref.shape[0])


def norm_stats(rows):
    centre = rows - jnp.mean(rows, -1, keepdims=True)
    spread = jnp.mean(centre * centre, -1, keepdims=True)
    q = lax.rsqrt(spread + 1e-05)
    return centre * q, q


def cdf_of(u):
    return 0.5 * (1.0 + lax.erf(u * 0.7071067811865476))


def gelu_grad(u):
    return cdf_of(u) + u * jnp.exp(-0.5 * u * u) * 0.3989422804014327


def plane_weights(heads, hashes):
    lanes = 128
    rows = heads * hashes
    wide = np.zeros((8 * lanes, 2 * lanes), np.float32)
    tall = np.zeros((64, 8 * rows), np.float32)
    for b in range(8):
        for h in range(heads):
            for m in range(hashes):
                half, power = divmod(m, 16)
                wide[b * lanes + h * hashes + m, half * lanes + h * 8 + b] = 2.0**power
                tall[half * 32 + h * 8 + b, b * rows + h * hashes + m] = 2.0**power
    return jnp.asarray(wide, BF16), jnp.asarray(tall, BF16)


def query_words(codes, wide):
    whole = codes.astype(F32).astype(I32)
    bits = jnp.concatenate(
        [((whole >> b) & 1).astype(F32).astype(BF16) for b in range(8)], axis=1
    )
    both = nn(bits, wide)
    return both[:, :128].astype(I32) | (both[:, 128:].astype(I32) << 16)


def key_words(codes, tall):
    whole = codes.astype(F32).astype(I32)
    bits = jnp.concatenate(
        [((whole >> b) & 1).astype(F32).astype(BF16) for b in range(8)], axis=0
    )
    both = nn(tall, bits)
    return both[:32].astype(I32) | (both[32:].astype(I32) << 16)


def matches(query_block, key_block, head):
    apart = None
    for b in range(8):
        word = head * 8 + b
        unlike = query_block[:, word : word + 1] ^ key_block[word : word + 1, :]
        apart = unlike if apart is None else apart | unlike
    return (32 - lax.population_count(apart)).astype(F32).astype(BF16)


def per_device(
    inputs,
    value_weight,
    value_bias,
    out_weight,
    out_bias,
    first_gain,
    first_shift,
    up_weight,
    up_bias,
    down_weight,
    down_bias,
    second_gain,
    second_shift,
    conv_weight,
    query_codes,
    key_codes,
    masked,
    out_grad,
):
    n = lax.axis_size("seq")
    tp = lax.axis_size("tp")
    tokens, width = inputs.shape
    heads, hashes = query_codes.shape[1], query_codes.shape[2]
    taps = conv_weight.shape[1]
    half = (taps - 1) // 2
    local = value_weight.shape[1]
    dim = local // heads
    units = up_weight.shape[1]
    chosen = tokens // 4
    rest = tokens - chosen
    piece = rest // tp
    part_rows = chosen // tp
    codes_rows = heads * hashes
    window = tokens + 128
    total = n * chosen
    ids = jnp.stack([lax.axis_index("seq"), lax.axis_index("tp")]).astype(I32)
    wide, tall = plane_weights(heads, hashes)

    previous = []

    def run(*args, also=(), **options):
        results = call(*args, after=(*previous, *also), **options)
        previous[:] = [(results[0], pltpu.HBM if 0 in options.get("far_out", ()) else pltpu.VMEM)]
        return results

    def swap(array, k):
        return lax.ppermute(array, "tp", [(i, i ^ k) for i in range(tp)])

    def others(array):
        return [swap(array, k) for k in range(1, tp)]

    def others_by_steps(array):
        far = swap(array, 2)
        return [swap(array, 1), far, swap(far, 1)]

    def exchange(array):
        return lax.all_to_all(array, "seq", 0, 0)

    query_t = jnp.transpose(query_codes, (1, 2, 0)).reshape(codes_rows, tokens)
    key_t = jnp.transpose(key_codes, (1, 2, 0)).reshape(codes_rows, tokens)
    value_t = value_weight.T
    out_all = [out_weight] + others_by_steps(out_weight)
    value_all = [value_t] + others_by_steps(value_t)

    def order_of(masked_ref):
        flags = jnp.broadcast_to(line(masked_ref).astype(F32), (8, tokens))
        upto = one_zero(iota((tokens, tokens), 0) <= iota((tokens, tokens), 1))
        count = nn(flags.astype(BF16), upto)
        spot = iota((8, tokens), 1).astype(F32)
        target = jnp.where(flags > 0, count - 1.0, count[:, tokens - 1 :] + spot - count)
        return one_zero(iota((tokens, tokens), 0) == target[:1].astype(I32))

    def placed_codes(query_ref):
        where = jnp.where(
            iota((128 - codes_rows, tokens), 0) == 0, iota((128 - codes_rows, tokens), 1), 0
        )
        return jnp.concatenate([query_ref[...], where], axis=0).astype(F32).astype(BF16)

    def order_body(masked_ref, query_ref, chosen_ref):
        top = nt(order_of(masked_ref)[:chosen], placed_codes(query_ref)).astype(BF16)
        for i in range(n):
            chosen_ref[i] = top

    (chosen_codes,) = run(
        order_body,
        ((n, chosen, 128), BF16),
        (masked, query_t),
        "order",
        far=(0, 1),
        us=2,
    )
    all_codes = exchange(chosen_codes)

    def prepare_body(inputs_ref, weight_ref, bias_ref, key_ref, query_ref, grad_ref, masked_ref, conv_ref,
                     value_ref, send_ref, top_ref, low_ref, cot_ref, band_ref, low_band_ref, back_ref,
                     codes_ref, order_ref, pad_ref):
        order_ref[...] = order_of(masked_ref)
        codes_ref[...] = nt(order_ref[chosen:], placed_codes(query_ref)).astype(BF16)
        values = (nt(inputs_ref[...], weight_ref[...]) + line(bias_ref)).astype(BF16)
        value_ref[...] = values
        same = one_zero(iota((local, local), 0) == iota((local, local), 1))
        send_ref[:codes_rows] = key_ref[...].astype(F32).astype(BF16)
        send_ref[codes_rows:] = nt(same, values).astype(BF16)
        order = order_ref[...]
        moved = nn(order, inputs_ref[...]).astype(BF16)
        top_ref[...] = moved[:chosen]
        low_ref[...] = moved[chosen:]
        pick = order_ref[:chosen]
        flags = jnp.broadcast_to(line(masked_ref).astype(F32), (8, tokens)).astype(BF16)
        valid = nt(pick, flags)[:, :1]
        parts = split3(grad_ref[...])
        cot_ref[...] = (nn(pick, parts[0]) + nn(pick, parts[1]) + nn(pick, parts[2])) * valid
        pad_ref[...] = jnp.zeros_like(pad_ref)
        pad_ref[:heads, :taps] = conv_ref[...]
        turn = one_zero(iota((128, 128), 0) + iota((128, 128), 1) == taps - 1)
        padded = pad_ref[...]
        parts = split3(padded)
        turned = nn(parts[0], turn) + nn(parts[1], turn) + nn(parts[2], turn)
        blank = jnp.zeros((8, window - 128), F32)
        for h in range(heads):
            for ahead, source in ((True, padded), (False, turned)):
                long = jnp.concatenate([source, blank], axis=1)
                spread = jnp.broadcast_to(long[h : h + 1], (tokens, window))
                band = pltpu.roll(spread, 0, 1, stride=1, stride_axis=0)
                for at, level in zip((0, window), split2(band)):
                    if ahead:
                        moved = nn(order, level).astype(BF16)
                        band_ref[h, :, at : at + window] = moved[:chosen]
                        low_band_ref[h, :, at : at + window] = moved[chosen:]
                    else:
                        back_ref[h, :, at : at + window] = level

    (values, value_send, top_inputs, low_inputs, cot, bands, low_bands, back_bands, rest_codes,
     order) = run(
        prepare_body,
        [((tokens, local), BF16), ((codes_rows + local, tokens), BF16), ((chosen, width), BF16),
         ((rest, width), BF16), ((chosen, width), F32), ((heads, chosen, 2 * window), BF16),
         ((heads, rest, 2 * window), BF16), ((heads, tokens, 2 * window), BF16), ((rest, 128), BF16),
         ((tokens, tokens), BF16)],
        (inputs, value_t, value_bias, key_t, query_t, out_grad, masked, conv_weight),
        "prepare",
        far=tuple(range(8)),
        far_out=(0, 2, 3, 4, 5, 6, 7, 8, 9),
        scratch=[pltpu.VMEM((8, 128), F32)],
        us=4,
    )
    all_keys = lax.all_gather(value_send, "seq", axis=0)

    def count_body(ids_ref, codes_ref, send_ref, value_ref, wide_ref, tall_ref, count_ref, out_ref, ready, finish):
        me = ids_ref[0]
        keys = key_words(send_ref[:codes_rows], tall_ref[...])
        queries = query_words(codes_ref[...].reshape(total, 128), wide_ref[...])
        for h in range(heads):
            for r in range(0, total, tokens):
                for c in range(0, tokens, 128):
                    count_ref[h, r : r + tokens, c : c + 128] = matches(
                        queries[r : r + tokens], keys[:, c : c + 128], h
                    )
        finish(0)
        for h in range(heads):
            turned = send_ref[codes_rows + h * dim : codes_rows + (h + 1) * dim]
            read = nt(count_ref[h], turned).astype(BF16)
            for i in range(n):
                out_ref[i, :chosen, h * dim : (h + 1) * dim] = read[i * chosen : (i + 1) * chosen]
        ready()
        for i in range(n):
            last, head_rows = value_ref[tokens - half :], value_ref[:half]
            rows = jnp.where(i == me + 1, last.astype(F32), head_rows.astype(F32))
            out_ref[i, chosen:] = rows.astype(BF16)

    counts, reads = run(
        count_body,
        [((heads, total, tokens), BF16), ((n, chosen + half, local), BF16)],
        (ids, all_codes, value_send, values, wide, tall),
        "count",
        far=(3,),
        late=(3,),
        far_out=(0,),
        early=(0,),
        smem=1,
        us=5,
    )
    reads = exchange(reads)

    def unit_rows(value_sum):
        return lax.rsqrt(jnp.mean(value_sum * value_sum, -1, keepdims=True) + 1e-05)

    def context_body(ids_ref, reads_ref, value_ref, band_ref, context_ref, sum_ref, near_ref, ready, finish):
        me = ids_ref[0]
        total_read = reads_ref[0, :chosen].astype(F32)
        for i in range(1, n):
            total_read += reads_ref[i, :chosen].astype(F32)
        total_read = total_read * (1.0 / hashes)
        sum_ref[...] = total_read
        before = reads_ref[jnp.maximum(me - 1, 0), chosen:].astype(F32)
        after = reads_ref[jnp.minimum(me + 1, n - 1), chosen:].astype(F32)
        near_ref[:half] = jnp.where(me > 0, before, 0.0).astype(BF16)
        ready()
        near_ref[half : half + tokens] = value_ref[...]
        near_ref[half + tokens : 2 * half + tokens] = jnp.where(me < n - 1, after, 0.0).astype(BF16)
        near_ref[2 * half + tokens :] = jnp.zeros((window - tokens - 2 * half, local), BF16)
        finish(2)
        near = near_ref[...]
        twice = jnp.concatenate([near, near], axis=0)
        for h in range(heads):
            cols = slice(h * dim, (h + 1) * dim)
            mine = total_read[:, cols]
            conv = nn(band_ref[h], twice[:, cols])
            context_ref[:, cols] = (mine * unit_rows(mine) + conv).astype(BF16)

    context, value_sum, near = run(
        context_body,
        [((chosen, local), BF16), ((chosen, local), F32), ((window, local), BF16)],
        (ids, reads, values, bands),
        "context",
        far=(2, 3),
        late=(2, 3),
        far_out=(2,),
        early=(2,),
        smem=1,
        us=2,
    )
    contexts = [context] + others(context)

    def paired(terms):
        while len(terms) > 1:
            terms = [terms[i] + terms[i + 1] for i in range(0, len(terms), 2)]
        return terms[0]

    def joined(context_refs, out_refs):
        return paired([nn(a[...], b[...]) for a, b in zip(context_refs, out_refs)])

    def feed(low, up_ref, up_bias_ref, down_ref):
        pre = nn(low, up_ref[...]) + line(up_bias_ref)
        act = (pre * cdf_of(pre)).astype(BF16)
        return pre, nn(act, down_ref[...]).astype(BF16)

    def first_body(*refs, ready, finish):
        context_refs, out_refs, refs = refs[:tp], refs[tp : 2 * tp], refs[2 * tp :]
        (inputs_ref, bias_ref, gain_ref, shift_ref, up_ref, up_bias_ref, down_ref,
         part_ref, hidden_ref, first_ref, pre_ref) = refs
        hidden = joined(context_refs, out_refs)
        ready()
        hidden = inputs_ref[...].astype(F32) + hidden + line(bias_ref)
        hidden_ref[...] = hidden
        finish(1)
        unit, _ = norm_stats(hidden)
        first = unit * line(gain_ref) + line(shift_ref)
        first_ref[...] = first
        finish(2)
        pre, part = feed(first.astype(BF16), up_ref, up_bias_ref, down_ref)
        pre_ref[...] = pre
        part_ref[...] = part

    part, hidden, first, pre_act = run(
        first_body,
        [((chosen, width), BF16), ((chosen, width), F32), ((chosen, width), F32), ((chosen, units), F32)],
        (*contexts, *out_all, top_inputs, out_bias, first_gain, first_shift, up_weight, up_bias, down_weight),
        "first",
        far=tuple(range(tp, 2 * tp + 4)) + (2 * tp + 5,),
        far_out=(1, 2, 3),
        early=(1, 2),
        late=tuple(range(2 * tp, 2 * tp + 4)) + (2 * tp + 5,),
        us=3,
    )
    parts = [part] + others(part)

    def slope_body(pre_ref, slope_ref):
        slope_ref[...] = gelu_grad(pre_ref[...])

    (slope,) = run(slope_body, ((chosen, units), F32), (pre_act,), "slope", far=(0,), us=1.5)

    def back_norm(grad, unit, q, gain):
        scaled = grad * gain
        return q * (
            scaled
            - jnp.mean(scaled, -1, keepdims=True)
            - unit * jnp.mean(scaled * unit, -1, keepdims=True)
        )

    def put_sums(ref, sums):
        for i, vector in enumerate(sums):
            ref[i : i + 1] = vector

    def column_sum(array):
        return jnp.sum(array, 0, keepdims=True)

    def second_body(ids_ref, *refs, ready, finish):
        part_refs, refs = refs[:tp], refs[tp:]
        (first_ref, bias_ref, gain_ref, shift_ref, cot_ref, slope_ref, down_ref, up_ref,
         context_ref, output_ref, grad_ref, back_ref, sums_ref, keep_ref, low_ref) = refs
        second = paired([r[...].astype(F32) for r in part_refs])
        ready()
        second = first_ref[...] + second + line(bias_ref)
        unit, q = norm_stats(second)
        output_ref[...] = (unit * line(gain_ref) + line(shift_ref)).astype(BF16)
        finish(0)
        grad = back_norm(cot_ref[...], unit, q, line(gain_ref))
        grad_ref[...] = grad
        low = grad.astype(BF16)
        grad_pre = (nt(low, down_ref[...]) * slope_ref[...]).astype(BF16)
        back_ref[...] = nt(grad_pre, up_ref[...]).astype(BF16)
        put_sums(sums_ref, [column_sum(cot_ref[...] * unit), column_sum(cot_ref[...]), column_sum(grad)])
        low_ref[:, :width] = first_ref[...].astype(BF16)
        low_ref[:, width:] = low
        keep_ref[:, : 2 * width] = low_ref[pl.ds(pl.multiple_of(ids_ref[1] % 2 * mid, mid), mid)]
        keep_ref[:, 2 * width : 2 * width + local] = context_ref[:mid]
        keep_ref[:, 2 * width + local : 2 * width + 2 * local] = context_ref[mid:]
        keep_ref[:, 2 * width + 2 * local :] = jnp.zeros((mid, kept - 2 * width - 2 * local), BF16)

    mid = chosen // 2
    kept = -(-2 * (width + local) // 1024) * 1024
    out_chosen, grad_second, back, sums, keep = run(
        second_body,
        [((chosen, width), BF16), ((chosen, width), F32), ((chosen, width), BF16), ((8, width), F32),
         ((mid, kept), BF16)],
        (ids, *parts, first, down_bias, second_gain, second_shift, cot, slope, down_weight, up_weight, context),
        "second",
        also=tuple((weight, pltpu.HBM) for weight in value_all[1:]),
        far=tuple(range(tp + 1, tp + 6)),
        late=tuple(range(tp + 1, tp + 6)),
        far_out=(0, 4),
        early=(0,),
        smem=1,
        scratch=[pltpu.VMEM((chosen, 2 * width), BF16)],
        us=3,
    )
    backs = [back] + others(back)
    keeps = lax.all_gather(keep, "seq", axis=0)

    def rest_counts(count_ref, queries, word_ref, head):
        @pl.loop(0, n * tokens // 256)
        def _(i):
            for c in range(2):
                lanes = pl.ds(pl.multiple_of(i * 256 + c * 128, 128), 128)
                count_ref[:, lanes] = matches(queries, word_ref[:, lanes], head)

    def rest_read(count_ref, keys_ref, head):
        start = codes_rows + head * dim
        turned = jnp.concatenate([keys_ref[i, start : start + dim] for i in range(n)], axis=1)
        return nt(count_ref[...], turned) * (1.0 / hashes)

    def rest_words_body(codes_ref, keys_ref, wide_ref, tall_ref, query_ref, word_ref, first_ref,
                        key_ref, count_ref, ready):
        queries = query_words(codes_ref[...], wide_ref[...])
        query_ref[...] = queries
        ready()
        for i in range(n):
            key_ref[:, i * tokens : (i + 1) * tokens] = keys_ref[i, :codes_rows]
        word_ref[...] = key_words(key_ref[...], tall_ref[...])
        rest_counts(count_ref, queries, word_ref, 0)
        first_ref[...] = rest_read(count_ref, keys_ref, 0)

    rest_queries, key_bits, rest_sum = run(
        rest_words_body,
        [((rest, 128), I32), ((32, n * tokens), I32), ((rest, dim), F32)],
        (rest_codes, all_keys, wide, tall),
        "rest_words",
        far=(0, 1, 2, 3),
        late=(1,),
        scratch=[pltpu.VMEM((codes_rows, n * tokens), BF16), pltpu.VMEM((rest, n * tokens), BF16)],
        us=5,
    )

    def hidden_body(ids_ref, *refs, ready, finish):
        back_refs, refs = refs[:tp], refs[tp:]
        grad_ref, hidden_ref, gain_ref, sums_ref, read_ref, weight_ref, out_ref, send_ref, share_ref, all_ref, attn_ref = refs
        grad = grad_ref[...] + paired([r[...].astype(F32) for r in back_refs])
        ready()
        unit, q = norm_stats(hidden_ref[...])
        grad_hidden = back_norm(grad, unit, q, line(gain_ref))
        out_ref[...] = grad_hidden
        finish(0)
        low = grad_hidden.astype(BF16)
        y = nt(low, weight_ref[...]).astype(BF16)
        for h in range(heads):
            cols = slice(h * dim, (h + 1) * dim)
            read, at = read_ref[:, cols], y[:, cols].astype(F32)
            r = unit_rows(read)
            back = r * (at - read * (r * r) * jnp.mean(at * read, -1, keepdims=True))
            send_ref[0, :, cols] = (back * (1.0 / hashes)).astype(BF16)
        send_ref[0, :, local:] = y
        for i in range(1, n):
            send_ref[i] = send_ref[0]
        attn_ref[...] = low
        share_ref[...] = attn_ref[pl.ds(pl.multiple_of(ids_ref[1] * part_rows, part_rows), part_rows)]
        all_ref[:3] = sums_ref[:3]
        put_sums(all_ref.at[3:6], [column_sum(grad * unit), column_sum(grad), column_sum(grad_hidden)])
        all_ref[6:] = jnp.zeros((2, width), F32)

    grad_hidden, read_send, share, sums = run(
        hidden_body,
        [((chosen, width), F32), ((n, chosen, 2 * local), BF16), ((part_rows, width), BF16), ((8, width), F32)],
        (ids, *backs, grad_second, hidden, first_gain, sums, value_sum, out_weight),
        "hidden",
        also=((all_keys, pltpu.HBM),),
        far=(tp + 2, tp + 3),
        late=(tp + 2, tp + 3),
        far_out=(0, 2, 3),
        early=(0,),
        smem=1,
        scratch=[pltpu.VMEM((chosen, width), BF16)],
        us=2,
    )
    read_all = exchange(read_send)

    def rest_body(query_ref, word_ref, first_ref, keys_ref, band_ref, near_ref, context_ref, count_ref, ready):
        queries = query_ref[...]
        for h in range(heads):
            if h:
                rest_counts(count_ref, queries, word_ref, h)
                if h == 1:
                    ready()
                    near = near_ref[...]
                    twice = jnp.concatenate([near, near], axis=0)
            cols = slice(h * dim, (h + 1) * dim)
            if h:
                mine = rest_read(count_ref, keys_ref, h)
                conv = nn(band_ref[h], twice[:, cols])
                context_ref[:, cols] = (mine * unit_rows(mine) + conv).astype(BF16)
        mine = first_ref[...]
        conv = nn(band_ref[0], twice[:, :dim])
        context_ref[:, :dim] = (mine * unit_rows(mine) + conv).astype(BF16)

    (rest_context,) = run(
        rest_body,
        ((rest, local), BF16),
        (rest_queries, key_bits, rest_sum, all_keys, low_bands, near),
        "rest_context",
        far=(3, 4, 5),
        late=(3, 4, 5),
        scratch=[pltpu.VMEM((rest, n * tokens), BF16)],
        us=6,
    )
    rest_contexts = [rest_context] + others(rest_context)

    def values_body(ids_ref, read_ref, count_ref, band_ref, codes_ref, grad_ref, dense_ref, ready):
        me = ids_ref[0]
        ready()
        dense = jnp.zeros((window, local), F32)
        for step in (-1, 0, 1):
            source = jnp.clip(me + step, 0, n - 1)
            inside = jnp.logical_and(me + step >= 0, me + step < n)
            there = read_ref[source][:, local:]
            spots = codes_ref[source][:, codes_rows : codes_rows + 1].astype(F32).astype(I32)
            spots = jnp.where(inside, spots + step * tokens + half, -1)
            place = one_zero(spots == iota((chosen, window), 1))
            dense += tn(place, there)
        dense_low = dense.astype(BF16)
        dense_ref[...] = dense_low
        twice = jnp.concatenate([dense_low, dense_low], axis=0)
        for h in range(heads):
            cols = slice(h * dim, (h + 1) * dim)
            read = read_ref[:, :, cols].reshape(total, dim)
            grad = tn(count_ref[h], read) + nn(band_ref[h], twice[:, cols])
            grad_ref[:, cols] = grad.astype(BF16)

    grad_values, dense = run(
        values_body,
        [((tokens, local), BF16), ((window, local), BF16)],
        (ids, read_all, counts, back_bands, all_codes),
        "values_back",
        smem=1,
        far=(2, 3, 4),
        late=(2, 3, 4),
        us=4,
    )
    grads = [grad_values] + others(grad_values)

    piece_rows = local // n
    extra = 8

    def value_grad_body(inputs_ref, grad_ref, dense_ref, near_ref, sums_ref, share_ref, send_ref, row_ref):
        grad = grad_ref[...]
        weight = tn(grad, inputs_ref[...]).astype(BF16)
        row_ref[...] = jnp.zeros_like(row_ref)
        row_ref[:1, :local] = column_sum(grad.astype(F32))
        row_ref[1:7] = sums_ref[:6]
        turn = one_zero(iota((tokens, tokens), 0) + iota((tokens, tokens), 1) == tokens - 1)
        turned = nn(turn, dense_ref[half : half + tokens]).astype(BF16)
        for h in range(heads):
            cols = slice(h * dim, (h + 1) * dim)
            both = nt(turned[:, cols], near_ref[:, cols])
            aligned = pltpu.roll(both, window - tokens + 1, 1, stride=1, stride_axis=0)
            row_ref[:1, 256 + 128 * h : 384 + 128 * h] = column_sum(aligned)[:, :128]
        for i in range(n):
            send_ref[i, :piece_rows] = weight[i * piece_rows : (i + 1) * piece_rows]
            send_ref[i, piece_rows : piece_rows + extra] = row_ref[...].astype(BF16)
            send_ref[i, piece_rows + extra :] = share_ref[...]

    (value_part,) = run(
        value_grad_body,
        ((n, piece_rows + extra + part_rows, width), BF16),
        (inputs, grad_values, dense, near, sums, share),
        "value_grad",
        also=tuple((array, pltpu.HBM) for array in rest_contexts[1:]),
        far=(0, 3, 4, 5),
        scratch=[pltpu.VMEM((extra, width), F32)],
        us=2.5,
    )
    value_part = exchange(value_part)

    def rest_first_body(*refs, ready):
        context_refs, out_refs, refs = refs[:tp], refs[tp : 2 * tp], refs[2 * tp :]
        (inputs_ref, bias_ref, gain_ref, shift_ref, up_ref, up_bias_ref, down_ref, part_ref, first_ref) = refs
        hidden = joined(context_refs, out_refs)
        ready()
        hidden = inputs_ref[...].astype(F32) + hidden + line(bias_ref)
        unit, _ = norm_stats(hidden)
        first = unit * line(gain_ref) + line(shift_ref)
        first_ref[...] = first
        part_ref[...] = feed(first.astype(BF16), up_ref, up_bias_ref, down_ref)[1]

    rest_part, rest_first = run(
        rest_first_body,
        [((rest, width), BF16), ((rest, width), F32)],
        (*rest_contexts, *out_all, low_inputs, out_bias, first_gain, first_shift, up_weight, up_bias,
         down_weight),
        "rest_first",
        far=tuple(range(2 * tp + 4)) + (2 * tp + 5,),
        late=tuple(range(2 * tp, 2 * tp + 4)) + (2 * tp + 5,),
        far_out=(1,),
        us=4,
    )
    rest_parts = [rest_part] + others(rest_part)
    keeps = [keeps, swap(lax.optimization_barrier((keeps, rest_part))[0], 1)]

    def input_body(*refs):
        grad_refs, weight_refs, (order_ref, hidden_ref, out_ref) = (
            refs[:tp], refs[tp : 2 * tp], refs[2 * tp :])
        pick = order_ref[:chosen]
        parts = split3(hidden_ref[...])
        placed = tn(pick, parts[0]) + tn(pick, parts[1]) + tn(pick, parts[2])
        out_ref[...] = placed + joined(grad_refs, weight_refs)

    (input_grad,) = run(
        input_body,
        ((tokens, width), F32),
        (*grads, *value_all, order, grad_hidden),
        "input_grad",
        far=tuple(range(2 * tp + 2)),
        far_out=(0,),
        us=0.05,
    )

    def value_sum_body(part_ref, send_ref, attn_ref, bias_ref, taps_ref, *vector_refs):
        rows = piece_rows + extra
        whole = part_ref[0, :rows].astype(F32)
        for i in range(1, n):
            whole += part_ref[i, :rows].astype(F32)
        for i in range(n):
            send_ref[i] = whole[:piece_rows].astype(BF16)
            attn_ref[i] = part_ref[i, rows:]
        bias_ref[...] = whole[piece_rows : piece_rows + 1, :local].reshape(local)
        for h in range(heads):
            taps_ref[h : h + 1] = whole[piece_rows : piece_rows + 1, 256 + 128 * h : 256 + 128 * h + taps]
        for i, ref in enumerate(vector_refs):
            ref[...] = whole[piece_rows + 1 + i : piece_rows + 2 + i].reshape(width)

    value_send_back, attn_share, grad_value_bias, grad_taps, *vectors = run(
        value_sum_body,
        [((n, piece_rows, width), BF16), ((n, part_rows, width), BF16), ((local,), F32), ((heads, taps), F32)]
        + [((width,), F32)] * 6,
        (value_part,),
        "value_sums",
        far_out=tuple(range(2, 10)),
        us=0.05,
    )
    attn_shares = [attn_share] + others(attn_share)
    value_back = exchange(value_send_back)

    def weights_body(keep_ref, far_ref, up_w_ref, up_bias_ref, down_w_ref,
                     up_ref, up_sum_ref, grad_ref, act_ref, pre_ref, raw_ref, back_ref, finish):
        sides = (keep_ref, far_ref)
        low = jnp.concatenate([ref[:, :, :width].reshape(total // 2, width) for ref in sides], axis=0)
        down = jnp.concatenate(
            [ref[:, :, width : 2 * width].reshape(total // 2, width) for ref in sides], axis=0
        )
        raw_ref[...] = nn(low, up_w_ref[...])
        back_ref[...] = nt(down, down_w_ref[...])
        up_sum = jnp.zeros((1, units), F32)
        for i in range(n):
            rows = slice(i * chosen, (i + 1) * chosen)
            pre = raw_ref[rows] + line(up_bias_ref)
            cdf = cdf_of(pre)
            act_ref[rows] = (pre * cdf).astype(BF16)
            slope = cdf + pre * jnp.exp(-0.5 * pre * pre) * 0.3989422804014327
            grad_pre = (back_ref[rows] * slope).astype(BF16)
            pre_ref[rows] = grad_pre
            up_sum += column_sum(grad_pre.astype(F32))
        up_sum_ref[...] = up_sum.reshape(units)
        up_ref[...] = tn(low, pre_ref[...])
        finish(0)
        grad_ref[...] = tn(act_ref[...], down)

    grad_up, up_sum, grad_down = run(
        weights_body,
        [((width, units), F32), ((units,), F32), ((units, width), F32)],
        (*keeps, up_weight, up_bias, down_weight),
        "weights",
        also=tuple((array, pltpu.VMEM) for array in rest_parts[1:]),
        far=(0, 1, 3),
        far_out=(0, 1, 2),
        early=(0,),
        scratch=[pltpu.VMEM((total, units), BF16)] * 2 + [pltpu.VMEM((total, units), F32)] * 2,
        us=3,
    )

    def last_body(ids_ref, *refs, ready, finish):
        part_refs, attn_refs, refs = refs[:tp], refs[tp : 2 * tp], refs[2 * tp :]
        (back_ref, first_ref, bias_ref, gain_ref, shift_ref, chosen_ref, order_ref, keep_ref,
         out_ref, grad_out_ref, grad_value_ref, sorted_ref, all_ref, context_ref) = refs
        for i in range(n):
            grad_value_ref[i * piece_rows : (i + 1) * piece_rows] = back_ref[i].astype(F32)
        finish(2)
        for k, ref in enumerate(attn_refs):
            for i in range(n):
                start = i * chosen + (ids_ref[1] ^ k) * part_rows
                all_ref[pl.ds(pl.multiple_of(start, part_rows), part_rows)] = ref[i]
        second = paired([r[...].astype(F32) for r in part_refs])
        ready()
        second = first_ref[...] + second + line(bias_ref)
        unit, _ = norm_stats(second)
        sorted_ref[:chosen] = chosen_ref[...]
        sorted_ref[chosen:] = (unit * line(gain_ref) + line(shift_ref)).astype(BF16)
        out_ref[...] = tn(order_ref[...], sorted_ref[...]).astype(BF16)
        finish(0)
        tops = keep_ref[:, :, 2 * width : 2 * width + local].reshape(total // 2, local)
        lows = keep_ref[:, :, 2 * width + local : 2 * width + 2 * local].reshape(total // 2, local)
        for i in range(n):
            context_ref[i * chosen : i * chosen + mid] = tops[i * mid : (i + 1) * mid]
            context_ref[i * chosen + mid : (i + 1) * chosen] = lows[i * mid : (i + 1) * mid]
        grad_out_ref[...] = tn(context_ref[...], all_ref[...])

    output, grad_out, grad_value = run(
        last_body,
        [((tokens, width), BF16), ((local, width), F32), ((local, width), F32)],
        (ids, *rest_parts, *attn_shares, value_back, rest_first, down_bias, second_gain, second_shift, out_chosen,
         order, keeps[0]),
        "last",
        smem=1,
        far=tuple(range(2 * tp + 2, 2 * tp + 9)),
        late=tuple(range(2 * tp + 2, 2 * tp + 9)),
        far_out=(0, 1, 2),
        early=(0, 2),
        scratch=[pltpu.VMEM((tokens, width), BF16), pltpu.VMEM((total, width), BF16),
                 pltpu.VMEM((total, local), BF16)],
        us=0.05,
    )
    return (
        output,
        input_grad,
        grad_value.T,
        grad_value_bias,
        grad_out,
        vectors[5],
        vectors[3],
        vectors[4],
        grad_up,
        up_sum,
        grad_down,
        vectors[2],
        vectors[0],
        vectors[1],
        grad_taps,
    )


def solution(mesh):
    return jax.shard_map(
        per_device,
        mesh=mesh,
        in_specs=(
            P("seq", None),
            P(None, "tp"),
            P("tp"),
            P("tp", None),
            P(),
            P(),
            P(),
            P(None, "tp"),
            P("tp"),
            P("tp", None),
            P(),
            P(),
            P(),
            P("tp", None),
            P("seq", "tp", None),
            P("seq", "tp", None),
            P("seq"),
            P("seq", None),
        ),
        out_specs=(
            P("seq", None),
            P("seq", None),
            P(None, "tp"),
            P("tp"),
            P("tp", None),
            P(),
            P(),
            P(),
            P(None, "tp"),
            P("tp"),
            P("tp", None),
            P(),
            P(),
            P(),
            P("tp", None),
        ),
        check_vma=False,
    )
```

```python
from functools import partial

import jax
import jax.numpy as jnp
import numpy as np
from jax import lax
from jax.experimental import pallas as pl
from jax.experimental.pallas import tpu as pltpu
from jax.sharding import PartitionSpec as P

F32, BF16, I32 = jnp.float32, jnp.bfloat16, jnp.int32
MIB = 1 << 20
VMEM_MIB = 20


def dot(a, b, dims):
    return lax.dot_general(a, b, (dims, ((), ())), preferred_element_type=F32)


def nn(a, b):
    return dot(a, b, ((1,), (0,)))


def nt(a, b):
    return dot(a, b, ((1,), (1,)))


def tn(a, b):
    return dot(a, b, ((0,), (0,)))


def split2(x):
    high = x.astype(BF16)
    return high, (x - high.astype(F32)).astype(BF16)


def split3(x):
    high = x.astype(BF16)
    rest = x - high.astype(F32)
    middle = rest.astype(BF16)
    return high, middle, (rest - middle.astype(F32)).astype(BF16)


def iota(shape, dim):
    return lax.broadcasted_iota(I32, shape, dim)


def one_zero(condition):
    return jnp.where(condition, 1.0, 0.0).astype(BF16)


def call(body, outs, args, name, scratch=(), smem=0, far=(), far_out=(), late=(), early=(),
         after=(), us=1.0):
    shapes = [outs] if isinstance(outs, tuple) else outs
    count = len(args)
    arrays = [*args, *(jax.ShapeDtypeStruct(shape, dtype) for shape, dtype in shapes)]
    moved = [*far, *(count + i for i in far_out)]
    spaces = [
        pltpu.SMEM if i < smem else pltpu.HBM if i in moved else pltpu.VMEM for i in range(len(arrays))
    ]
    inner = [pltpu.VMEM(arrays[i].shape, arrays[i].dtype) for i in moved]
    extra = len(after)

    held = sum(
        int(np.prod(ref.shape)) * jnp.dtype(ref.dtype).itemsize for ref in (*inner, *scratch)
    )
    limit = max(VMEM_MIB * MIB, held + 12 * MIB)

    def kernel(*refs):
        refs = list(refs[:count] + refs[count + extra :])
        given, here, rest = refs[: len(arrays)], refs[len(arrays) :][: len(inner)], refs[len(arrays) + len(inner) :]
        copies = []
        for slot, i in enumerate(moved):
            pair = (refs[i], here[slot]) if i < count else (here[slot], refs[i])
            copies.append(pltpu.make_async_copy(*pair, rest[-1].at[slot]))
            given[i] = here[slot]
        for copy in copies[: len(far)]:
            copy.start()
        for i, copy in zip(far, copies):
            if i not in late:
                copy.wait()

        def ready():
            for i, copy in zip(far, copies):
                if i in late:
                    copy.wait()

        sends = dict(zip(far_out, copies[len(far) :]))

        def finish(i):
            sends[i].start()

        options = {"ready": ready} if late else {}
        if early:
            options["finish"] = finish
        body(*given, *(rest[:-1] if moved else rest), **options)
        for i in sends:
            if i not in early:
                finish(i)
        for copy in sends.values():
            copy.wait()

    placed = [
        a if i < smem else pltpu.with_memory_space_constraint(a, spaces[i]) for i, a in enumerate(args)
    ]
    return pl.pallas_call(
        kernel,
        out_shape=[spaces[i](arrays[i].shape, arrays[i].dtype) for i in range(count, len(arrays))],
        in_specs=[pl.BlockSpec(memory_space=space) for space in spaces[:count]]
        + [pl.BlockSpec(memory_space=space) for _, space in after],
        out_specs=[pl.BlockSpec(memory_space=space) for space in spaces[count:]],
        scratch_shapes=[*inner, *scratch, *([pltpu.SemaphoreType.DMA((len(inner),))] if moved else [])],
        compiler_params=pltpu.CompilerParams(vmem_limit_bytes=limit),
        cost_estimate=pl.CostEstimate(
            flops=int(us * 1.1e9), bytes_accessed=0, transcendentals=0
        ),
        name=name,
    )(*placed, *(pltpu.with_memory_space_constraint(*pair) for pair in after))


def line(ref):
    return ref[...].reshape(1, ref.shape[0])


def norm_stats(rows):
    centre = rows - jnp.mean(rows, -1, keepdims=True)
    spread = jnp.mean(centre * centre, -1, keepdims=True)
    q = lax.rsqrt(spread + 1e-05)
    return centre * q, q


def cdf_of(u):
    return 0.5 * (1.0 + lax.erf(u * 0.7071067811865476))


def gelu_grad(u):
    return cdf_of(u) + u * jnp.exp(-0.5 * u * u) * 0.3989422804014327


def plane_weights(heads, hashes):
    lanes = 128
    rows = heads * hashes
    wide = np.zeros((8 * lanes, 2 * lanes), np.float32)
    tall = np.zeros((64, 8 * rows), np.float32)
    for b in range(8):
        for h in range(heads):
            for m in range(hashes):
                half, power = divmod(m, 16)
                wide[b * lanes + h * hashes + m, half * lanes + h * 8 + b] = 2.0**power
                tall[half * 32 + h * 8 + b, b * rows + h * hashes + m] = 2.0**power
    return jnp.asarray(wide, BF16), jnp.asarray(tall, BF16)


def query_words(codes, wide):
    whole = codes.astype(F32).astype(I32)
    bits = jnp.concatenate(
        [((whole >> b) & 1).astype(F32).astype(BF16) for b in range(8)], axis=1
    )
    both = nn(bits, wide)
    return both[:, :128].astype(I32) | (both[:, 128:].astype(I32) << 16)


def key_words(codes, tall):
    whole = codes.astype(F32).astype(I32)
    bits = jnp.concatenate(
        [((whole >> b) & 1).astype(F32).astype(BF16) for b in range(8)], axis=0
    )
    both = nn(tall, bits)
    return both[:32].astype(I32) | (both[32:].astype(I32) << 16)


def matches(query_block, key_block, head):
    apart = None
    for b in range(8):
        word = head * 8 + b
        unlike = query_block[:, word : word + 1] ^ key_block[word : word + 1, :]
        apart = unlike if apart is None else apart | unlike
    return (32 - lax.population_count(apart)).astype(F32).astype(BF16)


def per_device(
    inputs,
    value_weight,
    value_bias,
    out_weight,
    out_bias,
    first_gain,
    first_shift,
    up_weight,
    up_bias,
    down_weight,
    down_bias,
    second_gain,
    second_shift,
    conv_weight,
    query_codes,
    key_codes,
    masked,
    out_grad,
):
    n = lax.axis_size("seq")
    tp = lax.axis_size("tp")
    tokens, width = inputs.shape
    heads, hashes = query_codes.shape[1], query_codes.shape[2]
    taps = conv_weight.shape[1]
    half = (taps - 1) // 2
    local = value_weight.shape[1]
    dim = local // heads
    units = up_weight.shape[1]
    chosen = tokens // 4
    rest = tokens - chosen
    piece = rest // tp
    part_rows = chosen // tp
    codes_rows = heads * hashes
    window = tokens + 128
    total = n * chosen
    ids = jnp.stack([lax.axis_index("seq"), lax.axis_index("tp")]).astype(I32)
    wide, tall = plane_weights(heads, hashes)

    previous = []

    def run(*args, also=(), **options):
        results = call(*args, after=(*previous, *also), **options)
        previous[:] = [(results[0], pltpu.HBM if 0 in options.get("far_out", ()) else pltpu.VMEM)]
        return results

    def swap(array, k):
        return lax.ppermute(array, "tp", [(i, i ^ k) for i in range(tp)])

    def others(array):
        return [swap(array, k) for k in range(1, tp)]

    def others_by_steps(array):
        far = swap(array, 2)
        return [swap(array, 1), far, swap(far, 1)]

    def exchange(array):
        return lax.all_to_all(array, "seq", 0, 0)

    query_t = jnp.transpose(query_codes, (1, 2, 0)).reshape(codes_rows, tokens)
    key_t = jnp.transpose(key_codes, (1, 2, 0)).reshape(codes_rows, tokens)
    value_t = value_weight.T
    out_all = [out_weight] + others_by_steps(out_weight)
    value_all = [value_t] + others_by_steps(value_t)

    def order_of(masked_ref):
        flags = jnp.broadcast_to(line(masked_ref).astype(F32), (8, tokens))
        upto = one_zero(iota((tokens, tokens), 0) <= iota((tokens, tokens), 1))
        count = nn(flags.astype(BF16), upto)
        spot = iota((8, tokens), 1).astype(F32)
        target = jnp.where(flags > 0, count - 1.0, count[:, tokens - 1 :] + spot - count)
        return one_zero(iota((tokens, tokens), 0) == target[:1].astype(I32))

    def placed_codes(query_ref):
        where = jnp.where(
            iota((128 - codes_rows, tokens), 0) == 0, iota((128 - codes_rows, tokens), 1), 0
        )
        return jnp.concatenate([query_ref[...], where], axis=0).astype(F32).astype(BF16)

    def order_body(masked_ref, query_ref, chosen_ref):
        top = nt(order_of(masked_ref)[:chosen], placed_codes(query_ref)).astype(BF16)
        for i in range(n):
            chosen_ref[i] = top

    (chosen_codes,) = run(
        order_body,
        ((n, chosen, 128), BF16),
        (masked, query_t),
        "order",
        far=(0, 1),
        us=2,
    )
    all_codes = exchange(chosen_codes)

    def prepare_body(inputs_ref, weight_ref, bias_ref, key_ref, query_ref, grad_ref, masked_ref, conv_ref,
                     value_ref, send_ref, top_ref, low_ref, cot_ref, band_ref, low_band_ref, back_ref,
                     codes_ref, order_ref, pad_ref):
        order_ref[...] = order_of(masked_ref)
        codes_ref[...] = nt(order_ref[chosen:], placed_codes(query_ref)).astype(BF16)
        values = (nt(inputs_ref[...], weight_ref[...]) + line(bias_ref)).astype(BF16)
        value_ref[...] = values
        same = one_zero(iota((local, local), 0) == iota((local, local), 1))
        send_ref[:codes_rows] = key_ref[...].astype(F32).astype(BF16)
        send_ref[codes_rows:] = nt(same, values).astype(BF16)
        order = order_ref[...]
        moved = nn(order, inputs_ref[...]).astype(BF16)
        top_ref[...] = moved[:chosen]
        low_ref[...] = moved[chosen:]
        pick = order_ref[:chosen]
        flags = jnp.broadcast_to(line(masked_ref).astype(F32), (8, tokens)).astype(BF16)
        valid = nt(pick, flags)[:, :1]
        parts = split3(grad_ref[...])
        cot_ref[...] = (nn(pick, parts[0]) + nn(pick, parts[1]) + nn(pick, parts[2])) * valid
        pad_ref[...] = jnp.zeros_like(pad_ref)
        pad_ref[:heads, :taps] = conv_ref[...]
        turn = one_zero(iota((128, 128), 0) + iota((128, 128), 1) == taps - 1)
        padded = pad_ref[...]
        parts = split3(padded)
        turned = nn(parts[0], turn) + nn(parts[1], turn) + nn(parts[2], turn)
        blank = jnp.zeros((8, window - 128), F32)
        for h in range(heads):
            for ahead, source in ((True, padded), (False, turned)):
                long = jnp.concatenate([source, blank], axis=1)
                spread = jnp.broadcast_to(long[h : h + 1], (tokens, window))
                band = pltpu.roll(spread, 0, 1, stride=1, stride_axis=0)
                for at, level in zip((0, window), split2(band)):
                    if ahead:
                        moved = nn(order, level).astype(BF16)
                        band_ref[h, :, at : at + window] = moved[:chosen]
                        low_band_ref[h, :, at : at + window] = moved[chosen:]
                    else:
                        back_ref[h, :, at : at + window] = level

    (values, value_send, top_inputs, low_inputs, cot, bands, low_bands, back_bands, rest_codes,
     order) = run(
        prepare_body,
        [((tokens, local), BF16), ((codes_rows + local, tokens), BF16), ((chosen, width), BF16),
         ((rest, width), BF16), ((chosen, width), F32), ((heads, chosen, 2 * window), BF16),
         ((heads, rest, 2 * window), BF16), ((heads, tokens, 2 * window), BF16), ((rest, 128), BF16),
         ((tokens, tokens), BF16)],
        (inputs, value_t, value_bias, key_t, query_t, out_grad, masked, conv_weight),
        "prepare",
        far=tuple(range(8)),
        far_out=(0, 2, 3, 4, 5, 6, 7, 8, 9),
        scratch=[pltpu.VMEM((8, 128), F32)],
        us=4,
    )
    all_keys = lax.all_gather(value_send, "seq", axis=0)

    def count_body(ids_ref, codes_ref, send_ref, value_ref, wide_ref, tall_ref, count_ref, out_ref, ready, finish):
        me = ids_ref[0]
        keys = key_words(send_ref[:codes_rows], tall_ref[...])
        queries = query_words(codes_ref[...].reshape(total, 128), wide_ref[...])
        for h in range(heads):
            for r in range(0, total, tokens):
                for c in range(0, tokens, 128):
                    count_ref[h, r : r + tokens, c : c + 128] = matches(
                        queries[r : r + tokens], keys[:, c : c + 128], h
                    )
        finish(0)
        for h in range(heads):
            turned = send_ref[codes_rows + h * dim : codes_rows + (h + 1) * dim]
            read = nt(count_ref[h], turned).astype(BF16)
            for i in range(n):
                out_ref[i, :chosen, h * dim : (h + 1) * dim] = read[i * chosen : (i + 1) * chosen]
        ready()
        for i in range(n):
            last, head_rows = value_ref[tokens - half :], value_ref[:half]
            rows = jnp.where(i == me + 1, last.astype(F32), head_rows.astype(F32))
            out_ref[i, chosen:] = rows.astype(BF16)

    counts, reads = run(
        count_body,
        [((heads, total, tokens), BF16), ((n, chosen + half, local), BF16)],
        (ids, all_codes, value_send, values, wide, tall),
        "count",
        far=(3,),
        late=(3,),
        far_out=(0,),
        early=(0,),
        smem=1,
        us=5,
    )
    reads = exchange(reads)

    def unit_rows(value_sum):
        return lax.rsqrt(jnp.mean(value_sum * value_sum, -1, keepdims=True) + 1e-05)

    def context_body(ids_ref, reads_ref, value_ref, band_ref, context_ref, sum_ref, near_ref, ready, finish):
        me = ids_ref[0]
        total_read = reads_ref[0, :chosen].astype(F32)
        for i in range(1, n):
            total_read += reads_ref[i, :chosen].astype(F32)
        total_read = total_read * (1.0 / hashes)
        sum_ref[...] = total_read
        before = reads_ref[jnp.maximum(me - 1, 0), chosen:].astype(F32)
        after = reads_ref[jnp.minimum(me + 1, n - 1), chosen:].astype(F32)
        near_ref[:half] = jnp.where(me > 0, before, 0.0).astype(BF16)
        ready()
        near_ref[half : half + tokens] = value_ref[...]
        near_ref[half + tokens : 2 * half + tokens] = jnp.where(me < n - 1, after, 0.0).astype(BF16)
        near_ref[2 * half + tokens :] = jnp.zeros((window - tokens - 2 * half, local), BF16)
        finish(2)
        near = near_ref[...]
        twice = jnp.concatenate([near, near], axis=0)
        for h in range(heads):
            cols = slice(h * dim, (h + 1) * dim)
            mine = total_read[:, cols]
            conv = nn(band_ref[h], twice[:, cols])
            context_ref[:, cols] = (mine * unit_rows(mine) + conv).astype(BF16)

    context, value_sum, near = run(
        context_body,
        [((chosen, local), BF16), ((chosen, local), F32), ((window, local), BF16)],
        (ids, reads, values, bands),
        "context",
        far=(2, 3),
        late=(2, 3),
        far_out=(2,),
        early=(2,),
        smem=1,
        us=2,
    )
    contexts = [context] + others(context)

    def paired(terms):
        while len(terms) > 1:
            terms = [terms[i] + terms[i + 1] for i in range(0, len(terms), 2)]
        return terms[0]

    def joined(context_refs, out_refs):
        return paired([nn(a[...], b[...]) for a, b in zip(context_refs, out_refs)])

    def feed(low, up_ref, up_bias_ref, down_ref):
        pre = nn(low, up_ref[...]) + line(up_bias_ref)
        act = (pre * cdf_of(pre)).astype(BF16)
        return pre, nn(act, down_ref[...]).astype(BF16)

    def first_body(*refs, ready, finish):
        context_refs, out_refs, refs = refs[:tp], refs[tp : 2 * tp], refs[2 * tp :]
        (inputs_ref, bias_ref, gain_ref, shift_ref, up_ref, up_bias_ref, down_ref,
         part_ref, hidden_ref, first_ref, pre_ref) = refs
        hidden = joined(context_refs, out_refs)
        ready()
        hidden = inputs_ref[...].astype(F32) + hidden + line(bias_ref)
        hidden_ref[...] = hidden
        finish(1)
        unit, _ = norm_stats(hidden)
        first = unit * line(gain_ref) + line(shift_ref)
        first_ref[...] = first
        finish(2)
        pre, part = feed(first.astype(BF16), up_ref, up_bias_ref, down_ref)
        pre_ref[...] = pre
        part_ref[...] = part

    part, hidden, first, pre_act = run(
        first_body,
        [((chosen, width), BF16), ((chosen, width), F32), ((chosen, width), F32), ((chosen, units), F32)],
        (*contexts, *out_all, top_inputs, out_bias, first_gain, first_shift, up_weight, up_bias, down_weight),
        "first",
        far=tuple(range(tp, 2 * tp + 4)) + (2 * tp + 5,),
        far_out=(1, 2, 3),
        early=(1, 2),
        late=tuple(range(2 * tp, 2 * tp + 4)) + (2 * tp + 5,),
        us=3,
    )
    parts = [part] + others(part)

    def slope_body(pre_ref, slope_ref):
        slope_ref[...] = gelu_grad(pre_ref[...])

    (slope,) = run(slope_body, ((chosen, units), F32), (pre_act,), "slope", far=(0,), us=1.5)

    def back_norm(grad, unit, q, gain):
        scaled = grad * gain
        return q * (
            scaled
            - jnp.mean(scaled, -1, keepdims=True)
            - unit * jnp.mean(scaled * unit, -1, keepdims=True)
        )

    def put_sums(ref, sums):
        for i, vector in enumerate(sums):
            ref[i : i + 1] = vector

    def column_sum(array):
        return jnp.sum(array, 0, keepdims=True)

    def second_body(ids_ref, *refs, ready, finish):
        part_refs, refs = refs[:tp], refs[tp:]
        (first_ref, bias_ref, gain_ref, shift_ref, cot_ref, slope_ref, down_ref, up_ref,
         context_ref, output_ref, grad_ref, back_ref, sums_ref, keep_ref, low_ref) = refs
        second = paired([r[...].astype(F32) for r in part_refs])
        ready()
        second = first_ref[...] + second + line(bias_ref)
        unit, q = norm_stats(second)
        output_ref[...] = (unit * line(gain_ref) + line(shift_ref)).astype(BF16)
        finish(0)
        grad = back_norm(cot_ref[...], unit, q, line(gain_ref))
        grad_ref[...] = grad
        low = grad.astype(BF16)
        grad_pre = (nt(low, down_ref[...]) * slope_ref[...]).astype(BF16)
        back_ref[...] = nt(grad_pre, up_ref[...]).astype(BF16)
        put_sums(sums_ref, [column_sum(cot_ref[...] * unit), column_sum(cot_ref[...]), column_sum(grad)])
        low_ref[:, :width] = first_ref[...].astype(BF16)
        low_ref[:, width:] = low
        keep_ref[:, : 2 * width] = low_ref[pl.ds(pl.multiple_of(ids_ref[1] % 2 * mid, mid), mid)]
        keep_ref[:, 2 * width : 2 * width + local] = context_ref[:mid]
        keep_ref[:, 2 * width + local : 2 * width + 2 * local] = context_ref[mid:]
        keep_ref[:, 2 * width + 2 * local :] = jnp.zeros((mid, kept - 2 * width - 2 * local), BF16)

    mid = chosen // 2
    kept = -(-2 * (width + local) // 1024) * 1024
    out_chosen, grad_second, back, sums, keep = run(
        second_body,
        [((chosen, width), BF16), ((chosen, width), F32), ((chosen, width), BF16), ((8, width), F32),
         ((mid, kept), BF16)],
        (ids, *parts, first, down_bias, second_gain, second_shift, cot, slope, down_weight, up_weight, context),
        "second",
        also=tuple((weight, pltpu.HBM) for weight in value_all[1:]),
        far=tuple(range(tp + 1, tp + 6)),
        late=tuple(range(tp + 1, tp + 6)),
        far_out=(0, 4),
        early=(0,),
        smem=1,
        scratch=[pltpu.VMEM((chosen, 2 * width), BF16)],
        us=3,
    )
    backs = [back] + others(back)
    keeps = lax.all_gather(keep, "seq", axis=0)

    def rest_counts(count_ref, queries, word_ref, head):
        @pl.loop(0, n * tokens // 256)
        def _(i):
            for c in range(2):
                lanes = pl.ds(pl.multiple_of(i * 256 + c * 128, 128), 128)
                count_ref[:, lanes] = matches(queries, word_ref[:, lanes], head)

    def rest_read(count_ref, keys_ref, head):
        start = codes_rows + head * dim
        turned = jnp.concatenate([keys_ref[i, start : start + dim] for i in range(n)], axis=1)
        return nt(count_ref[...], turned) * (1.0 / hashes)

    def rest_words_body(codes_ref, keys_ref, wide_ref, tall_ref, query_ref, word_ref, first_ref,
                        key_ref, count_ref, ready):
        queries = query_words(codes_ref[...], wide_ref[...])
        query_ref[...] = queries
        ready()
        for i in range(n):
            key_ref[:, i * tokens : (i + 1) * tokens] = keys_ref[i, :codes_rows]
        word_ref[...] = key_words(key_ref[...], tall_ref[...])
        rest_counts(count_ref, queries, word_ref, 0)
        first_ref[...] = rest_read(count_ref, keys_ref, 0)

    rest_queries, key_bits, rest_sum = run(
        rest_words_body,
        [((rest, 128), I32), ((32, n * tokens), I32), ((rest, dim), F32)],
        (rest_codes, all_keys, wide, tall),
        "rest_words",
        far=(0, 1, 2, 3),
        late=(1,),
        scratch=[pltpu.VMEM((codes_rows, n * tokens), BF16), pltpu.VMEM((rest, n * tokens), BF16)],
        us=5,
    )

    def hidden_body(ids_ref, *refs, ready, finish):
        back_refs, refs = refs[:tp], refs[tp:]
        grad_ref, hidden_ref, gain_ref, sums_ref, read_ref, weight_ref, out_ref, send_ref, share_ref, all_ref, attn_ref = refs
        grad = grad_ref[...] + paired([r[...].astype(F32) for r in back_refs])
        ready()
        unit, q = norm_stats(hidden_ref[...])
        grad_hidden = back_norm(grad, unit, q, line(gain_ref))
        out_ref[...] = grad_hidden
        finish(0)
        low = grad_hidden.astype(BF16)
        y = nt(low, weight_ref[...]).astype(BF16)
        for h in range(heads):
            cols = slice(h * dim, (h + 1) * dim)
            read, at = read_ref[:, cols], y[:, cols].astype(F32)
            r = unit_rows(read)
            back = r * (at - read * (r * r) * jnp.mean(at * read, -1, keepdims=True))
            send_ref[0, :, cols] = (back * (1.0 / hashes)).astype(BF16)
        send_ref[0, :, local:] = y
        for i in range(1, n):
            send_ref[i] = send_ref[0]
        attn_ref[...] = low
        share_ref[...] = attn_ref[pl.ds(pl.multiple_of(ids_ref[1] * part_rows, part_rows), part_rows)]
        all_ref[:3] = sums_ref[:3]
        put_sums(all_ref.at[3:6], [column_sum(grad * unit), column_sum(grad), column_sum(grad_hidden)])
        all_ref[6:] = jnp.zeros((2, width), F32)

    grad_hidden, read_send, share, sums = run(
        hidden_body,
        [((chosen, width), F32), ((n, chosen, 2 * local), BF16), ((part_rows, width), BF16), ((8, width), F32)],
        (ids, *backs, grad_second, hidden, first_gain, sums, value_sum, out_weight),
        "hidden",
        also=((all_keys, pltpu.HBM),),
        far=(tp + 2, tp + 3),
        late=(tp + 2, tp + 3),
        far_out=(0, 2, 3),
        early=(0,),
        smem=1,
        scratch=[pltpu.VMEM((chosen, width), BF16)],
        us=2,
    )
    read_all = exchange(read_send)

    def rest_body(query_ref, word_ref, first_ref, keys_ref, band_ref, near_ref, context_ref, count_ref, ready):
        queries = query_ref[...]
        for h in range(heads):
            if h:
                rest_counts(count_ref, queries, word_ref, h)
                if h == 1:
                    ready()
                    near = near_ref[...]
                    twice = jnp.concatenate([near, near], axis=0)
            cols = slice(h * dim, (h + 1) * dim)
            if h:
                mine = rest_read(count_ref, keys_ref, h)
                conv = nn(band_ref[h], twice[:, cols])
                context_ref[:, cols] = (mine * unit_rows(mine) + conv).astype(BF16)
        mine = first_ref[...]
        conv = nn(band_ref[0], twice[:, :dim])
        context_ref[:, :dim] = (mine * unit_rows(mine) + conv).astype(BF16)

    (rest_context,) = run(
        rest_body,
        ((rest, local), BF16),
        (rest_queries, key_bits, rest_sum, all_keys, low_bands, near),
        "rest_context",
        far=(3, 4, 5),
        late=(3, 4, 5),
        scratch=[pltpu.VMEM((rest, n * tokens), BF16)],
        us=6,
    )
    rest_contexts = [rest_context] + others(rest_context)

    def values_body(ids_ref, read_ref, count_ref, band_ref, codes_ref, grad_ref, dense_ref, ready):
        me = ids_ref[0]
        ready()
        dense = jnp.zeros((window, local), F32)
        for step in (-1, 0, 1):
            source = jnp.clip(me + step, 0, n - 1)
            inside = jnp.logical_and(me + step >= 0, me + step < n)
            there = read_ref[source][:, local:]
            spots = codes_ref[source][:, codes_rows : codes_rows + 1].astype(F32).astype(I32)
            spots = jnp.where(inside, spots + step * tokens + half, -1)
            place = one_zero(spots == iota((chosen, window), 1))
            dense += tn(place, there)
        dense_low = dense.astype(BF16)
        dense_ref[...] = dense_low
        twice = jnp.concatenate([dense_low, dense_low], axis=0)
        for h in range(heads):
            cols = slice(h * dim, (h + 1) * dim)
            read = read_ref[:, :, cols].reshape(total, dim)
            grad = tn(count_ref[h], read) + nn(band_ref[h], twice[:, cols])
            grad_ref[:, cols] = grad.astype(BF16)

    grad_values, dense = run(
        values_body,
        [((tokens, local), BF16), ((window, local), BF16)],
        (ids, read_all, counts, back_bands, all_codes),
        "values_back",
        smem=1,
        far=(2, 3, 4),
        late=(2, 3, 4),
        us=4,
    )
    grads = [grad_values] + others(grad_values)

    piece_rows = local // n
    extra = 8

    def value_grad_body(inputs_ref, grad_ref, dense_ref, near_ref, sums_ref, share_ref, send_ref, row_ref):
        grad = grad_ref[...]
        weight = tn(grad, inputs_ref[...]).astype(BF16)
        row_ref[...] = jnp.zeros_like(row_ref)
        row_ref[:1, :local] = column_sum(grad.astype(F32))
        row_ref[1:7] = sums_ref[:6]
        turn = one_zero(iota((tokens, tokens), 0) + iota((tokens, tokens), 1) == tokens - 1)
        turned = nn(turn, dense_ref[half : half + tokens]).astype(BF16)
        for h in range(heads):
            cols = slice(h * dim, (h + 1) * dim)
            both = nt(turned[:, cols], near_ref[:, cols])
            aligned = pltpu.roll(both, window - tokens + 1, 1, stride=1, stride_axis=0)
            row_ref[:1, 256 + 128 * h : 384 + 128 * h] = column_sum(aligned)[:, :128]
        for i in range(n):
            send_ref[i, :piece_rows] = weight[i * piece_rows : (i + 1) * piece_rows]
            send_ref[i, piece_rows : piece_rows + extra] = row_ref[...].astype(BF16)
            send_ref[i, piece_rows + extra :] = share_ref[...]

    (value_part,) = run(
        value_grad_body,
        ((n, piece_rows + extra + part_rows, width), BF16),
        (inputs, grad_values, dense, near, sums, share),
        "value_grad",
        also=tuple((array, pltpu.HBM) for array in rest_contexts[1:]),
        far=(0, 3, 4, 5),
        scratch=[pltpu.VMEM((extra, width), F32)],
        us=2.5,
    )
    value_part = exchange(value_part)

    def rest_first_body(*refs, ready):
        context_refs, out_refs, refs = refs[:tp], refs[tp : 2 * tp], refs[2 * tp :]
        (inputs_ref, bias_ref, gain_ref, shift_ref, up_ref, up_bias_ref, down_ref, part_ref, first_ref) = refs
        hidden = joined(context_refs, out_refs)
        ready()
        hidden = inputs_ref[...].astype(F32) + hidden + line(bias_ref)
        unit, _ = norm_stats(hidden)
        first = unit * line(gain_ref) + line(shift_ref)
        first_ref[...] = first
        part_ref[...] = feed(first.astype(BF16), up_ref, up_bias_ref, down_ref)[1]

    rest_part, rest_first = run(
        rest_first_body,
        [((rest, width), BF16), ((rest, width), F32)],
        (*rest_contexts, *out_all, low_inputs, out_bias, first_gain, first_shift, up_weight, up_bias,
         down_weight),
        "rest_first",
        also=tuple((array, pltpu.HBM) for array in grads[1:]),
        far=tuple(range(2 * tp + 7)),
        late=tuple(range(2 * tp, 2 * tp + 7)),
        far_out=(1,),
        us=4,
    )
    rest_parts = [rest_part] + others(rest_part)
    keeps = [keeps, swap(lax.optimization_barrier((keeps, rest_part))[0], 1)]

    def input_body(*refs):
        grad_refs, weight_refs, (order_ref, hidden_ref, out_ref) = (
            refs[:tp], refs[tp : 2 * tp], refs[2 * tp :])
        pick = order_ref[:chosen]
        parts = split3(hidden_ref[...])
        placed = tn(pick, parts[0]) + tn(pick, parts[1]) + tn(pick, parts[2])
        out_ref[...] = placed + joined(grad_refs, weight_refs)

    (input_grad,) = run(
        input_body,
        ((tokens, width), F32),
        (*grads, *value_all, order, grad_hidden),
        "input_grad",
        far=tuple(range(2 * tp + 2)),
        far_out=(0,),
        us=0.05,
    )

    def value_sum_body(part_ref, send_ref, attn_ref, bias_ref, taps_ref, *vector_refs):
        rows = piece_rows + extra
        whole = part_ref[0, :rows].astype(F32)
        for i in range(1, n):
            whole += part_ref[i, :rows].astype(F32)
        for i in range(n):
            send_ref[i] = whole[:piece_rows].astype(BF16)
            attn_ref[i] = part_ref[i, rows:]
        bias_ref[...] = whole[piece_rows : piece_rows + 1, :local].reshape(local)
        for h in range(heads):
            taps_ref[h : h + 1] = whole[piece_rows : piece_rows + 1, 256 + 128 * h : 256 + 128 * h + taps]
        for i, ref in enumerate(vector_refs):
            ref[...] = whole[piece_rows + 1 + i : piece_rows + 2 + i].reshape(width)

    value_send_back, attn_share, grad_value_bias, grad_taps, *vectors = run(
        value_sum_body,
        [((n, piece_rows, width), BF16), ((n, part_rows, width), BF16), ((local,), F32), ((heads, taps), F32)]
        + [((width,), F32)] * 6,
        (value_part,),
        "value_sums",
        far_out=tuple(range(2, 10)),
        us=0.05,
    )
    attn_shares = [attn_share] + others(attn_share)
    value_back = exchange(value_send_back)

    def weights_body(keep_ref, far_ref, up_w_ref, up_bias_ref, down_w_ref,
                     up_ref, up_sum_ref, grad_ref, act_ref, pre_ref, raw_ref, back_ref, finish):
        sides = (keep_ref, far_ref)
        low = jnp.concatenate([ref[:, :, :width].reshape(total // 2, width) for ref in sides], axis=0)
        down = jnp.concatenate(
            [ref[:, :, width : 2 * width].reshape(total // 2, width) for ref in sides], axis=0
        )
        raw_ref[...] = nn(low, up_w_ref[...])
        back_ref[...] = nt(down, down_w_ref[...])
        up_sum = jnp.zeros((1, units), F32)
        for i in range(n):
            rows = slice(i * chosen, (i + 1) * chosen)
            pre = raw_ref[rows] + line(up_bias_ref)
            cdf = cdf_of(pre)
            act_ref[rows] = (pre * cdf).astype(BF16)
            slope = cdf + pre * jnp.exp(-0.5 * pre * pre) * 0.3989422804014327
            grad_pre = (back_ref[rows] * slope).astype(BF16)
            pre_ref[rows] = grad_pre
            up_sum += column_sum(grad_pre.astype(F32))
        up_sum_ref[...] = up_sum.reshape(units)
        up_ref[...] = tn(low, pre_ref[...])
        finish(0)
        grad_ref[...] = tn(act_ref[...], down)

    grad_up, up_sum, grad_down = run(
        weights_body,
        [((width, units), F32), ((units,), F32), ((units, width), F32)],
        (*keeps, up_weight, up_bias, down_weight),
        "weights",
        also=tuple((array, pltpu.VMEM) for array in rest_parts[1:]),
        far=(0, 1, 2, 3, 4),
        far_out=(0, 1, 2),
        early=(0,),
        scratch=[pltpu.VMEM((total, units), BF16)] * 2 + [pltpu.VMEM((total, units), F32)] * 2,
        us=3,
    )

    def last_body(ids_ref, *refs, ready, finish):
        part_refs, attn_refs, refs = refs[:tp], refs[tp : 2 * tp], refs[2 * tp :]
        (back_ref, first_ref, bias_ref, gain_ref, shift_ref, chosen_ref, order_ref, keep_ref,
         out_ref, grad_out_ref, grad_value_ref, sorted_ref, all_ref, context_ref) = refs
        for i in range(n):
            grad_value_ref[i * piece_rows : (i + 1) * piece_rows] = back_ref[i].astype(F32)
        finish(2)
        for k, ref in enumerate(attn_refs):
            for i in range(n):
                start = i * chosen + (ids_ref[1] ^ k) * part_rows
                all_ref[pl.ds(pl.multiple_of(start, part_rows), part_rows)] = ref[i]
        second = paired([r[...].astype(F32) for r in part_refs])
        ready()
        second = first_ref[...] + second + line(bias_ref)
        unit, _ = norm_stats(second)
        sorted_ref[:chosen] = chosen_ref[...]
        sorted_ref[chosen:] = (unit * line(gain_ref) + line(shift_ref)).astype(BF16)
        out_ref[...] = tn(order_ref[...], sorted_ref[...]).astype(BF16)
        finish(0)
        tops = keep_ref[:, :, 2 * width : 2 * width + local].reshape(total // 2, local)
        lows = keep_ref[:, :, 2 * width + local : 2 * width + 2 * local].reshape(total // 2, local)
        for i in range(n):
            context_ref[i * chosen : i * chosen + mid] = tops[i * mid : (i + 1) * mid]
            context_ref[i * chosen + mid : (i + 1) * chosen] = lows[i * mid : (i + 1) * mid]
        grad_out_ref[...] = tn(context_ref[...], all_ref[...])

    output, grad_out, grad_value = run(
        last_body,
        [((tokens, width), BF16), ((local, width), F32), ((local, width), F32)],
        (ids, *rest_parts, *attn_shares, value_back, rest_first, down_bias, second_gain, second_shift, out_chosen,
         order, keeps[0]),
        "last",
        smem=1,
        far=tuple(range(2 * tp + 2, 2 * tp + 9)),
        late=tuple(range(2 * tp + 2, 2 * tp + 9)),
        far_out=(0, 1, 2),
        early=(0, 2),
        scratch=[pltpu.VMEM((tokens, width), BF16), pltpu.VMEM((total, width), BF16),
                 pltpu.VMEM((total, local), BF16)],
        us=0.05,
    )
    return (
        output,
        input_grad,
        grad_value.T,
        grad_value_bias,
        grad_out,
        vectors[5],
        vectors[3],
        vectors[4],
        grad_up,
        up_sum,
        grad_down,
        vectors[2],
        vectors[0],
        vectors[1],
        grad_taps,
    )


def solution(mesh):
    return jax.shard_map(
        per_device,
        mesh=mesh,
        in_specs=(
            P("seq", None),
            P(None, "tp"),
            P("tp"),
            P("tp", None),
            P(),
            P(),
            P(),
            P(None, "tp"),
            P("tp"),
            P("tp", None),
            P(),
            P(),
            P(),
            P("tp", None),
            P("seq", "tp", None),
            P("seq", "tp", None),
            P("seq"),
            P("seq", None),
        ),
        out_specs=(
            P("seq", None),
            P("seq", None),
            P(None, "tp"),
            P("tp"),
            P("tp", None),
            P(),
            P(),
            P(),
            P(None, "tp"),
            P("tp"),
            P("tp", None),
            P(),
            P(),
            P(),
            P("tp", None),
        ),
        check_vma=False,
    )
```

```python
from functools import partial

import jax
import jax.numpy as jnp
import numpy as np
from jax import lax
from jax.experimental import pallas as pl
from jax.experimental.pallas import tpu as pltpu
from jax.sharding import PartitionSpec as P

F32, BF16, I32 = jnp.float32, jnp.bfloat16, jnp.int32
MIB = 1 << 20
VMEM_MIB = 20


def dot(a, b, dims):
    return lax.dot_general(a, b, (dims, ((), ())), preferred_element_type=F32)


def nn(a, b):
    return dot(a, b, ((1,), (0,)))


def nt(a, b):
    return dot(a, b, ((1,), (1,)))


def tn(a, b):
    return dot(a, b, ((0,), (0,)))


def split2(x):
    high = x.astype(BF16)
    return high, (x - high.astype(F32)).astype(BF16)


def split3(x):
    high = x.astype(BF16)
    rest = x - high.astype(F32)
    middle = rest.astype(BF16)
    return high, middle, (rest - middle.astype(F32)).astype(BF16)


def iota(shape, dim):
    return lax.broadcasted_iota(I32, shape, dim)


def one_zero(condition):
    return jnp.where(condition, 1.0, 0.0).astype(BF16)


def call(body, outs, args, name, scratch=(), smem=0, far=(), far_out=(), late=(), early=(),
         after=(), us=1.0):
    shapes = [outs] if isinstance(outs, tuple) else outs
    count = len(args)
    arrays = [*args, *(jax.ShapeDtypeStruct(shape, dtype) for shape, dtype in shapes)]
    moved = [*far, *(count + i for i in far_out)]
    spaces = [
        pltpu.SMEM if i < smem else pltpu.HBM if i in moved else pltpu.VMEM for i in range(len(arrays))
    ]
    inner = [pltpu.VMEM(arrays[i].shape, arrays[i].dtype) for i in moved]
    extra = len(after)

    held = sum(
        int(np.prod(ref.shape)) * jnp.dtype(ref.dtype).itemsize for ref in (*inner, *scratch)
    )
    limit = max(VMEM_MIB * MIB, held + 12 * MIB)

    def kernel(*refs):
        refs = list(refs[:count] + refs[count + extra :])
        given, here, rest = refs[: len(arrays)], refs[len(arrays) :][: len(inner)], refs[len(arrays) + len(inner) :]
        copies = []
        for slot, i in enumerate(moved):
            pair = (refs[i], here[slot]) if i < count else (here[slot], refs[i])
            copies.append(pltpu.make_async_copy(*pair, rest[-1].at[slot]))
            given[i] = here[slot]
        for copy in copies[: len(far)]:
            copy.start()
        for i, copy in zip(far, copies):
            if i not in late:
                copy.wait()

        def ready():
            for i, copy in zip(far, copies):
                if i in late:
                    copy.wait()

        sends = dict(zip(far_out, copies[len(far) :]))

        def finish(i):
            sends[i].start()

        options = {"ready": ready} if late else {}
        if early:
            options["finish"] = finish
        body(*given, *(rest[:-1] if moved else rest), **options)
        for i in sends:
            if i not in early:
                finish(i)
        for copy in sends.values():
            copy.wait()

    placed = [
        a if i < smem else pltpu.with_memory_space_constraint(a, spaces[i]) for i, a in enumerate(args)
    ]
    return pl.pallas_call(
        kernel,
        out_shape=[spaces[i](arrays[i].shape, arrays[i].dtype) for i in range(count, len(arrays))],
        in_specs=[pl.BlockSpec(memory_space=space) for space in spaces[:count]]
        + [pl.BlockSpec(memory_space=space) for _, space in after],
        out_specs=[pl.BlockSpec(memory_space=space) for space in spaces[count:]],
        scratch_shapes=[*inner, *scratch, *([pltpu.SemaphoreType.DMA((len(inner),))] if moved else [])],
        compiler_params=pltpu.CompilerParams(vmem_limit_bytes=limit),
        cost_estimate=pl.CostEstimate(
            flops=int(us * 1.1e9), bytes_accessed=0, transcendentals=0
        ),
        name=name,
    )(*placed, *(pltpu.with_memory_space_constraint(*pair) for pair in after))


def line(ref):
    return ref[...].reshape(1, ref.shape[0])


def norm_stats(rows):
    centre = rows - jnp.mean(rows, -1, keepdims=True)
    spread = jnp.mean(centre * centre, -1, keepdims=True)
    q = lax.rsqrt(spread + 1e-05)
    return centre * q, q


def cdf_of(u):
    return 0.5 * (1.0 + lax.erf(u * 0.7071067811865476))


def gelu_grad(u):
    return cdf_of(u) + u * jnp.exp(-0.5 * u * u) * 0.3989422804014327


def plane_weights(heads, hashes):
    lanes = 128
    rows = heads * hashes
    wide = np.zeros((8 * lanes, 2 * lanes), np.float32)
    tall = np.zeros((64, 8 * rows), np.float32)
    for b in range(8):
        for h in range(heads):
            for m in range(hashes):
                half, power = divmod(m, 16)
                wide[b * lanes + h * hashes + m, half * lanes + h * 8 + b] = 2.0**power
                tall[half * 32 + h * 8 + b, b * rows + h * hashes + m] = 2.0**power
    return jnp.asarray(wide, BF16), jnp.asarray(tall, BF16)


def query_words(codes, wide):
    whole = codes.astype(F32).astype(I32)
    bits = jnp.concatenate(
        [((whole >> b) & 1).astype(F32).astype(BF16) for b in range(8)], axis=1
    )
    both = nn(bits, wide)
    return both[:, :128].astype(I32) | (both[:, 128:].astype(I32) << 16)


def key_words(codes, tall):
    whole = codes.astype(F32).astype(I32)
    bits = jnp.concatenate(
        [((whole >> b) & 1).astype(F32).astype(BF16) for b in range(8)], axis=0
    )
    both = nn(tall, bits)
    return both[:32].astype(I32) | (both[32:].astype(I32) << 16)


def matches(query_block, key_block, head):
    apart = None
    for b in range(8):
        word = head * 8 + b
        unlike = query_block[:, word : word + 1] ^ key_block[word : word + 1, :]
        apart = unlike if apart is None else apart | unlike
    return (32 - lax.population_count(apart)).astype(F32).astype(BF16)


def per_device(
    inputs,
    value_weight,
    value_bias,
    out_weight,
    out_bias,
    first_gain,
    first_shift,
    up_weight,
    up_bias,
    down_weight,
    down_bias,
    second_gain,
    second_shift,
    conv_weight,
    query_codes,
    key_codes,
    masked,
    out_grad,
):
    n = lax.axis_size("seq")
    tp = lax.axis_size("tp")
    tokens, width = inputs.shape
    heads, hashes = query_codes.shape[1], query_codes.shape[2]
    taps = conv_weight.shape[1]
    half = (taps - 1) // 2
    local = value_weight.shape[1]
    dim = local // heads
    units = up_weight.shape[1]
    chosen = tokens // 4
    rest = tokens - chosen
    piece = rest // tp
    part_rows = chosen // tp
    codes_rows = heads * hashes
    window = tokens + 128
    total = n * chosen
    ids = jnp.stack([lax.axis_index("seq"), lax.axis_index("tp")]).astype(I32)
    wide, tall = plane_weights(heads, hashes)

    previous = []

    def run(*args, also=(), **options):
        results = call(*args, after=(*previous, *also), **options)
        previous[:] = [(results[0], pltpu.HBM if 0 in options.get("far_out", ()) else pltpu.VMEM)]
        return results

    def swap(array, k):
        return lax.ppermute(array, "tp", [(i, i ^ k) for i in range(tp)])

    def others(array):
        return [swap(array, k) for k in range(1, tp)]

    def others_by_steps(array):
        far = swap(array, 2)
        return [swap(array, 1), far, swap(far, 1)]

    def exchange(array):
        return lax.all_to_all(array, "seq", 0, 0)

    query_t = jnp.transpose(query_codes, (1, 2, 0)).reshape(codes_rows, tokens)
    key_t = jnp.transpose(key_codes, (1, 2, 0)).reshape(codes_rows, tokens)
    value_t = value_weight.T
    out_all = [out_weight] + others_by_steps(out_weight)
    value_all = [value_t] + others_by_steps(value_t)

    def order_of(masked_ref):
        flags = jnp.broadcast_to(line(masked_ref).astype(F32), (8, tokens))
        upto = one_zero(iota((tokens, tokens), 0) <= iota((tokens, tokens), 1))
        count = nn(flags.astype(BF16), upto)
        spot = iota((8, tokens), 1).astype(F32)
        target = jnp.where(flags > 0, count - 1.0, count[:, tokens - 1 :] + spot - count)
        return one_zero(iota((tokens, tokens), 0) == target[:1].astype(I32))

    def placed_codes(query_ref):
        where = jnp.where(
            iota((128 - codes_rows, tokens), 0) == 0, iota((128 - codes_rows, tokens), 1), 0
        )
        return jnp.concatenate([query_ref[...], where], axis=0).astype(F32).astype(BF16)

    def order_body(masked_ref, query_ref, chosen_ref):
        top = nt(order_of(masked_ref)[:chosen], placed_codes(query_ref)).astype(BF16)
        for i in range(n):
            chosen_ref[i] = top

    (chosen_codes,) = run(
        order_body,
        ((n, chosen, 128), BF16),
        (masked, query_t),
        "order",
        far=(0, 1),
        us=2,
    )
    all_codes = exchange(chosen_codes)

    def prepare_body(inputs_ref, weight_ref, bias_ref, key_ref, query_ref, grad_ref, masked_ref, conv_ref,
                     value_ref, send_ref, top_ref, low_ref, cot_ref, band_ref, low_band_ref, back_ref,
                     codes_ref, order_ref, pad_ref):
        order_ref[...] = order_of(masked_ref)
        codes_ref[...] = nt(order_ref[chosen:], placed_codes(query_ref)).astype(BF16)
        values = (nt(inputs_ref[...], weight_ref[...]) + line(bias_ref)).astype(BF16)
        value_ref[...] = values
        same = one_zero(iota((local, local), 0) == iota((local, local), 1))
        send_ref[:codes_rows] = key_ref[...].astype(F32).astype(BF16)
        send_ref[codes_rows:] = nt(same, values).astype(BF16)
        order = order_ref[...]
        moved = nn(order, inputs_ref[...]).astype(BF16)
        top_ref[...] = moved[:chosen]
        low_ref[...] = moved[chosen:]
        pick = order_ref[:chosen]
        flags = jnp.broadcast_to(line(masked_ref).astype(F32), (8, tokens)).astype(BF16)
        valid = nt(pick, flags)[:, :1]
        parts = split3(grad_ref[...])
        cot_ref[...] = (nn(pick, parts[0]) + nn(pick, parts[1]) + nn(pick, parts[2])) * valid
        pad_ref[...] = jnp.zeros_like(pad_ref)
        pad_ref[:heads, :taps] = conv_ref[...]
        turn = one_zero(iota((128, 128), 0) + iota((128, 128), 1) == taps - 1)
        padded = pad_ref[...]
        parts = split3(padded)
        turned = nn(parts[0], turn) + nn(parts[1], turn) + nn(parts[2], turn)
        blank = jnp.zeros((8, window - 128), F32)
        for h in range(heads):
            for ahead, source in ((True, padded), (False, turned)):
                long = jnp.concatenate([source, blank], axis=1)
                spread = jnp.broadcast_to(long[h : h + 1], (tokens, window))
                band = pltpu.roll(spread, 0, 1, stride=1, stride_axis=0)
                for at, level in zip((0, window), split2(band)):
                    if ahead:
                        moved = nn(order, level).astype(BF16)
                        band_ref[h, :, at : at + window] = moved[:chosen]
                        low_band_ref[h, :, at : at + window] = moved[chosen:]
                    else:
                        back_ref[h, :, at : at + window] = level

    (values, value_send, top_inputs, low_inputs, cot, bands, low_bands, back_bands, rest_codes,
     order) = run(
        prepare_body,
        [((tokens, local), BF16), ((codes_rows + local, tokens), BF16), ((chosen, width), BF16),
         ((rest, width), BF16), ((chosen, width), F32), ((heads, chosen, 2 * window), BF16),
         ((heads, rest, 2 * window), BF16), ((heads, tokens, 2 * window), BF16), ((rest, 128), BF16),
         ((tokens, tokens), BF16)],
        (inputs, value_t, value_bias, key_t, query_t, out_grad, masked, conv_weight),
        "prepare",
        far=tuple(range(8)),
        far_out=(0, 2, 3, 4, 5, 6, 7, 8, 9),
        scratch=[pltpu.VMEM((8, 128), F32)],
        us=4,
    )
    all_keys = lax.all_gather(value_send, "seq", axis=0)

    def count_body(codes_ref, send_ref, wide_ref, tall_ref, count_ref, out_ref, finish):
        keys = key_words(send_ref[:codes_rows], tall_ref[...])
        queries = query_words(codes_ref[...].reshape(total, 128), wide_ref[...])
        for h in range(heads):
            for r in range(0, total, tokens):
                for c in range(0, tokens, 128):
                    count_ref[h, r : r + tokens, c : c + 128] = matches(
                        queries[r : r + tokens], keys[:, c : c + 128], h
                    )
        finish(0)
        for h in range(heads):
            turned = send_ref[codes_rows + h * dim : codes_rows + (h + 1) * dim]
            read = nt(count_ref[h], turned).astype(BF16)
            for i in range(n):
                out_ref[i, :chosen, h * dim : (h + 1) * dim] = read[i * chosen : (i + 1) * chosen]

    counts, reads = run(
        count_body,
        [((heads, total, tokens), BF16), ((n, chosen, local), BF16)],
        (all_codes, value_send, wide, tall),
        "count",
        far_out=(0,),
        early=(0,),
        us=5,
    )
    edges = lax.optimization_barrier((values, reads))[0]
    before = lax.ppermute(edges[tokens - half :], "seq", [(i, i + 1) for i in range(n - 1)])
    behind = lax.ppermute(edges[:half], "seq", [(i + 1, i) for i in range(n - 1)])
    reads = exchange(reads)

    def unit_rows(value_sum):
        return lax.rsqrt(jnp.mean(value_sum * value_sum, -1, keepdims=True) + 1e-05)

    def context_body(reads_ref, value_ref, band_ref, before_ref, behind_ref, context_ref, sum_ref, near_ref, ready, finish):
        total_read = reads_ref[0].astype(F32)
        for i in range(1, n):
            total_read += reads_ref[i].astype(F32)
        total_read = total_read * (1.0 / hashes)
        sum_ref[...] = total_read
        near_ref[:half] = before_ref[...]
        ready()
        near_ref[half : half + tokens] = value_ref[...]
        near_ref[half + tokens : 2 * half + tokens] = behind_ref[...]
        near_ref[2 * half + tokens :] = jnp.zeros((window - tokens - 2 * half, local), BF16)
        finish(2)
        near = near_ref[...]
        twice = jnp.concatenate([near, near], axis=0)
        for h in range(heads):
            cols = slice(h * dim, (h + 1) * dim)
            mine = total_read[:, cols]
            conv = nn(band_ref[h], twice[:, cols])
            context_ref[:, cols] = (mine * unit_rows(mine) + conv).astype(BF16)

    context, value_sum, near = run(
        context_body,
        [((chosen, local), BF16), ((chosen, local), F32), ((window, local), BF16)],
        (reads, values, bands, before, behind),
        "context",
        far=(1, 2),
        late=(1, 2),
        far_out=(2,),
        early=(2,),
        us=2,
    )
    contexts = [context] + others(context)

    def paired(terms):
        while len(terms) > 1:
            terms = [terms[i] + terms[i + 1] for i in range(0, len(terms), 2)]
        return terms[0]

    def joined(context_refs, out_refs):
        return paired([nn(a[...], b[...]) for a, b in zip(context_refs, out_refs)])

    def feed(low, up_ref, up_bias_ref, down_ref):
        pre = nn(low, up_ref[...]) + line(up_bias_ref)
        act = (pre * cdf_of(pre)).astype(BF16)
        return pre, nn(act, down_ref[...]).astype(BF16)

    def first_body(*refs, ready, finish):
        context_refs, out_refs, refs = refs[:tp], refs[tp : 2 * tp], refs[2 * tp :]
        (inputs_ref, bias_ref, gain_ref, shift_ref, up_ref, up_bias_ref, down_ref,
         part_ref, hidden_ref, first_ref, pre_ref) = refs
        hidden = joined(context_refs, out_refs)
        ready()
        hidden = inputs_ref[...].astype(F32) + hidden + line(bias_ref)
        hidden_ref[...] = hidden
        finish(1)
        unit, _ = norm_stats(hidden)
        first = unit * line(gain_ref) + line(shift_ref)
        first_ref[...] = first
        finish(2)
        pre, part = feed(first.astype(BF16), up_ref, up_bias_ref, down_ref)
        pre_ref[...] = pre
        part_ref[...] = part

    part, hidden, first, pre_act = run(
        first_body,
        [((chosen, width), BF16), ((chosen, width), F32), ((chosen, width), F32), ((chosen, units), F32)],
        (*contexts, *out_all, top_inputs, out_bias, first_gain, first_shift, up_weight, up_bias, down_weight),
        "first",
        far=tuple(range(tp, 2 * tp + 4)) + (2 * tp + 5,),
        far_out=(1, 2, 3),
        early=(1, 2),
        late=tuple(range(2 * tp, 2 * tp + 4)) + (2 * tp + 5,),
        us=3,
    )
    parts = [part] + others(part)

    def slope_body(pre_ref, slope_ref):
        slope_ref[...] = gelu_grad(pre_ref[...])

    (slope,) = run(slope_body, ((chosen, units), F32), (pre_act,), "slope", far=(0,), us=1.5)

    def back_norm(grad, unit, q, gain):
        scaled = grad * gain
        return q * (
            scaled
            - jnp.mean(scaled, -1, keepdims=True)
            - unit * jnp.mean(scaled * unit, -1, keepdims=True)
        )

    def put_sums(ref, sums):
        for i, vector in enumerate(sums):
            ref[i : i + 1] = vector

    def column_sum(array):
        return jnp.sum(array, 0, keepdims=True)

    def second_body(ids_ref, *refs, ready, finish):
        part_refs, refs = refs[:tp], refs[tp:]
        (first_ref, bias_ref, gain_ref, shift_ref, cot_ref, slope_ref, down_ref, up_ref,
         context_ref, output_ref, grad_ref, back_ref, sums_ref, keep_ref, low_ref) = refs
        second = paired([r[...].astype(F32) for r in part_refs])
        ready()
        second = first_ref[...] + second + line(bias_ref)
        unit, q = norm_stats(second)
        output_ref[...] = (unit * line(gain_ref) + line(shift_ref)).astype(BF16)
        finish(0)
        grad = back_norm(cot_ref[...], unit, q, line(gain_ref))
        grad_ref[...] = grad
        low = grad.astype(BF16)
        grad_pre = (nt(low, down_ref[...]) * slope_ref[...]).astype(BF16)
        back_ref[...] = nt(grad_pre, up_ref[...]).astype(BF16)
        put_sums(sums_ref, [column_sum(cot_ref[...] * unit), column_sum(cot_ref[...]), column_sum(grad)])
        low_ref[:, :width] = first_ref[...].astype(BF16)
        low_ref[:, width:] = low
        keep_ref[:, : 2 * width] = low_ref[pl.ds(pl.multiple_of(ids_ref[1] % 2 * mid, mid), mid)]
        keep_ref[:, 2 * width : 2 * width + local] = context_ref[:mid]
        keep_ref[:, 2 * width + local : 2 * width + 2 * local] = context_ref[mid:]
        keep_ref[:, 2 * width + 2 * local :] = jnp.zeros((mid, kept - 2 * width - 2 * local), BF16)

    mid = chosen // 2
    kept = -(-2 * (width + local) // 1024) * 1024
    out_chosen, grad_second, back, sums, keep = run(
        second_body,
        [((chosen, width), BF16), ((chosen, width), F32), ((chosen, width), BF16), ((8, width), F32),
         ((mid, kept), BF16)],
        (ids, *parts, first, down_bias, second_gain, second_shift, cot, slope, down_weight, up_weight, context),
        "second",
        also=tuple((weight, pltpu.HBM) for weight in value_all[1:]),
        far=tuple(range(tp + 1, tp + 6)),
        late=tuple(range(tp + 1, tp + 6)),
        far_out=(0, 4),
        early=(0,),
        smem=1,
        scratch=[pltpu.VMEM((chosen, 2 * width), BF16)],
        us=3,
    )
    backs = [back] + others(back)
    keeps = lax.all_gather(keep, "seq", axis=0)

    def rest_counts(count_ref, queries, word_ref, head):
        @pl.loop(0, n * tokens // 256)
        def _(i):
            for c in range(2):
                lanes = pl.ds(pl.multiple_of(i * 256 + c * 128, 128), 128)
                count_ref[:, lanes] = matches(queries, word_ref[:, lanes], head)

    def rest_read(count_ref, keys_ref, head):
        start = codes_rows + head * dim
        turned = jnp.concatenate([keys_ref[i, start : start + dim] for i in range(n)], axis=1)
        return nt(count_ref[...], turned) * (1.0 / hashes)

    def rest_words_body(codes_ref, keys_ref, wide_ref, tall_ref, query_ref, word_ref, first_ref,
                        key_ref, count_ref, ready):
        queries = query_words(codes_ref[...], wide_ref[...])
        query_ref[...] = queries
        ready()
        for i in range(n):
            key_ref[:, i * tokens : (i + 1) * tokens] = keys_ref[i, :codes_rows]
        word_ref[...] = key_words(key_ref[...], tall_ref[...])
        rest_counts(count_ref, queries, word_ref, 0)
        first_ref[...] = rest_read(count_ref, keys_ref, 0)

    rest_queries, key_bits, rest_sum = run(
        rest_words_body,
        [((rest, 128), I32), ((32, n * tokens), I32), ((rest, dim), F32)],
        (rest_codes, all_keys, wide, tall),
        "rest_words",
        far=(0, 1, 2, 3),
        late=(1,),
        scratch=[pltpu.VMEM((codes_rows, n * tokens), BF16), pltpu.VMEM((rest, n * tokens), BF16)],
        us=5,
    )

    def hidden_body(ids_ref, *refs, ready, finish):
        back_refs, refs = refs[:tp], refs[tp:]
        grad_ref, hidden_ref, gain_ref, sums_ref, read_ref, weight_ref, out_ref, send_ref, share_ref, all_ref, attn_ref = refs
        grad = grad_ref[...] + paired([r[...].astype(F32) for r in back_refs])
        ready()
        unit, q = norm_stats(hidden_ref[...])
        grad_hidden = back_norm(grad, unit, q, line(gain_ref))
        out_ref[...] = grad_hidden
        finish(0)
        low = grad_hidden.astype(BF16)
        y = nt(low, weight_ref[...]).astype(BF16)
        for h in range(heads):
            cols = slice(h * dim, (h + 1) * dim)
            read, at = read_ref[:, cols], y[:, cols].astype(F32)
            r = unit_rows(read)
            back = r * (at - read * (r * r) * jnp.mean(at * read, -1, keepdims=True))
            send_ref[0, :, cols] = (back * (1.0 / hashes)).astype(BF16)
        send_ref[0, :, local:] = y
        for i in range(1, n):
            send_ref[i] = send_ref[0]
        attn_ref[...] = low
        share_ref[...] = attn_ref[pl.ds(pl.multiple_of(ids_ref[1] * part_rows, part_rows), part_rows)]
        all_ref[:3] = sums_ref[:3]
        put_sums(all_ref.at[3:6], [column_sum(grad * unit), column_sum(grad), column_sum(grad_hidden)])
        all_ref[6:] = jnp.zeros((2, width), F32)

    grad_hidden, read_send, share, sums = run(
        hidden_body,
        [((chosen, width), F32), ((n, chosen, 2 * local), BF16), ((part_rows, width), BF16), ((8, width), F32)],
        (ids, *backs, grad_second, hidden, first_gain, sums, value_sum, out_weight),
        "hidden",
        also=((all_keys, pltpu.HBM),),
        far=(tp + 2, tp + 3),
        late=(tp + 2, tp + 3),
        far_out=(0, 2, 3),
        early=(0,),
        smem=1,
        scratch=[pltpu.VMEM((chosen, width), BF16)],
        us=2,
    )
    read_all = exchange(read_send)

    def rest_body(query_ref, word_ref, first_ref, keys_ref, band_ref, near_ref, context_ref, count_ref, ready):
        queries = query_ref[...]
        for h in range(heads):
            if h:
                rest_counts(count_ref, queries, word_ref, h)
                if h == 1:
                    ready()
                    near = near_ref[...]
                    twice = jnp.concatenate([near, near], axis=0)
            cols = slice(h * dim, (h + 1) * dim)
            if h:
                mine = rest_read(count_ref, keys_ref, h)
                conv = nn(band_ref[h], twice[:, cols])
                context_ref[:, cols] = (mine * unit_rows(mine) + conv).astype(BF16)
        mine = first_ref[...]
        conv = nn(band_ref[0], twice[:, :dim])
        context_ref[:, :dim] = (mine * unit_rows(mine) + conv).astype(BF16)

    (rest_context,) = run(
        rest_body,
        ((rest, local), BF16),
        (rest_queries, key_bits, rest_sum, all_keys, low_bands, near),
        "rest_context",
        far=(3, 4, 5),
        late=(3, 4, 5),
        scratch=[pltpu.VMEM((rest, n * tokens), BF16)],
        us=6,
    )
    rest_contexts = [rest_context] + others(rest_context)

    def values_body(ids_ref, read_ref, count_ref, band_ref, codes_ref, grad_ref, dense_ref, ready):
        me = ids_ref[0]
        ready()
        dense = jnp.zeros((window, local), F32)
        for step in (-1, 0, 1):
            source = jnp.clip(me + step, 0, n - 1)
            inside = jnp.logical_and(me + step >= 0, me + step < n)
            there = read_ref[source][:, local:]
            spots = codes_ref[source][:, codes_rows : codes_rows + 1].astype(F32).astype(I32)
            spots = jnp.where(inside, spots + step * tokens + half, -1)
            place = one_zero(spots == iota((chosen, window), 1))
            dense += tn(place, there)
        dense_low = dense.astype(BF16)
        dense_ref[...] = dense_low
        twice = jnp.concatenate([dense_low, dense_low], axis=0)
        for h in range(heads):
            cols = slice(h * dim, (h + 1) * dim)
            read = read_ref[:, :, cols].reshape(total, dim)
            grad = tn(count_ref[h], read) + nn(band_ref[h], twice[:, cols])
            grad_ref[:, cols] = grad.astype(BF16)

    grad_values, dense = run(
        values_body,
        [((tokens, local), BF16), ((window, local), BF16)],
        (ids, read_all, counts, back_bands, all_codes),
        "values_back",
        smem=1,
        far=(2, 3, 4),
        late=(2, 3, 4),
        us=4,
    )
    grads = [grad_values] + others(grad_values)

    piece_rows = local // n
    extra = 8

    def value_grad_body(inputs_ref, grad_ref, dense_ref, near_ref, sums_ref, share_ref, send_ref, row_ref):
        grad = grad_ref[...]
        weight = tn(grad, inputs_ref[...]).astype(BF16)
        row_ref[...] = jnp.zeros_like(row_ref)
        row_ref[:1, :local] = column_sum(grad.astype(F32))
        row_ref[1:7] = sums_ref[:6]
        turn = one_zero(iota((tokens, tokens), 0) + iota((tokens, tokens), 1) == tokens - 1)
        turned = nn(turn, dense_ref[half : half + tokens]).astype(BF16)
        for h in range(heads):
            cols = slice(h * dim, (h + 1) * dim)
            both = nt(turned[:, cols], near_ref[:, cols])
            aligned = pltpu.roll(both, window - tokens + 1, 1, stride=1, stride_axis=0)
            row_ref[:1, 256 + 128 * h : 384 + 128 * h] = column_sum(aligned)[:, :128]
        for i in range(n):
            send_ref[i, :piece_rows] = weight[i * piece_rows : (i + 1) * piece_rows]
            send_ref[i, piece_rows : piece_rows + extra] = row_ref[...].astype(BF16)
            send_ref[i, piece_rows + extra :] = share_ref[...]

    (value_part,) = run(
        value_grad_body,
        ((n, piece_rows + extra + part_rows, width), BF16),
        (inputs, grad_values, dense, near, sums, share),
        "value_grad",
        also=tuple((array, pltpu.HBM) for array in rest_contexts[1:]),
        far=(0, 3, 4, 5),
        scratch=[pltpu.VMEM((extra, width), F32)],
        us=2.5,
    )
    value_part = exchange(value_part)

    def rest_first_body(*refs, ready):
        context_refs, out_refs, refs = refs[:tp], refs[tp : 2 * tp], refs[2 * tp :]
        (inputs_ref, bias_ref, gain_ref, shift_ref, up_ref, up_bias_ref, down_ref, part_ref, first_ref) = refs
        hidden = joined(context_refs, out_refs)
        ready()
        hidden = inputs_ref[...].astype(F32) + hidden + line(bias_ref)
        unit, _ = norm_stats(hidden)
        first = unit * line(gain_ref) + line(shift_ref)
        first_ref[...] = first
        part_ref[...] = feed(first.astype(BF16), up_ref, up_bias_ref, down_ref)[1]

    rest_part, rest_first = run(
        rest_first_body,
        [((rest, width), BF16), ((rest, width), F32)],
        (*rest_contexts, *out_all, low_inputs, out_bias, first_gain, first_shift, up_weight, up_bias,
         down_weight),
        "rest_first",
        also=tuple((array, pltpu.HBM) for array in grads[1:]),
        far=tuple(range(2 * tp + 7)),
        late=tuple(range(2 * tp, 2 * tp + 7)),
        far_out=(1,),
        us=4,
    )
    rest_parts = [rest_part] + others(rest_part)
    keeps = [keeps, swap(lax.optimization_barrier((keeps, rest_part))[0], 1)]

    def input_body(*refs):
        grad_refs, weight_refs, (order_ref, hidden_ref, out_ref) = (
            refs[:tp], refs[tp : 2 * tp], refs[2 * tp :])
        pick = order_ref[:chosen]
        parts = split3(hidden_ref[...])
        placed = tn(pick, parts[0]) + tn(pick, parts[1]) + tn(pick, parts[2])
        out_ref[...] = placed + joined(grad_refs, weight_refs)

    (input_grad,) = run(
        input_body,
        ((tokens, width), F32),
        (*grads, *value_all, order, grad_hidden),
        "input_grad",
        far=tuple(range(2 * tp + 2)),
        far_out=(0,),
        us=0.05,
    )

    def value_sum_body(part_ref, send_ref, attn_ref, bias_ref, taps_ref, *vector_refs):
        rows = piece_rows + extra
        whole = part_ref[0, :rows].astype(F32)
        for i in range(1, n):
            whole += part_ref[i, :rows].astype(F32)
        for i in range(n):
            send_ref[i] = whole[:piece_rows].astype(BF16)
            attn_ref[i] = part_ref[i, rows:]
        bias_ref[...] = whole[piece_rows : piece_rows + 1, :local].reshape(local)
        for h in range(heads):
            taps_ref[h : h + 1] = whole[piece_rows : piece_rows + 1, 256 + 128 * h : 256 + 128 * h + taps]
        for i, ref in enumerate(vector_refs):
            ref[...] = whole[piece_rows + 1 + i : piece_rows + 2 + i].reshape(width)

    value_send_back, attn_share, grad_value_bias, grad_taps, *vectors = run(
        value_sum_body,
        [((n, piece_rows, width), BF16), ((n, part_rows, width), BF16), ((local,), F32), ((heads, taps), F32)]
        + [((width,), F32)] * 6,
        (value_part,),
        "value_sums",
        far_out=tuple(range(2, 10)),
        us=0.05,
    )
    attn_shares = [attn_share] + others(attn_share)
    value_back = exchange(value_send_back)

    def weights_body(keep_ref, far_ref, up_w_ref, up_bias_ref, down_w_ref,
                     up_ref, up_sum_ref, grad_ref, act_ref, pre_ref, raw_ref, back_ref, finish):
        sides = (keep_ref, far_ref)
        low = jnp.concatenate([ref[:, :, :width].reshape(total // 2, width) for ref in sides], axis=0)
        down = jnp.concatenate(
            [ref[:, :, width : 2 * width].reshape(total // 2, width) for ref in sides], axis=0
        )
        raw_ref[...] = nn(low, up_w_ref[...])
        back_ref[...] = nt(down, down_w_ref[...])
        up_sum = jnp.zeros((1, units), F32)
        for i in range(n):
            rows = slice(i * chosen, (i + 1) * chosen)
            pre = raw_ref[rows] + line(up_bias_ref)
            cdf = cdf_of(pre)
            act_ref[rows] = (pre * cdf).astype(BF16)
            slope = cdf + pre * jnp.exp(-0.5 * pre * pre) * 0.3989422804014327
            grad_pre = (back_ref[rows] * slope).astype(BF16)
            pre_ref[rows] = grad_pre
            up_sum += column_sum(grad_pre.astype(F32))
        up_sum_ref[...] = up_sum.reshape(units)
        up_ref[...] = tn(low, pre_ref[...])
        finish(0)
        grad_ref[...] = tn(act_ref[...], down)

    grad_up, up_sum, grad_down = run(
        weights_body,
        [((width, units), F32), ((units,), F32), ((units, width), F32)],
        (*keeps, up_weight, up_bias, down_weight),
        "weights",
        also=tuple((array, pltpu.VMEM) for array in rest_parts[1:]),
        far=(0, 1, 2, 3, 4),
        far_out=(0, 1, 2),
        early=(0,),
        scratch=[pltpu.VMEM((total, units), BF16)] * 2 + [pltpu.VMEM((total, units), F32)] * 2,
        us=3,
    )

    def last_body(ids_ref, *refs, ready, finish):
        part_refs, attn_refs, refs = refs[:tp], refs[tp : 2 * tp], refs[2 * tp :]
        (back_ref, first_ref, bias_ref, gain_ref, shift_ref, chosen_ref, order_ref, keep_ref,
         out_ref, grad_out_ref, grad_value_ref, sorted_ref, all_ref, context_ref) = refs
        for i in range(n):
            grad_value_ref[i * piece_rows : (i + 1) * piece_rows] = back_ref[i].astype(F32)
        finish(2)
        for k, ref in enumerate(attn_refs):
            for i in range(n):
                start = i * chosen + (ids_ref[1] ^ k) * part_rows
                all_ref[pl.ds(pl.multiple_of(start, part_rows), part_rows)] = ref[i]
        second = paired([r[...].astype(F32) for r in part_refs])
        ready()
        second = first_ref[...] + second + line(bias_ref)
        unit, _ = norm_stats(second)
        sorted_ref[:chosen] = chosen_ref[...]
        sorted_ref[chosen:] = (unit * line(gain_ref) + line(shift_ref)).astype(BF16)
        out_ref[...] = tn(order_ref[...], sorted_ref[...]).astype(BF16)
        finish(0)
        tops = keep_ref[:, :, 2 * width : 2 * width + local].reshape(total // 2, local)
        lows = keep_ref[:, :, 2 * width + local : 2 * width + 2 * local].reshape(total // 2, local)
        for i in range(n):
            context_ref[i * chosen : i * chosen + mid] = tops[i * mid : (i + 1) * mid]
            context_ref[i * chosen + mid : (i + 1) * chosen] = lows[i * mid : (i + 1) * mid]
        grad_out_ref[...] = tn(context_ref[...], all_ref[...])

    output, grad_out, grad_value = run(
        last_body,
        [((tokens, width), BF16), ((local, width), F32), ((local, width), F32)],
        (ids, *rest_parts, *attn_shares, value_back, rest_first, down_bias, second_gain, second_shift, out_chosen,
         order, keeps[0]),
        "last",
        smem=1,
        far=tuple(range(2 * tp + 2, 2 * tp + 9)),
        late=tuple(range(2 * tp + 2, 2 * tp + 9)),
        far_out=(0, 1, 2),
        early=(0, 2),
        scratch=[pltpu.VMEM((tokens, width), BF16), pltpu.VMEM((total, width), BF16),
                 pltpu.VMEM((total, local), BF16)],
        us=0.05,
    )
    return (
        output,
        input_grad,
        grad_value.T,
        grad_value_bias,
        grad_out,
        vectors[5],
        vectors[3],
        vectors[4],
        grad_up,
        up_sum,
        grad_down,
        vectors[2],
        vectors[0],
        vectors[1],
        grad_taps,
    )


def solution(mesh):
    return jax.shard_map(
        per_device,
        mesh=mesh,
        in_specs=(
            P("seq", None),
            P(None, "tp"),
            P("tp"),
            P("tp", None),
            P(),
            P(),
            P(),
            P(None, "tp"),
            P("tp"),
            P("tp", None),
            P(),
            P(),
            P(),
            P("tp", None),
            P("seq", "tp", None),
            P("seq", "tp", None),
            P("seq"),
            P("seq", None),
        ),
        out_specs=(
            P("seq", None),
            P("seq", None),
            P(None, "tp"),
            P("tp"),
            P("tp", None),
            P(),
            P(),
            P(),
            P(None, "tp"),
            P("tp"),
            P("tp", None),
            P(),
            P(),
            P(),
            P("tp", None),
        ),
        check_vma=False,
    )
```

```python
from functools import partial

import jax
import jax.numpy as jnp
import numpy as np
from jax import lax
from jax.experimental import pallas as pl
from jax.experimental.pallas import tpu as pltpu
from jax.sharding import PartitionSpec as P

F32, BF16, I32 = jnp.float32, jnp.bfloat16, jnp.int32
MIB = 1 << 20
VMEM_MIB = 20


def dot(a, b, dims):
    return lax.dot_general(a, b, (dims, ((), ())), preferred_element_type=F32)


def nn(a, b):
    return dot(a, b, ((1,), (0,)))


def nt(a, b):
    return dot(a, b, ((1,), (1,)))


def tn(a, b):
    return dot(a, b, ((0,), (0,)))


def split2(x):
    high = x.astype(BF16)
    return high, (x - high.astype(F32)).astype(BF16)


def split3(x):
    high = x.astype(BF16)
    rest = x - high.astype(F32)
    middle = rest.astype(BF16)
    return high, middle, (rest - middle.astype(F32)).astype(BF16)


def iota(shape, dim):
    return lax.broadcasted_iota(I32, shape, dim)


def one_zero(condition):
    return jnp.where(condition, 1.0, 0.0).astype(BF16)


def call(body, outs, args, name, scratch=(), smem=0, far=(), far_out=(), late=(), early=(),
         after=(), us=1.0):
    shapes = [outs] if isinstance(outs, tuple) else outs
    count = len(args)
    arrays = [*args, *(jax.ShapeDtypeStruct(shape, dtype) for shape, dtype in shapes)]
    moved = [*far, *(count + i for i in far_out)]
    spaces = [
        pltpu.SMEM if i < smem else pltpu.HBM if i in moved else pltpu.VMEM for i in range(len(arrays))
    ]
    inner = [pltpu.VMEM(arrays[i].shape, arrays[i].dtype) for i in moved]
    extra = len(after)

    held = sum(
        int(np.prod(ref.shape)) * jnp.dtype(ref.dtype).itemsize for ref in (*inner, *scratch)
    )
    limit = max(VMEM_MIB * MIB, held + 12 * MIB)

    def kernel(*refs):
        refs = list(refs[:count] + refs[count + extra :])
        given, here, rest = refs[: len(arrays)], refs[len(arrays) :][: len(inner)], refs[len(arrays) + len(inner) :]
        copies = []
        for slot, i in enumerate(moved):
            pair = (refs[i], here[slot]) if i < count else (here[slot], refs[i])
            copies.append(pltpu.make_async_copy(*pair, rest[-1].at[slot]))
            given[i] = here[slot]
        for copy in copies[: len(far)]:
            copy.start()
        for i, copy in zip(far, copies):
            if i not in late:
                copy.wait()

        def ready():
            for i, copy in zip(far, copies):
                if i in late:
                    copy.wait()

        sends = dict(zip(far_out, copies[len(far) :]))

        def finish(i):
            sends[i].start()

        options = {"ready": ready} if late else {}
        if early:
            options["finish"] = finish
        body(*given, *(rest[:-1] if moved else rest), **options)
        for i in sends:
            if i not in early:
                finish(i)
        for copy in sends.values():
            copy.wait()

    placed = [
        a if i < smem else pltpu.with_memory_space_constraint(a, spaces[i]) for i, a in enumerate(args)
    ]
    return pl.pallas_call(
        kernel,
        out_shape=[spaces[i](arrays[i].shape, arrays[i].dtype) for i in range(count, len(arrays))],
        in_specs=[pl.BlockSpec(memory_space=space) for space in spaces[:count]]
        + [pl.BlockSpec(memory_space=space) for _, space in after],
        out_specs=[pl.BlockSpec(memory_space=space) for space in spaces[count:]],
        scratch_shapes=[*inner, *scratch, *([pltpu.SemaphoreType.DMA((len(inner),))] if moved else [])],
        compiler_params=pltpu.CompilerParams(vmem_limit_bytes=limit),
        cost_estimate=pl.CostEstimate(
            flops=int(us * 1.1e9), bytes_accessed=0, transcendentals=0
        ),
        name=name,
    )(*placed, *(pltpu.with_memory_space_constraint(*pair) for pair in after))


def line(ref):
    return ref[...].reshape(1, ref.shape[0])


def norm_stats(rows):
    centre = rows - jnp.mean(rows, -1, keepdims=True)
    spread = jnp.mean(centre * centre, -1, keepdims=True)
    q = lax.rsqrt(spread + 1e-05)
    return centre * q, q


def cdf_of(u):
    return 0.5 * (1.0 + lax.erf(u * 0.7071067811865476))


def gelu_grad(u):
    return cdf_of(u) + u * jnp.exp(-0.5 * u * u) * 0.3989422804014327


def plane_weights(heads, hashes):
    lanes = 128
    rows = heads * hashes
    wide = np.zeros((8 * lanes, 2 * lanes), np.float32)
    tall = np.zeros((64, 8 * rows), np.float32)
    for b in range(8):
        for h in range(heads):
            for m in range(hashes):
                half, power = divmod(m, 16)
                wide[b * lanes + h * hashes + m, half * lanes + h * 8 + b] = 2.0**power
                tall[half * 32 + h * 8 + b, b * rows + h * hashes + m] = 2.0**power
    return jnp.asarray(wide, BF16), jnp.asarray(tall, BF16)


def query_words(codes, wide):
    whole = codes.astype(F32).astype(I32)
    bits = jnp.concatenate(
        [((whole >> b) & 1).astype(F32).astype(BF16) for b in range(8)], axis=1
    )
    both = nn(bits, wide)
    return both[:, :128].astype(I32) | (both[:, 128:].astype(I32) << 16)


def key_words(codes, tall):
    whole = codes.astype(F32).astype(I32)
    bits = jnp.concatenate(
        [((whole >> b) & 1).astype(F32).astype(BF16) for b in range(8)], axis=0
    )
    both = nn(tall, bits)
    return both[:32].astype(I32) | (both[32:].astype(I32) << 16)


def matches(query_block, key_block, head):
    apart = None
    for b in range(8):
        word = head * 8 + b
        unlike = query_block[:, word : word + 1] ^ key_block[word : word + 1, :]
        apart = unlike if apart is None else apart | unlike
    return (32 - lax.population_count(apart)).astype(F32).astype(BF16)


def per_device(
    inputs,
    value_weight,
    value_bias,
    out_weight,
    out_bias,
    first_gain,
    first_shift,
    up_weight,
    up_bias,
    down_weight,
    down_bias,
    second_gain,
    second_shift,
    conv_weight,
    query_codes,
    key_codes,
    masked,
    out_grad,
):
    n = lax.axis_size("seq")
    tp = lax.axis_size("tp")
    tokens, width = inputs.shape
    heads, hashes = query_codes.shape[1], query_codes.shape[2]
    taps = conv_weight.shape[1]
    half = (taps - 1) // 2
    local = value_weight.shape[1]
    dim = local // heads
    units = up_weight.shape[1]
    chosen = tokens // 4
    rest = tokens - chosen
    piece = rest // tp
    part_rows = chosen // tp
    codes_rows = heads * hashes
    window = tokens + 128
    total = n * chosen
    ids = jnp.stack([lax.axis_index("seq"), lax.axis_index("tp")]).astype(I32)
    wide, tall = plane_weights(heads, hashes)

    previous = []

    def run(*args, also=(), **options):
        results = call(*args, after=(*previous, *also), **options)
        previous[:] = [(results[0], pltpu.HBM if 0 in options.get("far_out", ()) else pltpu.VMEM)]
        return results

    def swap(array, k):
        return lax.ppermute(array, "tp", [(i, i ^ k) for i in range(tp)])

    def others(array):
        return [swap(array, k) for k in range(1, tp)]

    def others_by_steps(array):
        far = swap(array, 2)
        return [swap(array, 1), far, swap(far, 1)]

    def exchange(array):
        return lax.all_to_all(array, "seq", 0, 0)

    query_t = jnp.transpose(query_codes, (1, 2, 0)).reshape(codes_rows, tokens)
    key_t = jnp.transpose(key_codes, (1, 2, 0)).reshape(codes_rows, tokens)
    value_t = value_weight.T
    out_all = [out_weight] + others_by_steps(out_weight)
    value_all = [value_t] + others_by_steps(value_t)

    def order_of(masked_ref):
        flags = jnp.broadcast_to(line(masked_ref).astype(F32), (8, tokens))
        upto = one_zero(iota((tokens, tokens), 0) <= iota((tokens, tokens), 1))
        count = nn(flags.astype(BF16), upto)
        spot = iota((8, tokens), 1).astype(F32)
        target = jnp.where(flags > 0, count - 1.0, count[:, tokens - 1 :] + spot - count)
        return one_zero(iota((tokens, tokens), 0) == target[:1].astype(I32))

    def placed_codes(query_ref):
        where = jnp.where(
            iota((128 - codes_rows, tokens), 0) == 0, iota((128 - codes_rows, tokens), 1), 0
        )
        return jnp.concatenate([query_ref[...], where], axis=0).astype(F32).astype(BF16)

    def order_body(masked_ref, query_ref, chosen_ref):
        top = nt(order_of(masked_ref)[:chosen], placed_codes(query_ref)).astype(BF16)
        for i in range(n):
            chosen_ref[i] = top

    (chosen_codes,) = run(
        order_body,
        ((n, chosen, 128), BF16),
        (masked, query_t),
        "order",
        far=(0, 1),
        us=2,
    )
    all_codes = exchange(chosen_codes)

    def prepare_body(inputs_ref, weight_ref, bias_ref, key_ref, query_ref, grad_ref, masked_ref, conv_ref,
                     value_ref, send_ref, top_ref, low_ref, cot_ref, band_ref, low_band_ref, back_ref,
                     codes_ref, order_ref, pad_ref):
        order_ref[...] = order_of(masked_ref)
        codes_ref[...] = nt(order_ref[chosen:], placed_codes(query_ref)).astype(BF16)
        values = (nt(inputs_ref[...], weight_ref[...]) + line(bias_ref)).astype(BF16)
        value_ref[...] = values
        same = one_zero(iota((local, local), 0) == iota((local, local), 1))
        send_ref[:codes_rows] = key_ref[...].astype(F32).astype(BF16)
        send_ref[codes_rows:] = nt(same, values).astype(BF16)
        order = order_ref[...]
        moved = nn(order, inputs_ref[...]).astype(BF16)
        top_ref[...] = moved[:chosen]
        low_ref[...] = moved[chosen:]
        pick = order_ref[:chosen]
        flags = jnp.broadcast_to(line(masked_ref).astype(F32), (8, tokens)).astype(BF16)
        valid = nt(pick, flags)[:, :1]
        parts = split3(grad_ref[...])
        cot_ref[...] = (nn(pick, parts[0]) + nn(pick, parts[1]) + nn(pick, parts[2])) * valid
        pad_ref[...] = jnp.zeros_like(pad_ref)
        pad_ref[:heads, :taps] = conv_ref[...]
        turn = one_zero(iota((128, 128), 0) + iota((128, 128), 1) == taps - 1)
        padded = pad_ref[...]
        parts = split3(padded)
        turned = nn(parts[0], turn) + nn(parts[1], turn) + nn(parts[2], turn)
        blank = jnp.zeros((8, window - 128), F32)
        for h in range(heads):
            for ahead, source in ((True, padded), (False, turned)):
                long = jnp.concatenate([source, blank], axis=1)
                spread = jnp.broadcast_to(long[h : h + 1], (tokens, window))
                band = pltpu.roll(spread, 0, 1, stride=1, stride_axis=0)
                for at, level in zip((0, window), split2(band)):
                    if ahead:
                        moved = nn(order, level).astype(BF16)
                        band_ref[h, :, at : at + window] = moved[:chosen]
                        low_band_ref[h, :, at : at + window] = moved[chosen:]
                    else:
                        back_ref[h, :, at : at + window] = level

    (values, value_send, top_inputs, low_inputs, cot, bands, low_bands, back_bands, rest_codes,
     order) = run(
        prepare_body,
        [((tokens, local), BF16), ((codes_rows + local, tokens), BF16), ((chosen, width), BF16),
         ((rest, width), BF16), ((chosen, width), F32), ((heads, chosen, 2 * window), BF16),
         ((heads, rest, 2 * window), BF16), ((heads, tokens, 2 * window), BF16), ((rest, 128), BF16),
         ((tokens, tokens), BF16)],
        (inputs, value_t, value_bias, key_t, query_t, out_grad, masked, conv_weight),
        "prepare",
        far=tuple(range(8)),
        far_out=(0, 2, 3, 4, 5, 6, 7, 8, 9),
        scratch=[pltpu.VMEM((8, 128), F32)],
        us=4,
    )
    all_keys = lax.all_gather(value_send, "seq", axis=0)

    def count_body(codes_ref, send_ref, wide_ref, tall_ref, count_ref, out_ref, finish):
        keys = key_words(send_ref[:codes_rows], tall_ref[...])
        queries = query_words(codes_ref[...].reshape(total, 128), wide_ref[...])
        for h in range(heads):
            for r in range(0, total, tokens):
                for c in range(0, tokens, 128):
                    count_ref[h, r : r + tokens, c : c + 128] = matches(
                        queries[r : r + tokens], keys[:, c : c + 128], h
                    )
        finish(0)
        for h in range(heads):
            turned = send_ref[codes_rows + h * dim : codes_rows + (h + 1) * dim]
            read = nt(count_ref[h], turned).astype(BF16)
            for i in range(n):
                out_ref[i, :chosen, h * dim : (h + 1) * dim] = read[i * chosen : (i + 1) * chosen]

    counts, reads = run(
        count_body,
        [((heads, total, tokens), BF16), ((n, chosen, local), BF16)],
        (all_codes, value_send, wide, tall),
        "count",
        far_out=(0,),
        early=(0,),
        us=5,
    )
    edges = lax.optimization_barrier((values, reads))[0]
    before = lax.ppermute(edges[tokens - half :], "seq", [(i, i + 1) for i in range(n - 1)])
    behind = lax.ppermute(edges[:half], "seq", [(i + 1, i) for i in range(n - 1)])
    reads = exchange(reads)

    def unit_rows(value_sum):
        return lax.rsqrt(jnp.mean(value_sum * value_sum, -1, keepdims=True) + 1e-05)

    def context_body(reads_ref, value_ref, band_ref, before_ref, behind_ref, context_ref, sum_ref, near_ref, ready, finish):
        total_read = reads_ref[0].astype(F32)
        for i in range(1, n):
            total_read += reads_ref[i].astype(F32)
        total_read = total_read * (1.0 / hashes)
        sum_ref[...] = total_read
        near_ref[:half] = before_ref[...]
        ready()
        near_ref[half : half + tokens] = value_ref[...]
        near_ref[half + tokens : 2 * half + tokens] = behind_ref[...]
        near_ref[2 * half + tokens :] = jnp.zeros((window - tokens - 2 * half, local), BF16)
        finish(2)
        near = near_ref[...]
        twice = jnp.concatenate([near, near], axis=0)
        for h in range(heads):
            cols = slice(h * dim, (h + 1) * dim)
            mine = total_read[:, cols]
            conv = nn(band_ref[h], twice[:, cols])
            context_ref[:, cols] = (mine * unit_rows(mine) + conv).astype(BF16)

    context, value_sum, near = run(
        context_body,
        [((chosen, local), BF16), ((chosen, local), F32), ((window, local), BF16)],
        (reads, values, bands, before, behind),
        "context",
        far=(1, 2),
        late=(1, 2),
        far_out=(2,),
        early=(2,),
        us=2,
    )
    contexts = [context] + others(context)

    def paired(terms):
        while len(terms) > 1:
            terms = [terms[i] + terms[i + 1] for i in range(0, len(terms), 2)]
        return terms[0]

    def joined(context_refs, out_refs):
        return paired([nn(a[...], b[...]) for a, b in zip(context_refs, out_refs)])

    def feed(low, up_ref, up_bias_ref, down_ref):
        pre = nn(low, up_ref[...]) + line(up_bias_ref)
        act = (pre * cdf_of(pre)).astype(BF16)
        return pre, nn(act, down_ref[...]).astype(BF16)

    def first_body(*refs, ready, finish):
        context_refs, out_refs, refs = refs[:tp], refs[tp : 2 * tp], refs[2 * tp :]
        (inputs_ref, bias_ref, gain_ref, shift_ref, up_ref, up_bias_ref, down_ref,
         part_ref, hidden_ref, first_ref, pre_ref) = refs
        hidden = joined(context_refs, out_refs)
        ready()
        hidden = inputs_ref[...].astype(F32) + hidden + line(bias_ref)
        hidden_ref[...] = hidden
        finish(1)
        unit, _ = norm_stats(hidden)
        first = unit * line(gain_ref) + line(shift_ref)
        first_ref[...] = first
        finish(2)
        pre, part = feed(first.astype(BF16), up_ref, up_bias_ref, down_ref)
        pre_ref[...] = pre
        part_ref[...] = part

    part, hidden, first, pre_act = run(
        first_body,
        [((chosen, width), BF16), ((chosen, width), F32), ((chosen, width), F32), ((chosen, units), F32)],
        (*contexts, *out_all, top_inputs, out_bias, first_gain, first_shift, up_weight, up_bias, down_weight),
        "first",
        far=tuple(range(tp, 2 * tp + 4)) + (2 * tp + 5,),
        far_out=(1, 2, 3),
        early=(1, 2),
        late=tuple(range(2 * tp, 2 * tp + 4)) + (2 * tp + 5,),
        us=3,
    )
    parts = [part] + others(part)

    def slope_body(pre_ref, slope_ref):
        slope_ref[...] = gelu_grad(pre_ref[...])

    (slope,) = run(slope_body, ((chosen, units), F32), (pre_act,), "slope", far=(0,), us=1.5)

    def back_norm(grad, unit, q, gain):
        scaled = grad * gain
        return q * (
            scaled
            - jnp.mean(scaled, -1, keepdims=True)
            - unit * jnp.mean(scaled * unit, -1, keepdims=True)
        )

    def put_sums(ref, sums):
        for i, vector in enumerate(sums):
            ref[i : i + 1] = vector

    def column_sum(array):
        return jnp.sum(array, 0, keepdims=True)

    def second_body(ids_ref, *refs, ready, finish):
        part_refs, refs = refs[:tp], refs[tp:]
        (first_ref, bias_ref, gain_ref, shift_ref, cot_ref, slope_ref, down_ref, up_ref,
         context_ref, output_ref, grad_ref, back_ref, sums_ref, keep_ref, low_ref) = refs
        second = paired([r[...].astype(F32) for r in part_refs])
        ready()
        second = first_ref[...] + second + line(bias_ref)
        unit, q = norm_stats(second)
        output_ref[...] = (unit * line(gain_ref) + line(shift_ref)).astype(BF16)
        finish(0)
        grad = back_norm(cot_ref[...], unit, q, line(gain_ref))
        grad_ref[...] = grad
        low = grad.astype(BF16)
        grad_pre = (nt(low, down_ref[...]) * slope_ref[...]).astype(BF16)
        back_ref[...] = nt(grad_pre, up_ref[...]).astype(BF16)
        put_sums(sums_ref, [column_sum(cot_ref[...] * unit), column_sum(cot_ref[...]), column_sum(grad)])
        low_ref[:, :width] = first_ref[...].astype(BF16)
        low_ref[:, width:] = low
        keep_ref[:, : 2 * width] = low_ref[pl.ds(pl.multiple_of(ids_ref[1] % 2 * mid, mid), mid)]
        keep_ref[:, 2 * width : 2 * width + local] = context_ref[:mid]
        keep_ref[:, 2 * width + local : 2 * width + 2 * local] = context_ref[mid:]
        keep_ref[:, 2 * width + 2 * local :] = jnp.zeros((mid, kept - 2 * width - 2 * local), BF16)

    mid = chosen // 2
    kept = -(-2 * (width + local) // 1024) * 1024
    out_chosen, grad_second, back, sums, keep = run(
        second_body,
        [((chosen, width), BF16), ((chosen, width), F32), ((chosen, width), BF16), ((8, width), F32),
         ((mid, kept), BF16)],
        (ids, *parts, first, down_bias, second_gain, second_shift, cot, slope, down_weight, up_weight, context),
        "second",
        also=tuple((weight, pltpu.HBM) for weight in value_all[1:]),
        far=tuple(range(tp + 1, tp + 6)),
        late=tuple(range(tp + 1, tp + 6)),
        far_out=(0, 4),
        early=(0,),
        smem=1,
        scratch=[pltpu.VMEM((chosen, 2 * width), BF16)],
        us=3,
    )
    backs = [back] + others(back)
    keeps = lax.all_gather(keep, "seq", axis=0)

    def rest_counts(count_ref, queries, word_ref, head):
        @pl.loop(0, n * tokens // 256)
        def _(i):
            for c in range(2):
                lanes = pl.ds(pl.multiple_of(i * 256 + c * 128, 128), 128)
                count_ref[:, lanes] = matches(queries, word_ref[:, lanes], head)

    def rest_read(count_ref, keys_ref, head):
        start = codes_rows + head * dim
        turned = jnp.concatenate([keys_ref[i, start : start + dim] for i in range(n)], axis=1)
        return nt(count_ref[...], turned) * (1.0 / hashes)

    def rest_words_body(codes_ref, keys_ref, wide_ref, tall_ref, query_ref, word_ref, first_ref,
                        key_ref, count_ref, ready):
        queries = query_words(codes_ref[...], wide_ref[...])
        query_ref[...] = queries
        ready()
        for i in range(n):
            key_ref[:, i * tokens : (i + 1) * tokens] = keys_ref[i, :codes_rows]
        word_ref[...] = key_words(key_ref[...], tall_ref[...])
        rest_counts(count_ref, queries, word_ref, 0)
        first_ref[...] = rest_read(count_ref, keys_ref, 0)

    rest_queries, key_bits, rest_sum = run(
        rest_words_body,
        [((rest, 128), I32), ((32, n * tokens), I32), ((rest, dim), F32)],
        (rest_codes, all_keys, wide, tall),
        "rest_words",
        far=(0, 1, 2, 3),
        late=(1,),
        scratch=[pltpu.VMEM((codes_rows, n * tokens), BF16), pltpu.VMEM((rest, n * tokens), BF16)],
        us=5,
    )

    def hidden_body(ids_ref, *refs, ready, finish):
        back_refs, refs = refs[:tp], refs[tp:]
        grad_ref, hidden_ref, gain_ref, sums_ref, read_ref, weight_ref, out_ref, send_ref, share_ref, all_ref, attn_ref = refs
        grad = grad_ref[...] + paired([r[...].astype(F32) for r in back_refs])
        ready()
        unit, q = norm_stats(hidden_ref[...])
        grad_hidden = back_norm(grad, unit, q, line(gain_ref))
        out_ref[...] = grad_hidden
        finish(0)
        low = grad_hidden.astype(BF16)
        y = nt(low, weight_ref[...]).astype(BF16)
        for h in range(heads):
            cols = slice(h * dim, (h + 1) * dim)
            read, at = read_ref[:, cols], y[:, cols].astype(F32)
            r = unit_rows(read)
            back = r * (at - read * (r * r) * jnp.mean(at * read, -1, keepdims=True))
            send_ref[0, :, cols] = (back * (1.0 / hashes)).astype(BF16)
        send_ref[0, :, local:] = y
        for i in range(1, n):
            send_ref[i] = send_ref[0]
        attn_ref[...] = low
        share_ref[...] = attn_ref[pl.ds(pl.multiple_of(ids_ref[1] * part_rows, part_rows), part_rows)]
        all_ref[:3] = sums_ref[:3]
        put_sums(all_ref.at[3:6], [column_sum(grad * unit), column_sum(grad), column_sum(grad_hidden)])
        all_ref[6:] = jnp.zeros((2, width), F32)

    grad_hidden, read_send, share, sums = run(
        hidden_body,
        [((chosen, width), F32), ((n, chosen, 2 * local), BF16), ((part_rows, width), BF16), ((8, width), F32)],
        (ids, *backs, grad_second, hidden, first_gain, sums, value_sum, out_weight),
        "hidden",
        also=((all_keys, pltpu.HBM),),
        far=(tp + 2, tp + 3),
        late=(tp + 2, tp + 3),
        far_out=(0, 2, 3),
        early=(0,),
        smem=1,
        scratch=[pltpu.VMEM((chosen, width), BF16)],
        us=2,
    )
    read_all = exchange(read_send)

    def rest_body(query_ref, word_ref, first_ref, keys_ref, band_ref, near_ref, context_ref, count_ref, ready):
        queries = query_ref[...]
        for h in range(heads):
            if h:
                rest_counts(count_ref, queries, word_ref, h)
                if h == 1:
                    ready()
                    near = near_ref[...]
                    twice = jnp.concatenate([near, near], axis=0)
            cols = slice(h * dim, (h + 1) * dim)
            if h:
                mine = rest_read(count_ref, keys_ref, h)
                conv = nn(band_ref[h], twice[:, cols])
                context_ref[:, cols] = (mine * unit_rows(mine) + conv).astype(BF16)
        mine = first_ref[...]
        conv = nn(band_ref[0], twice[:, :dim])
        context_ref[:, :dim] = (mine * unit_rows(mine) + conv).astype(BF16)

    (rest_context,) = run(
        rest_body,
        ((rest, local), BF16),
        (rest_queries, key_bits, rest_sum, all_keys, low_bands, near),
        "rest_context",
        far=(3, 4, 5),
        late=(3, 4, 5),
        scratch=[pltpu.VMEM((rest, n * tokens), BF16)],
        us=6,
    )
    rest_contexts = [rest_context] + others(rest_context)

    def values_body(ids_ref, read_ref, count_ref, band_ref, codes_ref, grad_ref, dense_ref, ready):
        me = ids_ref[0]
        ready()
        dense = jnp.zeros((window, local), F32)
        for step in (-1, 0, 1):
            source = jnp.clip(me + step, 0, n - 1)
            inside = jnp.logical_and(me + step >= 0, me + step < n)
            there = read_ref[source][:, local:]
            spots = codes_ref[source][:, codes_rows : codes_rows + 1].astype(F32).astype(I32)
            spots = jnp.where(inside, spots + step * tokens + half, -1)
            place = one_zero(spots == iota((chosen, window), 1))
            dense += tn(place, there)
        dense_low = dense.astype(BF16)
        dense_ref[...] = dense_low
        twice = jnp.concatenate([dense_low, dense_low], axis=0)
        for h in range(heads):
            cols = slice(h * dim, (h + 1) * dim)
            read = read_ref[:, :, cols].reshape(total, dim)
            grad = tn(count_ref[h], read) + nn(band_ref[h], twice[:, cols])
            grad_ref[:, cols] = grad.astype(BF16)

    grad_values, dense = run(
        values_body,
        [((tokens, local), BF16), ((window, local), BF16)],
        (ids, read_all, counts, back_bands, all_codes),
        "values_back",
        smem=1,
        far=(2, 3, 4),
        late=(2, 3, 4),
        us=4,
    )
    grads = [grad_values] + others(grad_values)

    piece_rows = local // n
    extra = 8

    def value_grad_body(inputs_ref, grad_ref, dense_ref, near_ref, sums_ref, share_ref, send_ref, row_ref):
        grad = grad_ref[...]
        weight = tn(grad, inputs_ref[...]).astype(BF16)
        row_ref[...] = jnp.zeros_like(row_ref)
        row_ref[:1, :local] = column_sum(grad.astype(F32))
        row_ref[1:7] = sums_ref[:6]
        turn = one_zero(iota((tokens, tokens), 0) + iota((tokens, tokens), 1) == tokens - 1)
        turned = nn(turn, dense_ref[half : half + tokens]).astype(BF16)
        for h in range(heads):
            cols = slice(h * dim, (h + 1) * dim)
            both = nt(turned[:, cols], near_ref[:, cols])
            aligned = pltpu.roll(both, window - tokens + 1, 1, stride=1, stride_axis=0)
            row_ref[:1, 256 + 128 * h : 384 + 128 * h] = column_sum(aligned)[:, :128]
        for i in range(n):
            send_ref[i, :piece_rows] = weight[i * piece_rows : (i + 1) * piece_rows]
            send_ref[i, piece_rows : piece_rows + extra] = row_ref[...].astype(BF16)
            send_ref[i, piece_rows + extra :] = share_ref[...]

    (value_part,) = run(
        value_grad_body,
        ((n, piece_rows + extra + part_rows, width), BF16),
        (inputs, grad_values, dense, near, sums, share),
        "value_grad",
        far=(0, 3, 4, 5),
        scratch=[pltpu.VMEM((extra, width), F32)],
        us=2.5,
    )
    value_part = exchange(value_part)

    def rest_first_body(*refs, ready):
        context_refs, out_refs, refs = refs[:tp], refs[tp : 2 * tp], refs[2 * tp :]
        (inputs_ref, bias_ref, gain_ref, shift_ref, up_ref, up_bias_ref, down_ref, part_ref, first_ref) = refs
        hidden = joined(context_refs, out_refs)
        ready()
        hidden = inputs_ref[...].astype(F32) + hidden + line(bias_ref)
        unit, _ = norm_stats(hidden)
        first = unit * line(gain_ref) + line(shift_ref)
        first_ref[...] = first
        part_ref[...] = feed(first.astype(BF16), up_ref, up_bias_ref, down_ref)[1]

    rest_part, rest_first = run(
        rest_first_body,
        [((rest, width), BF16), ((rest, width), F32)],
        (*rest_contexts, *out_all, low_inputs, out_bias, first_gain, first_shift, up_weight, up_bias,
         down_weight),
        "rest_first",
        also=tuple((array, pltpu.HBM) for array in grads[1:]),
        far=tuple(range(2 * tp + 7)),
        late=tuple(range(2 * tp, 2 * tp + 7)),
        far_out=(1,),
        us=4,
    )
    rest_parts = [rest_part] + others(rest_part)
    keeps = [keeps, swap(lax.optimization_barrier((keeps, rest_part))[0], 1)]

    def input_body(*refs):
        grad_refs, weight_refs, (order_ref, hidden_ref, out_ref) = (
            refs[:tp], refs[tp : 2 * tp], refs[2 * tp :])
        pick = order_ref[:chosen]
        parts = split3(hidden_ref[...])
        placed = tn(pick, parts[0]) + tn(pick, parts[1]) + tn(pick, parts[2])
        out_ref[...] = placed + joined(grad_refs, weight_refs)

    (input_grad,) = run(
        input_body,
        ((tokens, width), F32),
        (*grads, *value_all, order, grad_hidden),
        "input_grad",
        far=tuple(range(2 * tp + 2)),
        far_out=(0,),
        us=0.05,
    )

    def value_sum_body(part_ref, send_ref, attn_ref, bias_ref, taps_ref, *vector_refs):
        rows = piece_rows + extra
        whole = part_ref[0, :rows].astype(F32)
        for i in range(1, n):
            whole += part_ref[i, :rows].astype(F32)
        for i in range(n):
            send_ref[i] = whole[:piece_rows].astype(BF16)
            attn_ref[i] = part_ref[i, rows:]
        bias_ref[...] = whole[piece_rows : piece_rows + 1, :local].reshape(local)
        for h in range(heads):
            taps_ref[h : h + 1] = whole[piece_rows : piece_rows + 1, 256 + 128 * h : 256 + 128 * h + taps]
        for i, ref in enumerate(vector_refs):
            ref[...] = whole[piece_rows + 1 + i : piece_rows + 2 + i].reshape(width)

    value_send_back, attn_share, grad_value_bias, grad_taps, *vectors = run(
        value_sum_body,
        [((n, piece_rows, width), BF16), ((n, part_rows, width), BF16), ((local,), F32), ((heads, taps), F32)]
        + [((width,), F32)] * 6,
        (value_part,),
        "value_sums",
        far_out=tuple(range(2, 10)),
        us=0.05,
    )
    attn_shares = [attn_share] + others(attn_share)
    value_back = exchange(value_send_back)

    def weights_body(keep_ref, far_ref, up_w_ref, up_bias_ref, down_w_ref,
                     up_ref, up_sum_ref, grad_ref, act_ref, pre_ref, raw_ref, back_ref, finish):
        sides = (keep_ref, far_ref)
        low = jnp.concatenate([ref[:, :, :width].reshape(total // 2, width) for ref in sides], axis=0)
        down = jnp.concatenate(
            [ref[:, :, width : 2 * width].reshape(total // 2, width) for ref in sides], axis=0
        )
        raw_ref[...] = nn(low, up_w_ref[...])
        back_ref[...] = nt(down, down_w_ref[...])
        up_sum = jnp.zeros((1, units), F32)
        for i in range(n):
            rows = slice(i * chosen, (i + 1) * chosen)
            pre = raw_ref[rows] + line(up_bias_ref)
            cdf = cdf_of(pre)
            act_ref[rows] = (pre * cdf).astype(BF16)
            slope = cdf + pre * jnp.exp(-0.5 * pre * pre) * 0.3989422804014327
            grad_pre = (back_ref[rows] * slope).astype(BF16)
            pre_ref[rows] = grad_pre
            up_sum += column_sum(grad_pre.astype(F32))
        up_sum_ref[...] = up_sum.reshape(units)
        up_ref[...] = tn(low, pre_ref[...])
        finish(0)
        grad_ref[...] = tn(act_ref[...], down)

    grad_up, up_sum, grad_down = run(
        weights_body,
        [((width, units), F32), ((units,), F32), ((units, width), F32)],
        (*keeps, up_weight, up_bias, down_weight),
        "weights",
        also=tuple((array, pltpu.VMEM) for array in rest_parts[1:]),
        far=(0, 1, 2, 3, 4),
        far_out=(0, 1, 2),
        early=(0,),
        scratch=[pltpu.VMEM((total, units), BF16)] * 2 + [pltpu.VMEM((total, units), F32)] * 2,
        us=3,
    )

    def last_body(ids_ref, *refs, ready, finish):
        part_refs, attn_refs, refs = refs[:tp], refs[tp : 2 * tp], refs[2 * tp :]
        (back_ref, first_ref, bias_ref, gain_ref, shift_ref, chosen_ref, order_ref, keep_ref,
         out_ref, grad_out_ref, grad_value_ref, sorted_ref, all_ref, context_ref) = refs
        for i in range(n):
            grad_value_ref[i * piece_rows : (i + 1) * piece_rows] = back_ref[i].astype(F32)
        finish(2)
        for k, ref in enumerate(attn_refs):
            for i in range(n):
                start = i * chosen + (ids_ref[1] ^ k) * part_rows
                all_ref[pl.ds(pl.multiple_of(start, part_rows), part_rows)] = ref[i]
        second = paired([r[...].astype(F32) for r in part_refs])
        ready()
        second = first_ref[...] + second + line(bias_ref)
        unit, _ = norm_stats(second)
        sorted_ref[:chosen] = chosen_ref[...]
        sorted_ref[chosen:] = (unit * line(gain_ref) + line(shift_ref)).astype(BF16)
        out_ref[...] = tn(order_ref[...], sorted_ref[...]).astype(BF16)
        finish(0)
        tops = keep_ref[:, :, 2 * width : 2 * width + local].reshape(total // 2, local)
        lows = keep_ref[:, :, 2 * width + local : 2 * width + 2 * local].reshape(total // 2, local)
        for i in range(n):
            context_ref[i * chosen : i * chosen + mid] = tops[i * mid : (i + 1) * mid]
            context_ref[i * chosen + mid : (i + 1) * chosen] = lows[i * mid : (i + 1) * mid]
        grad_out_ref[...] = tn(context_ref[...], all_ref[...])

    output, grad_out, grad_value = run(
        last_body,
        [((tokens, width), BF16), ((local, width), F32), ((local, width), F32)],
        (ids, *rest_parts, *attn_shares, value_back, rest_first, down_bias, second_gain, second_shift, out_chosen,
         order, keeps[0]),
        "last",
        smem=1,
        far=tuple(range(2 * tp + 2, 2 * tp + 9)),
        late=tuple(range(2 * tp + 2, 2 * tp + 9)),
        far_out=(0, 1, 2),
        early=(0, 2),
        scratch=[pltpu.VMEM((tokens, width), BF16), pltpu.VMEM((total, width), BF16),
                 pltpu.VMEM((total, local), BF16)],
        us=0.05,
    )
    return (
        output,
        input_grad,
        grad_value.T,
        grad_value_bias,
        grad_out,
        vectors[5],
        vectors[3],
        vectors[4],
        grad_up,
        up_sum,
        grad_down,
        vectors[2],
        vectors[0],
        vectors[1],
        grad_taps,
    )


def solution(mesh):
    return jax.shard_map(
        per_device,
        mesh=mesh,
        in_specs=(
            P("seq", None),
            P(None, "tp"),
            P("tp"),
            P("tp", None),
            P(),
            P(),
            P(),
            P(None, "tp"),
            P("tp"),
            P("tp", None),
            P(),
            P(),
            P(),
            P("tp", None),
            P("seq", "tp", None),
            P("seq", "tp", None),
            P("seq"),
            P("seq", None),
        ),
        out_specs=(
            P("seq", None),
            P("seq", None),
            P(None, "tp"),
            P("tp"),
            P("tp", None),
            P(),
            P(),
            P(),
            P(None, "tp"),
            P("tp"),
            P("tp", None),
            P(),
            P(),
            P(),
            P("tp", None),
        ),
        check_vma=False,
    )
```
